32 devices in a mesh: dp: 8 (over z, x), fsdp: 4 (over y, core).
Axes of the slice: x: 2, y: 2, z: 4, core: 2. Of those that a mesh axis runs over, the one named last changes fastest.
Arguments:
- cached: bfloat16 [8, 4, 256, 1024], P('dp', 'fsdp'), may hold values from -60 to 60
- send_rows: int32 [8, 4, 8, 64], P('dp', 'fsdp'), may hold values from -1 to 255, as said below
- take_rows: int32 [8, 4, 256], P('dp', 'fsdp'), may hold values from -1 to 511, as said below
- utt_index: int32 [8, 4, 256], P('dp', 'fsdp'), may hold values from 0 to 9, never falling along the last dimension, each value on 1 to 64 neighbouring positions
- upstream: bfloat16 [8, 4, 512, 1536], P('dp', 'fsdp'), may hold values from -6 to 6
- in_proj: bfloat16 [512, 1536], P(None, 'fsdp'), may hold values from -2 to 2
- norm_gain: bfloat16 [1536], P('fsdp'), may hold values from 0.099609375 to 1.8984375
- conv_kernel: bfloat16 [31, 1536], P(None, 'fsdp'), may hold values from -1 to 1
Outputs:
- grad_proj: float32 [512, 1536], P(None, 'fsdp')
- grad_kernel: float32 [31, 1536], P(None, 'fsdp')
- grad_gain: float32 [1536], P('fsdp')
- step_loss: float32 [8, 4], P('dp', 'fsdp')
The draws below stay inside these ranges and needn't reach their ends.
Inputs may be any that keep to these rules, and one draw needn't show every extreme that they name: `send_rows`: entry [s, g, d, j] is -1 or the cache row of sender s (same fsdp group g) sent as entry j of its slot for device d. The used entries of a slot come first; a sender's used entries for one device lie in one aligned block of 64 cache rows; a sender's entries name distinct rows. Each device receives from 4 senders of its group, and some device of each group receives 64 rows from each of them. `take_rows`: entry [d, g, r] is -1 or s * 64 + j for a used entry send_rows[s, g, d, j]; each used entry is named once. The -1 entries of a device come last, the rows from one sender stand together, and some device of each group has no -1 entry. Sender 8 - 1 fills its whole slot for every device that it serves.
All inputs are finite; a program needn't handle non-finite values.
Results may differ from the reference program's by a relative error of at most 0.003.
Values may be sent and summed in bfloat16 or wider, within the bound.
No kernel may reach another device: no remote copies, remote signals or barrier semaphores. Data moves between devices by JAX's collectives and lax.ppermute only.
A program may use at most 64 MiB of HBM per device.

```python
import math
import jax
import jax.numpy as jnp
import numpy as np
from jax import lax

FEAT = 128
STACK = 4
D = 1536
KW = 31
PAIRS = 256
UTT_MOST = 64
SLOT = 64
UTTS = 10
N_DP = 8
N_FSDP = 4


def routing(key):
    senders = N_DP
    owner_count = N_DP // 2

    def one_group(group_key):
        subkeys = jax.random.split(group_key, 6)
        dest_perm = jax.random.permutation(subkeys[0], senders)
        send_perm = jax.random.permutation(subkeys[1], senders)
        offsets = jax.random.permutation(subkeys[2], senders)[:owner_count]
        owners = send_perm[(dest_perm[:, None] + offsets[None, :]) % senders]
        piece_lens = jax.random.randint(subkeys[3], (senders, owner_count), 1, SLOT + 1)
        full_dest = jax.random.randint(subkeys[4], (), 0, senders)
        piece_lens = jnp.where(jnp.arange(senders)[:, None] == full_dest, SLOT, piece_lens)
        piece_lens = jnp.where(owners == senders - 1, SLOT, piece_lens)
        ends = jnp.cumsum(piece_lens, axis=1)
        starts = ends - piece_lens
        live_total = ends[:, -1]
        row_ids = jnp.arange(PAIRS)
        piece_of = jnp.sum((starts[:, None, :] <= row_ids[None, :, None]).astype(jnp.int32), axis=2) - 1
        piece_start = jnp.take_along_axis(starts, piece_of, axis=1)
        piece_owner = jnp.take_along_axis(owners, piece_of, axis=1)
        take_list = jnp.where(row_ids[None, :] < live_total[:, None], piece_owner * SLOT + row_ids[None, :] - piece_start, -1)
        rotation = jax.random.randint(subkeys[5], (senders, owner_count), 0, SLOT)
        slot_ids = jnp.arange(SLOT)
        block_ids = jnp.arange(owner_count)
        cache_ids = block_ids[None, :, None] * SLOT + (slot_ids[None, None, :] + rotation[:, :, None]) % SLOT
        cache_ids = jnp.where(slot_ids[None, None, :] < piece_lens[:, :, None], cache_ids, -1)
        send_list = jnp.full((senders, senders, SLOT), -1, jnp.int32)
        send_list = send_list.at[owners, jnp.arange(senders)[:, None]].set(cache_ids.astype(jnp.int32))
        return (send_list, take_list.astype(jnp.int32))
    group_keys = jax.random.split(key, N_FSDP)
    send_all, take_all = jax.vmap(one_group)(group_keys)
    return (jnp.transpose(send_all, (1, 0, 2, 3)).astype(jnp.int32), jnp.transpose(take_all, (1, 0, 2)).astype(jnp.int32))


def draw_send_rows(key, part):
    return routing(jax.random.fold_in(key, 11))[0]


def draw_take_rows(key, part):
    return routing(jax.random.fold_in(key, 11))[1]


def draw_cached(key, part):
    subkeys = jax.random.split(jax.random.fold_in(key, 23), 3)
    shape = (N_DP, N_FSDP, PAIRS, 2 * STACK, FEAT)
    base = jnp.clip(jax.random.normal(subkeys[0], shape, jnp.float32), -5.0, 5.0)
    frame_scale = jnp.exp(jax.random.uniform(subkeys[1], (N_DP, N_FSDP, PAIRS, 2 * STACK, 1), jnp.float32, -1.15, 1.15))
    feat_scale = jnp.exp(jax.random.uniform(subkeys[2], (FEAT,), jnp.float32, -1.15, 1.15))
    values_all = base * frame_scale * feat_scale
    return values_all.reshape(N_DP, N_FSDP, PAIRS, 2 * STACK * FEAT).astype(jnp.bfloat16)


def draw_in_proj(key, part):
    subkeys = jax.random.split(jax.random.fold_in(key, 37), 2)
    shape = (STACK * FEAT, D)
    column_scale = jnp.exp(jax.random.uniform(subkeys[1], (D,), jnp.float32, -1.15, 1.15))
    base = jnp.clip(jax.random.normal(subkeys[0], shape, jnp.float32), -4.0, 4.0)
    return (base * column_scale / math.sqrt(STACK * FEAT)).astype(jnp.bfloat16)


def block_levels(key, dims, cuts, least, largest):
    def one(position, parts):
        steps = jax.random.uniform(jax.random.fold_in(jax.random.fold_in(key, 6), position), (parts,), jnp.float32, least / len(cuts), largest / len(cuts))
        return jnp.repeat(jnp.exp(steps), dims[position] // parts).reshape((-1,) + (1,) * (len(dims) - position - 1))

    factor_of = one(*cuts[0])
    for cut in cuts[1:]:
        factor_of = factor_of * one(*cut)
    return factor_of


def split_up(count, total, reach, lean):
    portions = [(1 << 20) // math.isqrt(grade ** lean) + 1 for grade in range(2, count + 1)]
    rest, holding = total - reach - (count - 1), [1] * (count - 1)
    while rest > 0:
        candidates = [i for i in range(count - 1) if holding[i] < reach]
        pool, left = sum([portions[i] for i in candidates]), rest
        for i in candidates:
            addition = min(reach - holding[i], max(1, left * portions[i] // pool), rest)
            holding[i] = holding[i] + addition
            rest = rest - addition
    return np.array([reach] + holding)


def uneven_parts(own_key, count, total, bound, slope):
    if count == 2:
        one = jax.random.randint(own_key, (), max(1, total - bound), min(bound, total - 1) + 1)
        return jnp.stack([one, total - one])
    tallies = jnp.asarray(split_up(count, total, bound, slope), jnp.int32)
    twos = (count - 1) // 2
    source_of, receiver = tallies[1:1 + 2 * twos:2], tallies[2:2 + 2 * twos:2]
    margin = jnp.minimum(source_of - 1, bound - receiver)
    shifted = jax.random.randint(jax.random.fold_in(own_key, 1), (twos,), 0, 1 << 20) % (margin + 1)
    tallies = tallies.at[1:1 + 2 * twos:2].set(source_of - shifted).at[2:2 + 2 * twos:2].set(receiver + shifted)
    return tallies[jax.random.permutation(jax.random.fold_in(own_key, 2), count)]


def noise(own_key, extent, width, bound, cuts=(), held_as=jnp.bfloat16):
    array = width * jax.random.normal(own_key, extent, jnp.float32)
    if cuts:
        array = array * block_levels(own_key, extent, cuts, -0.22, 0.18)
    return jnp.clip(array, -bound, bound).astype(held_as)


def setup_inputs(seed: int = 0) -> dict:
    seeds = jax.random.split(jax.random.key(seed), 9)
    return {
        "cached": draw_cached(jax.random.fold_in(seeds[8], 71), 0),
        "send_rows": draw_send_rows(jax.random.fold_in(seeds[8], 71), 0),
        "take_rows": draw_take_rows(jax.random.fold_in(seeds[8], 71), 0),
        "utt_index": jax.vmap(lambda own: jnp.searchsorted(jnp.cumsum(uneven_parts(own, UTTS, PAIRS, UTT_MOST, 1)), jnp.arange(PAIRS), side="right"))(jax.random.split(seeds[3], N_DP * N_FSDP)).reshape((N_DP, N_FSDP, PAIRS)).astype(jnp.int32),
        "upstream": noise(seeds[4], (N_DP, N_FSDP, 2 * PAIRS, D), 1.0, 6.0, ((0, 8), (1, 4))),
        "in_proj": draw_in_proj(jax.random.fold_in(seeds[8], 71), 0),
        "norm_gain": jnp.clip(1.0 + 0.18 * jax.random.normal(seeds[6], (D,), jnp.float32), 0.099609375, 1.8984375).astype(jnp.bfloat16),
        "conv_kernel": noise(seeds[7], (KW, D), KW ** -0.5, 1.0, ((1, 4),)),
    }


def spread_conv(source_field, kernel_taps, tap_weights):
    tap_count = kernel_taps.shape[0]
    half_width = tap_count // 2
    step_count = source_field.shape[0]
    padded = jnp.pad(source_field, ((half_width, half_width), (0, 0)))
    summed = jnp.zeros_like(source_field)
    for offset in range(tap_count):
        summed = summed + kernel_taps[offset] * (tap_weights[:, offset:offset + 1] * padded[offset:offset + step_count])
    return summed

def build_mask(live_steps, utterances, tap_count):
    half_width = tap_count // 2
    step_count = live_steps.shape[0]
    live_pad = jnp.pad(live_steps, (half_width, half_width))
    utter_pad = jnp.pad(utterances, (half_width, half_width), constant_values=-1)
    columns = []
    for offset in range(tap_count):
        columns.append(live_steps & live_pad[offset:offset + step_count] & (utterances == utter_pad[offset:offset + step_count]))
    return jnp.stack(columns, axis=1).astype(jnp.float32)

def layer_terms(encoded, live_steps, utterances, grad_above, gain, kernel):
    tap_count = kernel.shape[0]
    half_width = tap_count // 2
    step_count = encoded.shape[0]
    tap_weights = build_mask(live_steps, utterances, tap_count)
    row_mean = lax.optimization_barrier(jnp.mean(encoded, axis=1, keepdims=True))
    centered = encoded - row_mean
    row_var = lax.optimization_barrier(jnp.mean(centered * centered, axis=1, keepdims=True))
    inv_std = lax.rsqrt(row_var + 1e-05)
    normalized = centered * inv_std
    gain_f32 = gain.astype(jnp.float32)
    kernel_taps = kernel.astype(jnp.float32)
    normed = normalized * gain_f32
    conv_out = spread_conv(normed, kernel_taps, tap_weights)
    gate_sig = jax.nn.sigmoid(conv_out)
    output = encoded + conv_out * gate_sig
    scale = (encoded.shape[0] * encoded.shape[1]) ** (-0.5)
    grad_out = jnp.where(live_steps[:, None], grad_above.astype(jnp.float32), jnp.zeros((), jnp.float32)) * scale
    device_loss = jnp.sum(output * grad_out)
    grad_conv = grad_out * (gate_sig * (1.0 + conv_out * (1.0 - gate_sig)))
    grad_normed = spread_conv(grad_conv, kernel_taps[::-1], tap_weights)
    padded = jnp.pad(normed, ((half_width, half_width), (0, 0)))
    grad_taps = jnp.stack([lax.optimization_barrier(jnp.sum(grad_conv * tap_weights[:, offset:offset + 1] * padded[offset:offset + step_count], axis=0)) for offset in range(tap_count)])
    grad_scale = lax.optimization_barrier(jnp.sum(grad_normed * normalized, axis=0))
    grad_hat = grad_normed * gain_f32
    grad_x = grad_out + inv_std * (grad_hat - lax.optimization_barrier(jnp.mean(grad_hat, axis=1, keepdims=True)) - normalized * lax.optimization_barrier(jnp.mean(grad_hat * normalized, axis=1, keepdims=True)))
    return (device_loss, grad_x.astype(jnp.bfloat16), grad_taps, grad_scale)

def reference(cached, send_rows, take_rows, utt_index, upstream, in_proj, norm_gain, conv_kernel):
    is_live = take_rows >= 0
    safe_index = jnp.maximum(take_rows, 0).astype(jnp.int32)
    sender = (safe_index // SLOT).astype(jnp.int32)
    slot_entry = (safe_index % SLOT).astype(jnp.int32)
    fsdp_index = jnp.arange(N_FSDP).astype(jnp.int32)[None, :, None]
    destination = jnp.arange(N_DP).astype(jnp.int32)[:, None, None]
    cache_index = jnp.maximum(send_rows[sender, fsdp_index, destination, slot_entry], 0).astype(jnp.int32)
    work_rows = cached[sender, fsdp_index, cache_index]
    work_rows = jnp.where(is_live[..., None], work_rows, jnp.zeros((), cached.dtype))
    devices_all = N_DP * N_FSDP
    work_flat = work_rows.reshape(devices_all, PAIRS, 2 * STACK * FEAT)
    live_flat = is_live.reshape(devices_all, PAIRS)
    utter_flat = utt_index.reshape(devices_all, PAIRS)
    above_flat = upstream.reshape(devices_all, 2 * PAIRS, D)
    proj_f32 = in_proj.astype(jnp.float32)

    def device_step(running, inputs):
        pair_rows, live_pairs, utter_pairs, grad_above = inputs
        frames = pair_rows.reshape(2 * PAIRS, STACK * FEAT).astype(jnp.float32)
        live_steps = jnp.repeat(live_pairs, 2)
        utterances = jnp.repeat(utter_pairs, 2)
        encoded = jnp.dot(frames, proj_f32, precision=lax.Precision.HIGHEST)
        device_loss, grad_x, grad_taps, grad_scale = layer_terms(encoded, live_steps, utterances, grad_above, norm_gain, conv_kernel)
        grad_weight = jnp.dot(frames.T, grad_x.astype(jnp.float32), precision=lax.Precision.HIGHEST)
        return ((running[0] + grad_weight, running[1] + grad_taps, running[2] + grad_scale), device_loss)
    initial = (jnp.zeros((STACK * FEAT, D), jnp.float32), jnp.zeros((KW, D), jnp.float32), jnp.zeros((D,), jnp.float32))
    totals, losses = lax.scan(device_step, initial, (work_flat, live_flat, utter_flat, above_flat))
    return (totals[0], totals[1], totals[2], losses.reshape(N_DP, N_FSDP))
```

```python
import functools
import math

import jax
import jax.numpy as jnp
import numpy as np
from jax import lax
from jax.experimental import pallas as pl
from jax.experimental.pallas import tpu as pltpu
from jax.sharding import PartitionSpec as P

GAP = 16
POINTS = 256
FREQS = 128
STARTS = (0, 224, 432)
LENGTHS = (224, 208, 224)
BLOCK_STEPS = ((0, 208), (128, 384), (304, 512))
WIDE_STEPS = ((0, 224), (112, 400), (288, 512))
BLOCK_K = ((208, 208, 224), (256, 256, 256), (208, 208, 224))
WIDE_K = ((224, 224, 320), (288, 288, 320), (224, 224, 320))
AHEAD_AT = tuple(int(v) for v in np.cumsum([0] + [sum(k) for k in WIDE_K + BLOCK_K]))
BEHIND_AT = tuple(int(v) for v in np.cumsum([0] + [b - a for a, b in WIDE_STEPS + BLOCK_STEPS]))
CH = 256
ROWS = 64
F32 = jnp.float32
BF16 = jnp.bfloat16
VMEM_LIMIT = 40 * 1024 * 1024


def k_slices(steps, sizes):
    out = []
    for size in sizes:
        first = steps[0] if steps[0] + size <= 512 else 512 - size
        out.append((first, first + size))
    return out


def split(value):
    hi = value.astype(BF16)
    return hi, (value - hi.astype(F32)).astype(BF16)


def split_np(value):
    hi = value.astype(jnp.bfloat16)
    lo = (value - hi.astype(np.float64)).astype(jnp.bfloat16)
    return hi, lo


def transforms(tap_count):
    omega = 2 * np.pi * (np.arange(FREQS) + 0.5) / POINTS
    angle = omega[:, None] * np.arange(POINTS)[None, :]
    forward = np.concatenate([np.cos(angle), -np.sin(angle)], axis=0)
    f_hi, f_lo = split_np(forward)
    back = np.concatenate([f_hi.T, f_lo.T, f_hi.T], axis=1)
    shift = omega[:, None] * (np.arange(32) - tap_count // 2)[None, :]
    tap_ok = (np.arange(32) < tap_count)[None, :]
    taps = np.concatenate([np.cos(shift), np.sin(shift)], axis=0) * tap_ok / FREQS
    t_hi, t_lo = split_np(taps)
    tap_fwd = np.concatenate([t_hi, t_lo], axis=1)
    lag = np.concatenate([np.cos(shift), -np.sin(shift)], axis=0) * tap_ok / FREQS
    l_hi, l_lo = split_np(lag.T)
    lags = np.concatenate([l_hi, l_lo, l_hi], axis=1)
    return f_hi, f_lo, back, tap_fwd, lags


def dot(a, b):
    return jnp.dot(a, b, preferred_element_type=F32)


def dot_t(a, b):
    return lax.dot_general(a, b, (((0,), (0,)), ((), ())), preferred_element_type=F32)


def pick_kernel(index_ref, rows_ref, out_ref):
    count = rows_ref.shape[0]
    total = index_ref.shape[1]
    number = lax.broadcasted_iota(jnp.int32, (count, total), 0)
    choose = jnp.where(number == index_ref[...], 1.0, 0.0).astype(BF16)
    out_ref[...] = dot_t(choose, rows_ref[...]).astype(BF16)


def prep_kernel(pos_ref, hi_ref, lo_ref, back_ref, ahead_ref, behind_ref):
    f_hi = hi_ref[...]
    f_lo = lo_ref[...]
    back = back_ref[...]
    for part in range(6):
        sizes = (WIDE_K + BLOCK_K)[part]
        steps = (WIDE_STEPS + BLOCK_STEPS)[part]
        total = sum(sizes)
        place = pos_ref[part : part + 1, :total]
        number = lax.broadcasted_iota(jnp.int32, (POINTS, total), 0)
        hot = jnp.where(number == place, 1.0, 0.0).astype(BF16)
        lane = lax.broadcasted_iota(jnp.int32, (1, total), 1)
        middle = (lane >= sizes[0]) & (lane < sizes[0] + sizes[1])
        ahead = jnp.where(middle, dot(f_lo, hot), dot(f_hi, hot)).astype(BF16)
        ahead_ref[:, AHEAD_AT[part] : AHEAD_AT[part + 1]] = ahead
        held = steps[1] - steps[0]
        padded = -(-held // 128) * 128
        wide = dot_t(hot[:, :padded], back)
        behind_ref[BEHIND_AT[part] : BEHIND_AT[part + 1]] = wide[:held].astype(BF16)


def layer_kernel(
    core_ref, arrived_ref, take_ref, tapf_ref, lag_ref, params_hbm, up_hbm, ahead_hbm, behind_hbm,
    keep_ref, send_ref, loss_ref,
    params_ref, up_ref, ahead_ref, behind_ref, sems,
    frames_ref, frames_t_ref, x_ref, h_ref, stat_ref, acc_ref, acc2_ref,
    hi_ref, lo_ref, ghi_ref, glo_ref, spec_ref, nspec_ref, phi_ref, plo_ref,
    coef_ref, c_ref, small_ref, lossacc_ref,
):
    copies = [
        pltpu.make_async_copy(source, target, sems.at[k])
        for k, (source, target) in enumerate(
            ((params_hbm, params_ref), (ahead_hbm, ahead_ref), (behind_hbm, behind_ref), (up_hbm, up_ref))
        )
    ]
    for copy in copies:
        copy.start()
    steps, width = up_ref.shape
    slots, pair_width = arrived_ref.shape
    depth = pair_width // 2
    chunks = width // CH
    scale = (steps * width) ** -0.5
    tiles = [slice(r, r + ROWS) for r in range(0, steps, ROWS)]
    wide_of = [slice(AHEAD_AT[j], AHEAD_AT[j + 1]) for j in range(3)]
    block_of = [slice(AHEAD_AT[j], AHEAD_AT[j + 1]) for j in range(3, 6)]
    back_wide = [slice(BEHIND_AT[j], BEHIND_AT[j + 1]) for j in range(3)]
    back_block = [slice(BEHIND_AT[j], BEHIND_AT[j + 1]) for j in range(3, 6)]

    take = take_ref[...]
    number = lax.broadcasted_iota(jnp.int32, (slots, steps), 0)
    odd = lax.broadcasted_iota(jnp.int32, (slots, steps), 1) % 2
    here = number == take
    even_hot = jnp.where(here & (odd == 0), 1.0, 0.0).astype(BF16)
    odd_hot = jnp.where(here & (odd == 1), 1.0, 0.0).astype(BF16)
    frames = dot_t(even_hot, arrived_ref[:, :depth]) + dot_t(odd_hot, arrived_ref[:, depth:])
    frames_ref[...] = frames.astype(BF16)
    frames_t_ref[...] = jnp.transpose(frames).astype(BF16)
    live = dot_t(even_hot + odd_hot, jnp.ones((slots, 128), BF16))
    stat_ref[2] = live * scale

    acc_ref[...] = jnp.zeros_like(acc_ref)
    copies[0].wait()

    def project(i, carry):
        cols = pl.ds(pl.multiple_of(i * CH, CH), CH)
        x = dot(frames_ref[...], params_ref[:depth, cols])
        x_ref[:, cols] = x
        acc_ref[...] += x[:, :128] + x[:, 128:]
        return carry

    lax.fori_loop(0, chunks, project, 0)
    mean = jnp.sum(acc_ref[...], axis=1, keepdims=True) * (1.0 / width)
    stat_ref[0] = jnp.broadcast_to(mean, (steps, 128))

    for rows in tiles:
        m = stat_ref[0, rows]
        total = jnp.zeros((ROWS, 128), F32)
        for k in range(width // 128):
            d = x_ref[rows, k * 128 : (k + 1) * 128] - m
            total = total + d * d
        var = jnp.sum(total, axis=1, keepdims=True) * (1.0 / width)
        stat_ref[1, rows] = jnp.broadcast_to(lax.rsqrt(var + 1e-05), (ROWS, 128))

    acc_ref[...] = jnp.zeros_like(acc_ref)
    acc2_ref[...] = jnp.zeros_like(acc2_ref)
    lossacc_ref[...] = jnp.zeros_like(lossacc_ref)

    for copy in copies[1:]:
        copy.wait()

    def twice(value):
        return jnp.concatenate([value, value], axis=1)

    def stack(hi, lo, slices):
        (a, b), (c, d), (e, f) = slices
        return jnp.concatenate([hi[a:b], hi[c:d], lo[e:f]], axis=0)

    def middle(i, carry):
        cols = pl.ds(pl.multiple_of(i * CH, CH), CH)
        gain = params_ref[depth + 16 : depth + 32, cols][15:16].astype(F32)
        taps = params_ref[depth : depth + 32, cols]
        coef_ref[...] = dot(tapf_ref[...], jnp.concatenate([taps, taps], axis=0))
        for rows in tiles:
            xhat = (x_ref[rows, cols] - twice(stat_ref[0, rows])) * twice(stat_ref[1, rows])
            hi, lo = split(xhat * gain)
            hi_ref[rows] = hi
            lo_ref[rows] = lo
        for j in range(3):
            nspec_ref[j] = dot(ahead_ref[:, block_of[j]], stack(hi_ref, lo_ref, k_slices(BLOCK_STEPS[j], BLOCK_K[j])))
        for j in range(3):
            for f in range(0, FREQS, 32):
                lower, upper = slice(f, f + 32), slice(FREQS + f, FREQS + f + 32)
                re, im = nspec_ref[j, lower], nspec_ref[j, upper]
                cre, cim = coef_ref[lower], coef_ref[upper]
                hi, lo = split(re * cre - im * cim)
                phi_ref[j, lower] = hi
                plo_ref[j, lower] = lo
                hi, lo = split(re * cim + im * cre)
                phi_ref[j, upper] = hi
                plo_ref[j, upper] = lo
        parts = [
            dot(behind_ref[back_wide[j]], jnp.concatenate([phi_ref[j], phi_ref[j], plo_ref[j]], axis=0))
            for j in range(3)
        ]
        c_ref[0:112] = parts[0][0:112]
        c_ref[112:224] = parts[0][112:224] + parts[1][0:112]
        c_ref[224:288] = parts[1][112:176]
        c_ref[288:400] = parts[1][176:288] + parts[2][0:112]
        c_ref[400:512] = parts[2][112:224]
        loss = jnp.zeros((1, CH), F32)
        for rows in tiles:
            conv = c_ref[rows]
            sig = jax.nn.sigmoid(conv)
            go = up_ref[rows, cols].astype(F32) * twice(stat_ref[2, rows])
            out = x_ref[rows, cols] + conv * sig
            loss = loss + jnp.sum(out * go, axis=0, keepdims=True)
            hi, lo = split(go * (sig * (1.0 + conv * (1.0 - sig))))
            ghi_ref[rows] = hi
            glo_ref[rows] = lo
        lossacc_ref[...] += loss
        for j in range(3):
            spec_ref[j] = dot(ahead_ref[:, wide_of[j]], stack(ghi_ref, glo_ref, k_slices(WIDE_STEPS[j], WIDE_K[j])))
        for f in range(0, FREQS, 32):
            lower, upper = slice(f, f + 32), slice(FREQS + f, FREQS + f + 32)
            cre, cim = coef_ref[lower], coef_ref[upper]
            zre = jnp.zeros((32, CH), F32)
            zim = jnp.zeros((32, CH), F32)
            for j in range(3):
                nre, nim = nspec_ref[j, lower], nspec_ref[j, upper]
                re, im = spec_ref[j, lower], spec_ref[j, upper]
                zre = zre + (nre * re + nim * im)
                zim = zim + (nim * re - nre * im)
                hi, lo = split(re * cre + im * cim)
                phi_ref[j, lower] = hi
                plo_ref[j, lower] = lo
                hi, lo = split(im * cre - re * cim)
                phi_ref[j, upper] = hi
                plo_ref[j, upper] = lo
            hi, lo = split(zre)
            phi_ref[3, lower] = hi
            plo_ref[3, lower] = lo
            hi, lo = split(zim)
            phi_ref[3, upper] = hi
            plo_ref[3, upper] = lo
        tap_grad = dot(lag_ref[...], jnp.concatenate([phi_ref[3], phi_ref[3], plo_ref[3]], axis=0))
        parts = [
            dot(behind_ref[back_block[j]], jnp.concatenate([phi_ref[j], phi_ref[j], plo_ref[j]], axis=0))
            for j in range(3)
        ]
        c_ref[0:128] = parts[0][0:128]
        c_ref[128:208] = parts[0][128:208] + parts[1][0:80]
        c_ref[208:304] = parts[1][80:176]
        c_ref[304:384] = parts[1][176:256] + parts[2][0:80]
        c_ref[384:512] = parts[2][80:208]
        gain_grad = jnp.zeros((1, CH), F32)
        for rows in tiles:
            gn = c_ref[rows]
            xhat = (x_ref[rows, cols] - twice(stat_ref[0, rows])) * twice(stat_ref[1, rows])
            gain_grad = gain_grad + jnp.sum(gn * xhat, axis=0, keepdims=True)
            h = gn * gain
            hx = h * xhat
            h_ref[rows, cols] = h
            acc_ref[rows] += h[:, :128] + h[:, 128:]
            acc2_ref[rows] += hx[:, :128] + hx[:, 128:]
        last = lax.broadcasted_iota(jnp.int32, (32, CH), 0) == 31
        small_ref[:, cols] = jnp.where(last, gain_grad, tap_grad)
        return carry

    lax.fori_loop(0, chunks, middle, 0)
    loss_ref[...] = jnp.sum(lossacc_ref[...], axis=1, keepdims=True)
    for rows in tiles:
        m1 = jnp.sum(acc_ref[rows], axis=1, keepdims=True) * (1.0 / width)
        m2 = jnp.sum(acc2_ref[rows], axis=1, keepdims=True) * (1.0 / width)
        acc_ref[rows] = jnp.broadcast_to(m1, (ROWS, 128))
        acc2_ref[rows] = jnp.broadcast_to(m2, (ROWS, 128))

    halves, filled_to, _ = keep_ref.shape
    per_block = width // (2 * halves) // 128
    held = depth + 32

    def finish(core):
        for i in range(chunks):
            cols = slice(i * CH, (i + 1) * CH)
            for rows in tiles:
                inv = twice(stat_ref[1, rows])
                xhat = (x_ref[rows, cols] - twice(stat_ref[0, rows])) * inv
                go = up_ref[rows, cols].astype(F32) * twice(stat_ref[2, rows])
                inner = h_ref[rows, cols] - twice(acc_ref[rows]) - xhat * twice(acc2_ref[rows])
                hi_ref[rows] = (go + inv * inner).astype(BF16)
            weight = dot(frames_t_ref[...], hi_ref[...])
            for half in range(CH // 128):
                tile = i * (CH // 128) + half
                block, inside = tile // per_block, (tile % per_block) * held
                lanes = slice(half * 128, half * 128 + 128)
                small = small_ref[:, tile * 128 : (tile + 1) * 128]
                target = keep_ref if block % 2 == core else send_ref
                target[block // 2, inside : inside + depth] = weight[:, lanes]
                target[block // 2, inside + depth : inside + held] = small

    pl.when(core_ref[0, 0] == 0)(lambda: finish(0))
    pl.when(core_ref[0, 0] != 0)(lambda: finish(1))
    filled = per_block * held
    if filled_to > filled:
        for half in range(halves):
            for ref in (keep_ref, send_ref):
                ref[half, filled:] = jnp.zeros((filled_to - filled, 128), F32)


def vmem(count):
    return [pl.BlockSpec(memory_space=pltpu.VMEM)] * count


def pick(index, rows):
    total = index.shape[1]
    return pl.pallas_call(
        pick_kernel,
        out_shape=jax.ShapeDtypeStruct((total, rows.shape[1]), BF16),
        in_specs=vmem(2),
        out_specs=vmem(1)[0],
        compiler_params=pltpu.CompilerParams(vmem_limit_bytes=VMEM_LIMIT),
        cost_estimate=pl.CostEstimate(
            flops=2 * total * rows.size, bytes_accessed=6 * rows.size, transcendentals=0
        ),
        name="pick_rows",
    )(index, rows)


def positions(utterances):
    steps = utterances.shape[0]
    place = jnp.arange(steps, dtype=jnp.int32) + GAP * utterances
    most = max(sum(sizes) for sizes in WIDE_K + BLOCK_K)
    lines = []
    for kind, (ranges, sizes_of) in enumerate(((WIDE_STEPS, WIDE_K), (BLOCK_STEPS, BLOCK_K))):
        for j in range(3):
            local = place - (STARTS[j] - GAP)
            low, high = (0, LENGTHS[j] + 2 * GAP) if kind == 0 else (GAP, LENGTHS[j] + GAP)
            local = jnp.where((local >= low) & (local < high), local, -1)
            inside = jnp.arange(steps)
            local = jnp.where((inside >= ranges[j][0]) & (inside < ranges[j][1]), local, -1)
            pieces = [local[a:b] for a, b in k_slices(ranges[j], sizes_of[j])]
            line = jnp.concatenate(pieces)
            lines.append(jnp.pad(line, (0, most - line.shape[0]), constant_values=-1))
    lines.extend([jnp.full((most,), -1, jnp.int32)] * 2)
    return jnp.stack(lines)


def prepare(utterances, f_hi, f_lo, back):
    shapes = [
        jax.ShapeDtypeStruct((POINTS, AHEAD_AT[-1]), BF16),
        jax.ShapeDtypeStruct((BEHIND_AT[-1], 3 * POINTS), BF16),
    ]
    return pl.pallas_call(
        prep_kernel,
        out_shape=shapes,
        in_specs=vmem(4),
        out_specs=vmem(2),
        compiler_params=pltpu.CompilerParams(vmem_limit_bytes=VMEM_LIMIT),
        cost_estimate=pl.CostEstimate(flops=3 * 10**9, bytes_accessed=8 * 10**6, transcendentals=0),
        name="prepare_transforms",
    )(positions(utterances), f_hi, f_lo, back)


def layer(core, arrived, take, params, upstream, tap_fwd, lags, ahead, behind, out_rows, halves):
    steps, width = upstream.shape
    depth = arrived.shape[1] // 2
    hbm = pl.BlockSpec(memory_space=pltpu.HBM)
    scratch = [
        pltpu.VMEM(params.shape, BF16),
        pltpu.VMEM(upstream.shape, BF16),
        pltpu.VMEM(ahead.shape, BF16),
        pltpu.VMEM(behind.shape, BF16),
        pltpu.SemaphoreType.DMA((4,)),
        pltpu.VMEM((steps, depth), BF16),
        pltpu.VMEM((depth, steps), BF16),
        pltpu.VMEM((steps, width), F32),
        pltpu.VMEM((steps, width), F32),
        pltpu.VMEM((3, steps, 128), F32),
        pltpu.VMEM((steps, 128), F32),
        pltpu.VMEM((steps, 128), F32),
        pltpu.VMEM((steps, CH), BF16),
        pltpu.VMEM((steps, CH), BF16),
        pltpu.VMEM((steps, CH), BF16),
        pltpu.VMEM((steps, CH), BF16),
        pltpu.VMEM((3, POINTS, CH), F32),
        pltpu.VMEM((3, POINTS, CH), F32),
        pltpu.VMEM((4, POINTS, CH), BF16),
        pltpu.VMEM((4, POINTS, CH), BF16),
        pltpu.VMEM((POINTS, CH), F32),
        pltpu.VMEM((steps, CH), F32),
        pltpu.VMEM((32, width), F32),
        pltpu.VMEM((1, CH), F32),
    ]
    return pl.pallas_call(
        layer_kernel,
        out_shape=[
            jax.ShapeDtypeStruct((halves, out_rows, 128), F32),
            jax.ShapeDtypeStruct((halves, out_rows, 128), F32),
            jax.ShapeDtypeStruct((1, 1), F32),
        ],
        in_specs=[pl.BlockSpec(memory_space=pltpu.SMEM)] + vmem(4) + [hbm] * 4,
        out_specs=vmem(3),
        scratch_shapes=scratch,
        compiler_params=pltpu.CompilerParams(vmem_limit_bytes=VMEM_LIMIT),
        cost_estimate=pl.CostEstimate(flops=10**10, bytes_accessed=16 * 10**6, transcendentals=10**6),
        name="layer_step",
    )(core, arrived, take, tap_fwd, lags, params, upstream, ahead, behind)


def per_device(
    dp, fsdp, cached, send_rows, take_rows, utt_index, upstream, in_proj, norm_gain, conv_kernel
):
    tap_count = conv_kernel.shape[0]
    f_hi, f_lo, back, tap_fwd, lags = [jnp.asarray(m) for m in transforms(tap_count)]
    local = jnp.concatenate([in_proj, conv_kernel, norm_gain[None, :]], axis=0)
    params = lax.all_gather(local, "fsdp", axis=1, tiled=True)
    wanted = send_rows[0, 0]
    outgoing = pick(wanted.reshape(1, -1), cached[0, 0])
    outgoing, take_own, utt_own = lax.optimization_barrier(
        (outgoing, take_rows[0, 0], utt_index[0, 0])
    )
    outgoing = outgoing.reshape(wanted.shape + outgoing.shape[1:])
    arrived = lax.all_to_all(outgoing, "dp", split_axis=0, concat_axis=0, tiled=True)
    arrived = arrived.reshape(-1, arrived.shape[2])
    take = jnp.repeat(take_own, 2)[None, :]
    ahead, behind = prepare(jnp.repeat(utt_own, 2), f_hi, f_lo, back)

    shard_cols = in_proj.shape[1]
    held = local.shape[0]
    tiles = shard_cols // 128
    part = -(-(held * tiles) // dp)
    part = -(-part // 16) * 16
    halves = fsdp // 2
    core = (lax.axis_index("fsdp") % 2).astype(jnp.int32).reshape(1, 1)
    keep, send, loss = layer(
        core, arrived, take, params, upstream[0, 0], tap_fwd, lags, ahead, behind, part * dp, halves
    )
    other = lax.ppermute(send, "fsdp", [(i, i ^ 1) for i in range(fsdp)])
    chip = (keep + other).astype(BF16).reshape(halves * dp, part, 128)
    groups = [
        [d * fsdp + 2 * y + c for y in range(halves) for d in range(dp)] for c in range(2)
    ]
    pieces = lax.all_to_all(
        chip, ("dp", "fsdp"), split_axis=0, concat_axis=0, tiled=True, axis_index_groups=groups
    )
    piece = jnp.sum(pieces.astype(F32), axis=0).astype(BF16)
    whole = lax.all_gather(piece, "dp", axis=0, tiled=True)
    whole = whole[: held * tiles].reshape(tiles, held, 128).transpose(1, 0, 2)
    whole = whole.reshape(held, shard_cols).astype(F32)
    depth = in_proj.shape[0]
    return (
        whole[:depth],
        whole[depth : depth + tap_count],
        whole[depth + tap_count],
        loss,
    )


def solution(mesh):
    placed = (
        P("dp", "fsdp", None, None),
        P("dp", "fsdp", None, None),
        P("dp", "fsdp", None),
        P("dp", "fsdp", None),
        P("dp", "fsdp", None, None),
        P(None, "fsdp"),
        P("fsdp"),
        P(None, "fsdp"),
    )
    return jax.shard_map(
        functools.partial(per_device, mesh.shape["dp"], mesh.shape["fsdp"]),
        mesh=mesh,
        in_specs=placed,
        out_specs=(P(None, "fsdp"), P(None, "fsdp"), P("fsdp"), P("dp", "fsdp")),
        check_vma=False,
    )
```

```python
import functools
import math

import jax
import jax.numpy as jnp
import numpy as np
from jax import lax
from jax.experimental import pallas as pl
from jax.experimental.pallas import tpu as pltpu
from jax.sharding import PartitionSpec as P

GAP = 16
POINTS = 256
FREQS = 128
STARTS = (0, 224, 432)
LENGTHS = (224, 208, 224)
BLOCK_STEPS = ((0, 208), (128, 384), (304, 512))
WIDE_STEPS = ((0, 224), (112, 400), (288, 512))
BLOCK_K = ((208, 208, 224), (256, 256, 256), (208, 208, 224))
WIDE_K = ((224, 224, 320), (288, 288, 320), (224, 224, 320))
AHEAD_AT = tuple(int(v) for v in np.cumsum([0] + [sum(k) for k in WIDE_K + BLOCK_K]))
BEHIND_AT = tuple(int(v) for v in np.cumsum([0] + [b - a for a, b in WIDE_STEPS + BLOCK_STEPS]))
CH = 256
ROWS = 64
F32 = jnp.float32
BF16 = jnp.bfloat16
VMEM_LIMIT = 60 * 1024 * 1024
FEW = 16


def k_slices(steps, sizes):
    out = []
    for size in sizes:
        first = steps[0] if steps[0] + size <= 512 else 512 - size
        out.append((first, first + size))
    return out


def split(value):
    hi = value.astype(BF16)
    return hi, (value - hi.astype(F32)).astype(BF16)


def split_np(value):
    hi = value.astype(jnp.bfloat16)
    lo = (value - hi.astype(np.float64)).astype(jnp.bfloat16)
    return hi, lo


def transforms(tap_count):
    omega = 2 * np.pi * (np.arange(FREQS) + 0.5) / POINTS
    angle = omega[:, None] * np.arange(POINTS)[None, :]
    forward = np.concatenate([np.cos(angle), -np.sin(angle)], axis=0)
    f_hi, f_lo = split_np(forward)
    back = np.concatenate([f_hi.T, f_lo.T, f_hi.T], axis=1)
    shift = omega[:, None] * (np.arange(32) - tap_count // 2)[None, :]
    tap_ok = (np.arange(32) < tap_count)[None, :]
    taps = np.concatenate([np.cos(shift), np.sin(shift)], axis=0) * tap_ok / FREQS
    t_hi, t_lo = split_np(taps)
    tap_fwd = np.concatenate([t_hi, t_lo], axis=1)
    lag = np.concatenate([np.cos(shift), -np.sin(shift)], axis=0) * tap_ok / FREQS
    l_hi, l_lo = split_np(lag.T)
    lags = np.concatenate([l_hi, l_lo, l_hi], axis=1)
    return f_hi, f_lo, back, tap_fwd, lags


def dot(a, b):
    return jnp.dot(a, b, preferred_element_type=F32)


def dot_t(a, b):
    return lax.dot_general(a, b, (((0,), (0,)), ((), ())), preferred_element_type=F32)


def pick_kernel(ids_ref, index_ref, rows_ref, *out_refs):
    count = rows_ref.shape[0]
    rows = rows_ref[...]
    if len(out_refs) == 1:
        index = index_ref[...]
        number = lax.broadcasted_iota(jnp.int32, (count, index.shape[1]), 0)
        choose = jnp.where(number == index, 1.0, 0.0).astype(BF16)
        out_refs[0][...] = dot_t(choose, rows).astype(BF16)
        return
    slot = index_ref.shape[1]
    number = lax.broadcasted_iota(jnp.int32, (count, slot), 0)
    for k, out_ref in enumerate(out_refs):
        index = index_ref[pl.ds(ids_ref[0, 2] ^ k, 1), :]
        choose = jnp.where(number == index, 1.0, 0.0).astype(BF16)
        out_ref[...] = dot_t(choose, rows).astype(BF16)


def runs(first, last, part):
    out = []
    row = first
    while row < last:
        stop = min(last, (row // part + 1) * part)
        out.append((row // part, row % part, row % part + stop - row, row - first))
        row = stop
    return out


def unpack_kernel(count, ids_ref, *refs):
    piece_refs, (proj_ref, taps_ref, gain_ref, held_ref) = refs[:count], refs[count:]
    parts, part, _ = held_ref.shape
    for k in range(parts):
        piece = piece_refs[k][...] if count == parts else piece_refs[0][k * part : (k + 1) * part]
        held_ref[k] = piece.astype(F32)
    depth, width = proj_ref.shape
    held = depth + 32
    for tile in range(width // 128):
        lanes = slice(tile * 128, tile * 128 + 128)
        for p, start, stop, offset in runs(tile * held, tile * held + depth, part):
            proj_ref[offset : offset + stop - start, lanes] = held_ref[p ^ ids_ref[0, 2], start:stop]
        last = [
            held_ref[p ^ ids_ref[0, 2], start:stop]
            for p, start, stop, _ in runs(tile * held + depth, tile * held + held, part)
        ]
        last = last[0] if len(last) == 1 else jnp.concatenate(last, axis=0)
        taps_ref[:, lanes] = last[: taps_ref.shape[0]]
        gain_ref[:, lanes] = last[taps_ref.shape[0] : taps_ref.shape[0] + 1]


def prep_kernel(pos_ref, hi_ref, lo_ref, back_ref, ahead_ref, behind_ref):
    f_hi = hi_ref[...]
    f_lo = lo_ref[...]
    back = back_ref[...]
    for part in range(6):
        sizes = (WIDE_K + BLOCK_K)[part]
        steps = (WIDE_STEPS + BLOCK_STEPS)[part]
        total = sum(sizes)
        place = pos_ref[part : part + 1, :total]
        number = lax.broadcasted_iota(jnp.int32, (POINTS, total), 0)
        hot = jnp.where(number == place, 1.0, 0.0).astype(BF16)
        lane = lax.broadcasted_iota(jnp.int32, (1, total), 1)
        middle = (lane >= sizes[0]) & (lane < sizes[0] + sizes[1])
        ahead = jnp.where(middle, dot(f_lo, hot), dot(f_hi, hot)).astype(BF16)
        ahead_ref[:, AHEAD_AT[part] : AHEAD_AT[part + 1]] = ahead
        held = steps[1] - steps[0]
        padded = -(-held // 128) * 128
        wide = dot_t(hot[:, :padded], back)
        behind_ref[BEHIND_AT[part] : BEHIND_AT[part + 1]] = wide[:held].astype(BF16)


def layer_kernel(count, ids_ref, *refs):
    arrived_refs = refs[:count]
    (
        take_ref, tapf_ref, lag_ref, small_in_ref, params_hbm, up_hbm, ahead_hbm, behind_hbm,
        keep_ref, send_ref, loss_ref,
        params_ref, up_ref, ahead_ref, behind_ref, sems,
        frames_ref, frames_t_ref, x_ref, h_ref, stat_ref, acc_ref, acc2_ref,
        hi_ref, lo_ref, ghi_ref, glo_ref, spec_ref, nspec_ref, phi_ref, plo_ref,
        coef_ref, c_ref, small_ref, lossacc_ref,
    ) = refs[count:]
    copies = [
        pltpu.make_async_copy(source, target, sems.at[k])
        for k, (source, target) in enumerate(
            ((params_hbm, params_ref), (ahead_hbm, ahead_ref), (behind_hbm, behind_ref), (up_hbm, up_ref))
        )
    ]
    for copy in copies:
        copy.start()
    steps, width = up_ref.shape
    slots = sum(ref.shape[0] for ref in arrived_refs)
    pair_width = arrived_refs[0].shape[1]
    depth = pair_width // 2
    chunks = width // CH
    scale = (steps * width) ** -0.5
    tiles = [slice(r, r + ROWS) for r in range(0, steps, ROWS)]
    wide_of = [slice(AHEAD_AT[j], AHEAD_AT[j + 1]) for j in range(3)]
    block_of = [slice(AHEAD_AT[j], AHEAD_AT[j + 1]) for j in range(3, 6)]
    back_wide = [slice(BEHIND_AT[j], BEHIND_AT[j + 1]) for j in range(3)]
    back_block = [slice(BEHIND_AT[j], BEHIND_AT[j + 1]) for j in range(3, 6)]

    take = take_ref[...]
    number = lax.broadcasted_iota(jnp.int32, (slots, steps), 0)
    odd = lax.broadcasted_iota(jnp.int32, (slots, steps), 1) % 2
    here = number == take
    even_hot = jnp.where(here & (odd == 0), 1.0, 0.0).astype(BF16)
    odd_hot = jnp.where(here & (odd == 1), 1.0, 0.0).astype(BF16)
    first = jnp.concatenate([ref[:, :depth] for ref in arrived_refs], axis=0)
    second = jnp.concatenate([ref[:, depth:] for ref in arrived_refs], axis=0)
    frames = dot_t(even_hot, first) + dot_t(odd_hot, second)
    frames_ref[...] = frames.astype(BF16)
    frames_t_ref[...] = jnp.transpose(frames).astype(BF16)
    live = dot_t(even_hot + odd_hot, jnp.ones((slots, 128), BF16))
    stat_ref[2] = live * scale

    acc_ref[...] = jnp.zeros_like(acc_ref)
    copies[0].wait()

    def project(i, carry):
        cols = pl.ds(pl.multiple_of(i * CH, CH), CH)
        x = dot(frames_ref[...], params_ref[:, cols])
        x_ref[:, cols] = x
        acc_ref[...] += x[:, :128] + x[:, 128:]
        return carry

    lax.fori_loop(0, chunks, project, 0)
    mean = jnp.sum(acc_ref[...], axis=1, keepdims=True) * (1.0 / width)
    stat_ref[0] = jnp.broadcast_to(mean, (steps, 128))

    for rows in tiles:
        m = stat_ref[0, rows]
        total = jnp.zeros((ROWS, 128), F32)
        for k in range(width // 128):
            d = x_ref[rows, k * 128 : (k + 1) * 128] - m
            total = total + d * d
        var = jnp.sum(total, axis=1, keepdims=True) * (1.0 / width)
        stat_ref[1, rows] = jnp.broadcast_to(lax.rsqrt(var + 1e-05), (ROWS, 128))

    acc_ref[...] = jnp.zeros_like(acc_ref)
    acc2_ref[...] = jnp.zeros_like(acc2_ref)
    lossacc_ref[...] = jnp.zeros_like(lossacc_ref)

    for copy in copies[1:]:
        copy.wait()

    def twice(value):
        return jnp.concatenate([value, value], axis=1)

    def stack(hi, lo, slices):
        (a, b), (c, d), (e, f) = slices
        return jnp.concatenate([hi[a:b], hi[c:d], lo[e:f]], axis=0)

    def middle(i, carry):
        cols = pl.ds(pl.multiple_of(i * CH, CH), CH)
        gain = small_in_ref[16:32, cols][15:16].astype(F32)
        taps = small_in_ref[:, cols]
        coef_ref[...] = dot(tapf_ref[...], jnp.concatenate([taps, taps], axis=0))
        for rows in tiles:
            xhat = (x_ref[rows, cols] - twice(stat_ref[0, rows])) * twice(stat_ref[1, rows])
            hi, lo = split(xhat * gain)
            hi_ref[rows] = hi
            lo_ref[rows] = lo
        for j in range(3):
            nspec_ref[j] = dot(ahead_ref[:, block_of[j]], stack(hi_ref, lo_ref, k_slices(BLOCK_STEPS[j], BLOCK_K[j])))
        for j in range(3):
            for f in range(0, FREQS, 32):
                lower, upper = slice(f, f + 32), slice(FREQS + f, FREQS + f + 32)
                re, im = nspec_ref[j, lower], nspec_ref[j, upper]
                cre, cim = coef_ref[lower], coef_ref[upper]
                hi, lo = split(re * cre - im * cim)
                phi_ref[j, lower] = hi
                plo_ref[j, lower] = lo
                hi, lo = split(re * cim + im * cre)
                phi_ref[j, upper] = hi
                plo_ref[j, upper] = lo
        parts = [
            dot(behind_ref[back_wide[j]], jnp.concatenate([phi_ref[j], phi_ref[j], plo_ref[j]], axis=0))
            for j in range(3)
        ]
        c_ref[0:112] = parts[0][0:112]
        c_ref[112:224] = parts[0][112:224] + parts[1][0:112]
        c_ref[224:288] = parts[1][112:176]
        c_ref[288:400] = parts[1][176:288] + parts[2][0:112]
        c_ref[400:512] = parts[2][112:224]
        loss = jnp.zeros((1, CH), F32)
        for rows in tiles:
            conv = c_ref[rows]
            sig = jax.nn.sigmoid(conv)
            go = up_ref[rows, cols].astype(F32) * twice(stat_ref[2, rows])
            out = x_ref[rows, cols] + conv * sig
            loss = loss + jnp.sum(out * go, axis=0, keepdims=True)
            hi, lo = split(go * (sig * (1.0 + conv * (1.0 - sig))))
            ghi_ref[rows] = hi
            glo_ref[rows] = lo
        lossacc_ref[...] += loss
        for j in range(3):
            spec_ref[j] = dot(ahead_ref[:, wide_of[j]], stack(ghi_ref, glo_ref, k_slices(WIDE_STEPS[j], WIDE_K[j])))
        for f in range(0, FREQS, 32):
            lower, upper = slice(f, f + 32), slice(FREQS + f, FREQS + f + 32)
            cre, cim = coef_ref[lower], coef_ref[upper]
            zre = jnp.zeros((32, CH), F32)
            zim = jnp.zeros((32, CH), F32)
            for j in range(3):
                nre, nim = nspec_ref[j, lower], nspec_ref[j, upper]
                re, im = spec_ref[j, lower], spec_ref[j, upper]
                zre = zre + (nre * re + nim * im)
                zim = zim + (nim * re - nre * im)
                hi, lo = split(re * cre + im * cim)
                phi_ref[j, lower] = hi
                plo_ref[j, lower] = lo
                hi, lo = split(im * cre - re * cim)
                phi_ref[j, upper] = hi
                plo_ref[j, upper] = lo
            hi, lo = split(zre)
            phi_ref[3, lower] = hi
            plo_ref[3, lower] = lo
            hi, lo = split(zim)
            phi_ref[3, upper] = hi
            plo_ref[3, upper] = lo
        tap_grad = dot(lag_ref[...], jnp.concatenate([phi_ref[3], phi_ref[3], plo_ref[3]], axis=0))
        parts = [
            dot(behind_ref[back_block[j]], jnp.concatenate([phi_ref[j], phi_ref[j], plo_ref[j]], axis=0))
            for j in range(3)
        ]
        c_ref[0:128] = parts[0][0:128]
        c_ref[128:208] = parts[0][128:208] + parts[1][0:80]
        c_ref[208:304] = parts[1][80:176]
        c_ref[304:384] = parts[1][176:256] + parts[2][0:80]
        c_ref[384:512] = parts[2][80:208]
        gain_grad = jnp.zeros((1, CH), F32)
        for rows in tiles:
            gn = c_ref[rows]
            xhat = (x_ref[rows, cols] - twice(stat_ref[0, rows])) * twice(stat_ref[1, rows])
            gain_grad = gain_grad + jnp.sum(gn * xhat, axis=0, keepdims=True)
            h = gn * gain
            hx = h * xhat
            h_ref[rows, cols] = h
            acc_ref[rows] += h[:, :128] + h[:, 128:]
            acc2_ref[rows] += hx[:, :128] + hx[:, 128:]
        last = lax.broadcasted_iota(jnp.int32, (32, CH), 0) == 31
        small_ref[:, cols] = jnp.where(last, gain_grad, tap_grad)
        return carry

    lax.fori_loop(0, chunks, middle, 0)
    loss_ref[...] = jnp.sum(lossacc_ref[...], axis=1, keepdims=True)
    for rows in tiles:
        m1 = jnp.sum(acc_ref[rows], axis=1, keepdims=True) * (1.0 / width)
        m2 = jnp.sum(acc2_ref[rows], axis=1, keepdims=True) * (1.0 / width)
        acc_ref[rows] = jnp.broadcast_to(m1, (ROWS, 128))
        acc2_ref[rows] = jnp.broadcast_to(m2, (ROWS, 128))

    halves, parts, part, _ = keep_ref.shape
    per_block = width // (2 * halves) // 128
    held = depth + 32

    def finish(core):
        for i in range(chunks):
            cols = slice(i * CH, (i + 1) * CH)
            for rows in tiles:
                inv = twice(stat_ref[1, rows])
                xhat = (x_ref[rows, cols] - twice(stat_ref[0, rows])) * inv
                go = up_ref[rows, cols].astype(F32) * twice(stat_ref[2, rows])
                inner = h_ref[rows, cols] - twice(acc_ref[rows]) - xhat * twice(acc2_ref[rows])
                hi_ref[rows] = (go + inv * inner).astype(BF16)
            weight = dot(frames_t_ref[...], hi_ref[...])
            for half in range(CH // 128):
                tile = i * (CH // 128) + half
                block, inside = tile // per_block, (tile % per_block) * held
                lanes = slice(half * 128, half * 128 + 128)
                small = small_ref[:, tile * 128 : (tile + 1) * 128]
                target = keep_ref if block % 2 == core else send_ref
                side = (block // 2) ^ ids_ref[0, 1]
                for p, start, stop, offset in runs(inside, inside + depth, part):
                    value = weight[offset : offset + stop - start, lanes]
                    target[side, p ^ ids_ref[0, 2], start:stop] = value
                for p, start, stop, offset in runs(inside + depth, inside + held, part):
                    value = small[offset : offset + stop - start]
                    target[side, p ^ ids_ref[0, 2], start:stop] = value

    pl.when(ids_ref[0, 0] == 0)(lambda: finish(0))
    pl.when(ids_ref[0, 0] != 0)(lambda: finish(1))
    for p, start, stop, _ in runs(per_block * held, parts * part, part):
        for side in range(halves):
            for ref in (keep_ref, send_ref):
                ref[side, p ^ ids_ref[0, 2], start:stop] = jnp.zeros((stop - start, 128), F32)


def vmem(count):
    return [pl.BlockSpec(memory_space=pltpu.VMEM)] * count


SCALARS = pl.BlockSpec(memory_space=pltpu.SMEM)


def pick(ids, index, rows):
    dp, slot = index.shape
    width = rows.shape[1]
    if dp > FEW:
        index = index.reshape(1, -1)
        shapes = [jax.ShapeDtypeStruct((dp * slot, width), BF16)]
    else:
        shapes = [jax.ShapeDtypeStruct((slot, width), BF16)] * dp
    return pl.pallas_call(
        pick_kernel,
        out_shape=shapes,
        in_specs=[SCALARS] + vmem(2),
        out_specs=vmem(len(shapes)),
        compiler_params=pltpu.CompilerParams(vmem_limit_bytes=VMEM_LIMIT),
        cost_estimate=pl.CostEstimate(
            flops=2 * dp * slot * rows.size, bytes_accessed=6 * rows.size, transcendentals=0
        ),
        name="pick_rows",
    )(ids, index, rows)


def unpack(ids, pieces, parts, part, depth, tap_count, width):
    return pl.pallas_call(
        functools.partial(unpack_kernel, len(pieces)),
        out_shape=[
            jax.ShapeDtypeStruct((depth, width), F32),
            jax.ShapeDtypeStruct((tap_count, width), F32),
            jax.ShapeDtypeStruct((1, width), F32),
        ],
        in_specs=[SCALARS] + vmem(len(pieces)),
        out_specs=vmem(3),
        scratch_shapes=[pltpu.VMEM((parts, part, 128), F32)],
        compiler_params=pltpu.CompilerParams(vmem_limit_bytes=VMEM_LIMIT),
        cost_estimate=pl.CostEstimate(flops=10**6, bytes_accessed=12 * 10**5, transcendentals=0),
        name="unpack_gradients",
    )(ids, *pieces)


def positions(utterances):
    steps = utterances.shape[0]
    place = jnp.arange(steps, dtype=jnp.int32) + GAP * utterances
    most = max(sum(sizes) for sizes in WIDE_K + BLOCK_K)
    lines = []
    for kind, (ranges, sizes_of) in enumerate(((WIDE_STEPS, WIDE_K), (BLOCK_STEPS, BLOCK_K))):
        for j in range(3):
            local = place - (STARTS[j] - GAP)
            low, high = (0, LENGTHS[j] + 2 * GAP) if kind == 0 else (GAP, LENGTHS[j] + GAP)
            local = jnp.where((local >= low) & (local < high), local, -1)
            inside = jnp.arange(steps)
            local = jnp.where((inside >= ranges[j][0]) & (inside < ranges[j][1]), local, -1)
            pieces = [local[a:b] for a, b in k_slices(ranges[j], sizes_of[j])]
            line = jnp.concatenate(pieces)
            lines.append(jnp.pad(line, (0, most - line.shape[0]), constant_values=-1))
    lines.extend([jnp.full((most,), -1, jnp.int32)] * 2)
    return jnp.stack(lines)


def prepare(utterances, f_hi, f_lo, back):
    shapes = [
        jax.ShapeDtypeStruct((POINTS, AHEAD_AT[-1]), BF16),
        jax.ShapeDtypeStruct((BEHIND_AT[-1], 3 * POINTS), BF16),
    ]
    return pl.pallas_call(
        prep_kernel,
        out_shape=shapes,
        in_specs=vmem(4),
        out_specs=vmem(2),
        compiler_params=pltpu.CompilerParams(vmem_limit_bytes=VMEM_LIMIT),
        cost_estimate=pl.CostEstimate(flops=3 * 10**9, bytes_accessed=8 * 10**6, transcendentals=0),
        name="prepare_transforms",
    )(positions(utterances), f_hi, f_lo, back)


def layer(
    ids, arrived, take, small, params, upstream, tap_fwd, lags, ahead, behind, parts, part, halves
):
    steps, width = upstream.shape
    depth = arrived[0].shape[1] // 2
    hbm = pl.BlockSpec(memory_space=pltpu.HBM)
    scratch = [
        pltpu.VMEM(params.shape, BF16),
        pltpu.VMEM(upstream.shape, BF16),
        pltpu.VMEM(ahead.shape, BF16),
        pltpu.VMEM(behind.shape, BF16),
        pltpu.SemaphoreType.DMA((4,)),
        pltpu.VMEM((steps, depth), BF16),
        pltpu.VMEM((depth, steps), BF16),
        pltpu.VMEM((steps, width), F32),
        pltpu.VMEM((steps, width), F32),
        pltpu.VMEM((3, steps, 128), F32),
        pltpu.VMEM((steps, 128), F32),
        pltpu.VMEM((steps, 128), F32),
        pltpu.VMEM((steps, CH), BF16),
        pltpu.VMEM((steps, CH), BF16),
        pltpu.VMEM((steps, CH), BF16),
        pltpu.VMEM((steps, CH), BF16),
        pltpu.VMEM((3, POINTS, CH), F32),
        pltpu.VMEM((3, POINTS, CH), F32),
        pltpu.VMEM((4, POINTS, CH), BF16),
        pltpu.VMEM((4, POINTS, CH), BF16),
        pltpu.VMEM((POINTS, CH), F32),
        pltpu.VMEM((steps, CH), F32),
        pltpu.VMEM((32, width), F32),
        pltpu.VMEM((1, CH), F32),
    ]
    return pl.pallas_call(
        functools.partial(layer_kernel, len(arrived)),
        out_shape=[
            jax.ShapeDtypeStruct((halves, parts, part, 128), F32),
            jax.ShapeDtypeStruct((halves, parts, part, 128), F32),
            jax.ShapeDtypeStruct((1, 1), F32),
        ],
        in_specs=[SCALARS] + vmem(len(arrived) + 4) + [hbm] * 4,
        out_specs=vmem(3),
        scratch_shapes=scratch,
        compiler_params=pltpu.CompilerParams(vmem_limit_bytes=VMEM_LIMIT),
        cost_estimate=pl.CostEstimate(flops=10**10, bytes_accessed=16 * 10**6, transcendentals=10**6),
        name="layer_step",
    )(ids, *arrived, take, tap_fwd, lags, small, params, upstream, ahead, behind)


def per_device(
    dp, fsdp, cached, send_rows, take_rows, utt_index, upstream, in_proj, norm_gain, conv_kernel
):
    tap_count = conv_kernel.shape[0]
    f_hi, f_lo, back, tap_fwd, lags = [jnp.asarray(m) for m in transforms(tap_count)]
    params = lax.all_gather(in_proj, "fsdp", axis=1, tiled=True)
    few = dp <= FEW
    place = lax.axis_index("fsdp")
    ours = lax.axis_index("dp") if few else 0
    ids = jnp.stack([place % 2, place // 2, ours]).astype(jnp.int32)[None, :]
    wanted = send_rows[0, 0]
    outgoing = pick(ids, wanted, cached[0, 0])
    outgoing, take_own, utt_own, taps_own, gain_own = lax.optimization_barrier(
        (outgoing, take_rows[0, 0], utt_index[0, 0], conv_kernel, norm_gain)
    )

    def swap(value, k):
        return lax.ppermute(value, "dp", [(i, i ^ k) for i in range(dp)])

    far_first = [k for k in range(dp // 2, dp)] + [k for k in range(dp // 2 - 1, 0, -1)]
    if few:
        got = {k: swap(outgoing[k], k) for k in far_first}
        arrived = [outgoing[0]] + [got[k] for k in range(1, dp)]
        take_own = jnp.where(take_own >= 0, take_own ^ (ours * wanted.shape[1]), -1)
    else:
        sent = outgoing[0].reshape(wanted.shape + outgoing[0].shape[1:])
        back_in = lax.all_to_all(sent, "dp", split_axis=0, concat_axis=0, tiled=True)
        arrived = [back_in.reshape(-1, back_in.shape[2])]
    small = lax.all_gather(
        jnp.concatenate([taps_own, gain_own[None, :]], axis=0), "fsdp", axis=1, tiled=True
    )
    take = jnp.repeat(take_own, 2)[None, :]
    ahead, behind = prepare(jnp.repeat(utt_own, 2), f_hi, f_lo, back)

    depth, shard_cols = in_proj.shape
    held = depth + 32
    tiles = shard_cols // 128
    part = -(-(held * tiles) // dp)
    part = -(-part // 16) * 16
    halves = fsdp // 2
    keep, send, loss = layer(
        ids, arrived, take, small, params, upstream[0, 0], tap_fwd, lags, ahead, behind,
        dp, part, halves,
    )
    other = lax.ppermute(send, "fsdp", [(i, i ^ 1) for i in range(fsdp)])
    half = dp // 2
    across = [(i, i ^ 2) for i in range(fsdp)]
    sums = {}
    for low, high in ((half, dp), (0, half)):
        theirs = (keep[1, low:high] + other[1, low:high]).astype(BF16)
        theirs = lax.ppermute(theirs, "fsdp", across)
        mine = keep[0, low:high] + other[0, low:high]
        sums[low] = mine + theirs.astype(F32)
    if few:
        got = {}
        for k in far_first:
            low = half if k >= half else 0
            got[k] = swap(sums[low][k - low].astype(BF16), k)
        total = sums[0][0]
        for k in range(1, dp):
            total = total + got[k].astype(F32)
        piece = total.astype(BF16)
        far = {k: swap(piece, k) for k in range(dp - 2, 0, -2)}
        pieces = {0: piece, 1: swap(piece, 1), **far}
        for k in far:
            pieces[k + 1] = swap(far[k], 1)
        pieces = [pieces[k] for k in range(dp)]
    else:
        chip = jnp.concatenate([sums[0], sums[half]], axis=0).astype(BF16)
        shared = lax.all_to_all(chip, "dp", split_axis=0, concat_axis=0, tiled=True)
        piece = jnp.sum(shared.astype(F32), axis=0).astype(BF16)
        pieces = [lax.all_gather(piece, "dp", axis=0, tiled=True)]
    proj, taps, gain = unpack(ids, pieces, dp, part, depth, tap_count, shard_cols)
    return (proj, taps, gain[0], loss)


def solution(mesh):
    placed = (
        P("dp", "fsdp", None, None),
        P("dp", "fsdp", None, None),
        P("dp", "fsdp", None),
        P("dp", "fsdp", None),
        P("dp", "fsdp", None, None),
        P(None, "fsdp"),
        P("fsdp"),
        P(None, "fsdp"),
    )
    return jax.shard_map(
        functools.partial(per_device, mesh.shape["dp"], mesh.shape["fsdp"]),
        mesh=mesh,
        in_specs=placed,
        out_specs=(P(None, "fsdp"), P(None, "fsdp"), P("fsdp"), P("dp", "fsdp")),
        check_vma=False,
    )
```

```python
import functools
import math

import jax
import jax.numpy as jnp
import numpy as np
from jax import lax
from jax.experimental import pallas as pl
from jax.experimental.pallas import tpu as pltpu
from jax.sharding import PartitionSpec as P

GAP = 16
POINTS = 256
FREQS = 128
STARTS = (0, 224, 432)
LENGTHS = (224, 208, 224)
BLOCK_STEPS = ((0, 208), (128, 384), (304, 512))
WIDE_STEPS = ((0, 224), (112, 400), (288, 512))
BLOCK_K = ((208, 208, 224), (256, 256, 256), (208, 208, 224))
WIDE_K = ((224, 224, 320), (288, 288, 320), (224, 224, 320))
AHEAD_AT = tuple(int(v) for v in np.cumsum([0] + [sum(k) for k in WIDE_K + BLOCK_K]))
BEHIND_AT = tuple(int(v) for v in np.cumsum([0] + [b - a for a, b in WIDE_STEPS + BLOCK_STEPS]))
CH = 256
ROWS = 64
F32 = jnp.float32
BF16 = jnp.bfloat16
VMEM_LIMIT = 60 * 1024 * 1024
FEW = 16


def k_slices(steps, sizes):
    out = []
    for size in sizes:
        first = steps[0] if steps[0] + size <= 512 else 512 - size
        out.append((first, first + size))
    return out


def split(value):
    hi = value.astype(BF16)
    return hi, (value - hi.astype(F32)).astype(BF16)


def split_np(value):
    hi = value.astype(jnp.bfloat16)
    lo = (value - hi.astype(np.float64)).astype(jnp.bfloat16)
    return hi, lo


def transforms(tap_count):
    omega = 2 * np.pi * (np.arange(FREQS) + 0.5) / POINTS
    angle = omega[:, None] * np.arange(POINTS)[None, :]
    forward = np.concatenate([np.cos(angle), -np.sin(angle)], axis=0)
    f_hi, f_lo = split_np(forward)
    back = np.concatenate([f_hi.T, f_lo.T, f_hi.T], axis=1)
    shift = omega[:, None] * (np.arange(32) - tap_count // 2)[None, :]
    tap_ok = (np.arange(32) < tap_count)[None, :]
    taps = np.concatenate([np.cos(shift), np.sin(shift)], axis=0) * tap_ok / FREQS
    t_hi, t_lo = split_np(taps)
    tap_fwd = np.concatenate([t_hi, t_lo], axis=1)
    lag = np.concatenate([np.cos(shift), -np.sin(shift)], axis=0) * tap_ok / FREQS
    l_hi, l_lo = split_np(lag.T)
    lags = np.concatenate([l_hi, l_lo, l_hi], axis=1)
    return f_hi, f_lo, back, tap_fwd, lags


def dot(a, b):
    return jnp.dot(a, b, preferred_element_type=F32)


def dot_t(a, b):
    return lax.dot_general(a, b, (((0,), (0,)), ((), ())), preferred_element_type=F32)


def pick_kernel(ours_ref, index_ref, rows_ref, proj_ref, taps_ref, gain_ref, packed_ref, *refs):
    out_refs, tail_ref = refs[:-1], refs[-1]
    depth, tap_count = proj_ref.shape[0], taps_ref.shape[0]
    packed_ref[:depth] = proj_ref[...]
    tail_ref[:tap_count] = taps_ref[...].astype(F32)
    tail_ref[tap_count:] = gain_ref[...].astype(F32)
    packed_ref[depth:] = tail_ref[...].astype(BF16)
    count = rows_ref.shape[0]
    rows = rows_ref[...]
    if len(out_refs) == 1:
        index = index_ref[...]
        number = lax.broadcasted_iota(jnp.int32, (count, index.shape[1]), 0)
        choose = jnp.where(number == index, 1.0, 0.0).astype(BF16)
        out_refs[0][...] = dot_t(choose, rows).astype(BF16)
        return
    slot = index_ref.shape[1]
    number = lax.broadcasted_iota(jnp.int32, (count, slot), 0)
    for k, out_ref in enumerate(out_refs):
        index = index_ref[pl.ds(ours_ref[0, 0] ^ k, 1), :]
        choose = jnp.where(number == index, 1.0, 0.0).astype(BF16)
        out_ref[...] = dot_t(choose, rows).astype(BF16)


def runs(first, last, part):
    out = []
    row = first
    while row < last:
        stop = min(last, (row // part + 1) * part)
        out.append((row // part, row % part, row % part + stop - row, row - first))
        row = stop
    return out


def unpack_kernel(count, ours_ref, *refs):
    piece_refs, (proj_ref, taps_ref, gain_ref, held_ref) = refs[:count], refs[count:]
    parts, part, _ = held_ref.shape
    for k in range(parts):
        piece = piece_refs[k][...] if count == parts else piece_refs[0][k * part : (k + 1) * part]
        held_ref[k] = piece.astype(F32)
    depth, width = proj_ref.shape
    held = depth + 32
    for tile in range(width // 128):
        lanes = slice(tile * 128, tile * 128 + 128)
        for p, start, stop, offset in runs(tile * held, tile * held + depth, part):
            proj_ref[offset : offset + stop - start, lanes] = held_ref[p ^ ours_ref[0, 0], start:stop]
        last = [
            held_ref[p ^ ours_ref[0, 0], start:stop]
            for p, start, stop, _ in runs(tile * held + depth, tile * held + held, part)
        ]
        last = last[0] if len(last) == 1 else jnp.concatenate(last, axis=0)
        taps_ref[:, lanes] = last[: taps_ref.shape[0]]
        gain_ref[lanes] = last[taps_ref.shape[0] : taps_ref.shape[0] + 1].reshape(128)


def prep_kernel(pos_ref, hi_ref, lo_ref, back_ref, ahead_ref, behind_ref):
    f_hi = hi_ref[...]
    f_lo = lo_ref[...]
    back = back_ref[...]
    for part in range(6):
        sizes = (WIDE_K + BLOCK_K)[part]
        steps = (WIDE_STEPS + BLOCK_STEPS)[part]
        total = sum(sizes)
        place = pos_ref[part : part + 1, :total]
        number = lax.broadcasted_iota(jnp.int32, (POINTS, total), 0)
        hot = jnp.where(number == place, 1.0, 0.0).astype(BF16)
        lane = lax.broadcasted_iota(jnp.int32, (1, total), 1)
        middle = (lane >= sizes[0]) & (lane < sizes[0] + sizes[1])
        ahead = jnp.where(middle, dot(f_lo, hot), dot(f_hi, hot)).astype(BF16)
        ahead_ref[:, AHEAD_AT[part] : AHEAD_AT[part + 1]] = ahead
        held = steps[1] - steps[0]
        padded = -(-held // 128) * 128
        wide = dot_t(hot[:, :padded], back)
        behind_ref[BEHIND_AT[part] : BEHIND_AT[part + 1]] = wide[:held].astype(BF16)


def layer_kernel(count, core_ref, side_ref, ours_ref, *refs):
    arrived_refs = refs[:count]
    (
        take_ref, tapf_ref, lag_ref, params_hbm, up_hbm, ahead_hbm, behind_hbm,
        keep_ref, send_ref, loss_ref,
        params_ref, up_ref, ahead_ref, behind_ref, sems,
        frames_ref, frames_t_ref, x_ref, h_ref, stat_ref, acc_ref, acc2_ref,
        hi_ref, lo_ref, ghi_ref, glo_ref, spec_ref, nspec_ref, phi_ref, plo_ref,
        coef_ref, c_ref, small_ref, lossacc_ref,
    ) = refs[count:]
    copies = [
        pltpu.make_async_copy(source, target, sems.at[k])
        for k, (source, target) in enumerate(
            ((params_hbm, params_ref), (ahead_hbm, ahead_ref), (behind_hbm, behind_ref), (up_hbm, up_ref))
        )
    ]
    for copy in copies:
        copy.start()
    steps, width = up_ref.shape
    slots = sum(ref.shape[0] for ref in arrived_refs)
    pair_width = arrived_refs[0].shape[1]
    depth = pair_width // 2
    chunks = width // CH
    scale = (steps * width) ** -0.5
    tiles = [slice(r, r + ROWS) for r in range(0, steps, ROWS)]
    wide_of = [slice(AHEAD_AT[j], AHEAD_AT[j + 1]) for j in range(3)]
    block_of = [slice(AHEAD_AT[j], AHEAD_AT[j + 1]) for j in range(3, 6)]
    back_wide = [slice(BEHIND_AT[j], BEHIND_AT[j + 1]) for j in range(3)]
    back_block = [slice(BEHIND_AT[j], BEHIND_AT[j + 1]) for j in range(3, 6)]

    take = take_ref[...]
    number = lax.broadcasted_iota(jnp.int32, (slots, steps), 0)
    odd = lax.broadcasted_iota(jnp.int32, (slots, steps), 1) % 2
    here = number == take
    even_hot = jnp.where(here & (odd == 0), 1.0, 0.0).astype(BF16)
    odd_hot = jnp.where(here & (odd == 1), 1.0, 0.0).astype(BF16)
    first = jnp.concatenate([ref[:, :depth] for ref in arrived_refs], axis=0)
    second = jnp.concatenate([ref[:, depth:] for ref in arrived_refs], axis=0)
    frames = dot_t(even_hot, first) + dot_t(odd_hot, second)
    frames_ref[...] = frames.astype(BF16)
    frames_t_ref[...] = jnp.transpose(frames).astype(BF16)
    live = dot_t(even_hot + odd_hot, jnp.ones((slots, 128), BF16))
    stat_ref[2] = live * scale

    acc_ref[...] = jnp.zeros_like(acc_ref)
    copies[0].wait()

    def project(i, carry):
        cols = pl.ds(pl.multiple_of(i * CH, CH), CH)
        x = dot(frames_ref[...], params_ref[:depth, cols])
        x_ref[:, cols] = x
        acc_ref[...] += x[:, :128] + x[:, 128:]
        return carry

    lax.fori_loop(0, chunks, project, 0)
    mean = jnp.sum(acc_ref[...], axis=1, keepdims=True) * (1.0 / width)
    stat_ref[0] = jnp.broadcast_to(mean, (steps, 128))

    for rows in tiles:
        m = stat_ref[0, rows]
        total = jnp.zeros((ROWS, 128), F32)
        for k in range(width // 128):
            d = x_ref[rows, k * 128 : (k + 1) * 128] - m
            total = total + d * d
        var = jnp.sum(total, axis=1, keepdims=True) * (1.0 / width)
        stat_ref[1, rows] = jnp.broadcast_to(lax.rsqrt(var + 1e-05), (ROWS, 128))

    acc_ref[...] = jnp.zeros_like(acc_ref)
    acc2_ref[...] = jnp.zeros_like(acc2_ref)
    lossacc_ref[...] = jnp.zeros_like(lossacc_ref)

    for copy in copies[1:]:
        copy.wait()

    def twice(value):
        return jnp.concatenate([value, value], axis=1)

    def stack(hi, lo, slices):
        (a, b), (c, d), (e, f) = slices
        return jnp.concatenate([hi[a:b], hi[c:d], lo[e:f]], axis=0)

    def chunk(i, b):
        hi_b, lo_b, ghi_b, glo_b = hi_ref.at[b], lo_ref.at[b], ghi_ref.at[b], glo_ref.at[b]
        spec_b, nspec_b, phi_b, plo_b = spec_ref.at[b], nspec_ref.at[b], phi_ref.at[b], plo_ref.at[b]
        coef_b, c_b = coef_ref.at[b], c_ref.at[b]
        cols = pl.ds(pl.multiple_of(i * CH, CH), CH)
        gain = params_ref[depth + 16 : depth + 32, cols][15:16].astype(F32)
        taps = params_ref[depth : depth + 32, cols]
        coef_b[...] = dot(tapf_ref[...], jnp.concatenate([taps, taps], axis=0))
        for t, rows in enumerate(tiles):
            xhat = (x_ref[rows, cols] - twice(stat_ref[0, rows])) * twice(stat_ref[1, rows])
            hi, lo = split(xhat * gain)
            hi_b[rows] = hi
            lo_b[rows] = lo
            if t in (2, 5):
                yield
        yield
        for j in range(3):
            nspec_b[j] = dot(ahead_ref[:, block_of[j]], stack(hi_b, lo_b, k_slices(BLOCK_STEPS[j], BLOCK_K[j])))
            yield
        for j in range(3):
            for f in range(0, FREQS, 32):
                lower, upper = slice(f, f + 32), slice(FREQS + f, FREQS + f + 32)
                re, im = nspec_b[j, lower], nspec_b[j, upper]
                cre, cim = coef_b[lower], coef_b[upper]
                hi, lo = split(re * cre - im * cim)
                phi_b[j, lower] = hi
                plo_b[j, lower] = lo
                hi, lo = split(re * cim + im * cre)
                phi_b[j, upper] = hi
                plo_b[j, upper] = lo
            yield
        parts = []
        for j in range(3):
            held_j = jnp.concatenate([phi_b[j], phi_b[j], plo_b[j]], axis=0)
            parts.append(dot(behind_ref[back_wide[j]], held_j))
            if j == 1:
                c_b[0:112] = parts[0][0:112]
                c_b[112:224] = parts[0][112:224] + parts[1][0:112]
                c_b[224:288] = parts[1][112:176]
            if j == 2:
                c_b[288:400] = parts[1][176:288] + parts[2][0:112]
                c_b[400:512] = parts[2][112:224]
            yield
        loss = jnp.zeros((1, CH), F32)
        for t, rows in enumerate(tiles):
            conv = c_b[rows]
            sig = jax.nn.sigmoid(conv)
            go = up_ref[rows, cols].astype(F32) * twice(stat_ref[2, rows])
            out = x_ref[rows, cols] + conv * sig
            loss = loss + jnp.sum(out * go, axis=0, keepdims=True)
            hi, lo = split(go * (sig * (1.0 + conv * (1.0 - sig))))
            ghi_b[rows] = hi
            glo_b[rows] = lo
            if t in (2, 5):
                yield
        lossacc_ref[...] += loss
        yield
        for j in range(3):
            spec_b[j] = dot(ahead_ref[:, wide_of[j]], stack(ghi_b, glo_b, k_slices(WIDE_STEPS[j], WIDE_K[j])))
            yield
        for f in range(0, FREQS, 32):
            lower, upper = slice(f, f + 32), slice(FREQS + f, FREQS + f + 32)
            cre, cim = coef_b[lower], coef_b[upper]
            zre = jnp.zeros((32, CH), F32)
            zim = jnp.zeros((32, CH), F32)
            for j in range(3):
                nre, nim = nspec_b[j, lower], nspec_b[j, upper]
                re, im = spec_b[j, lower], spec_b[j, upper]
                zre = zre + (nre * re + nim * im)
                zim = zim + (nim * re - nre * im)
                hi, lo = split(re * cre + im * cim)
                phi_b[j, lower] = hi
                plo_b[j, lower] = lo
                hi, lo = split(im * cre - re * cim)
                phi_b[j, upper] = hi
                plo_b[j, upper] = lo
            hi, lo = split(zre)
            phi_b[3, lower] = hi
            plo_b[3, lower] = lo
            hi, lo = split(zim)
            phi_b[3, upper] = hi
            plo_b[3, upper] = lo
            if f != 32:
                yield
        parts = []
        for j in range(3):
            held_j = jnp.concatenate([phi_b[j], phi_b[j], plo_b[j]], axis=0)
            parts.append(dot(behind_ref[back_block[j]], held_j))
            if j == 1:
                c_b[0:128] = parts[0][0:128]
                c_b[128:208] = parts[0][128:208] + parts[1][0:80]
                c_b[208:304] = parts[1][80:176]
            if j == 2:
                c_b[304:384] = parts[1][176:256] + parts[2][0:80]
                c_b[384:512] = parts[2][80:208]
            yield
        tap_grad = dot(lag_ref[...], jnp.concatenate([phi_b[3], phi_b[3], plo_b[3]], axis=0))
        gain_grad = jnp.zeros((1, CH), F32)
        for t, rows in enumerate(tiles):
            gn = c_b[rows]
            xhat = (x_ref[rows, cols] - twice(stat_ref[0, rows])) * twice(stat_ref[1, rows])
            gain_grad = gain_grad + jnp.sum(gn * xhat, axis=0, keepdims=True)
            h = gn * gain
            hx = h * xhat
            h_ref[rows, cols] = h
            acc_ref[rows] += h[:, :128] + h[:, 128:]
            acc2_ref[rows] += hx[:, :128] + hx[:, 128:]
            if t in (2, 5):
                yield
        last = lax.broadcasted_iota(jnp.int32, (32, CH), 0) == 31
        small_ref[:, cols] = jnp.where(last, gain_grad, tap_grad)

    def middle(i, carry):
        lead, follow = chunk(2 * i, 0), chunk(2 * i + 1, 1)
        for _ in range(3):
            next(lead)
        running = [lead, follow]
        while running:
            running = [g for g in running if next(g, running) is not running]
        return carry

    lax.fori_loop(0, chunks // 2, middle, 0)
    loss_ref[...] = jnp.sum(lossacc_ref[...], axis=1, keepdims=True)
    for rows in tiles:
        m1 = jnp.sum(acc_ref[rows], axis=1, keepdims=True) * (1.0 / width)
        m2 = jnp.sum(acc2_ref[rows], axis=1, keepdims=True) * (1.0 / width)
        acc_ref[rows] = jnp.broadcast_to(m1, (ROWS, 128))
        acc2_ref[rows] = jnp.broadcast_to(m2, (ROWS, 128))

    halves, parts, part, _ = keep_ref.shape
    per_block = width // (2 * halves) // 128
    held = depth + 32

    def grad_rows(i):
        cols = slice(i * CH, (i + 1) * CH)
        for rows in tiles:
            inv = twice(stat_ref[1, rows])
            xhat = (x_ref[rows, cols] - twice(stat_ref[0, rows])) * inv
            go = up_ref[rows, cols].astype(F32) * twice(stat_ref[2, rows])
            inner = h_ref[rows, cols] - twice(acc_ref[rows]) - xhat * twice(acc2_ref[rows])
            hi_ref[i % 2, rows] = (go + inv * inner).astype(BF16)

    def finish(core):
        grad_rows(0)
        for i in range(chunks):
            if i + 1 < chunks:
                grad_rows(i + 1)
            weight = dot(frames_t_ref[...], hi_ref[i % 2])
            for half in range(CH // 128):
                tile = i * (CH // 128) + half
                block, inside = tile // per_block, (tile % per_block) * held
                lanes = slice(half * 128, half * 128 + 128)
                small = small_ref[:, tile * 128 : (tile + 1) * 128]
                target = keep_ref if block % 2 == core else send_ref
                side = (block // 2) ^ side_ref[0, 0]
                for p, start, stop, offset in runs(inside, inside + depth, part):
                    value = weight[offset : offset + stop - start, lanes]
                    target[side, p ^ ours_ref[0, 0], start:stop] = value
                for p, start, stop, offset in runs(inside + depth, inside + held, part):
                    value = small[offset : offset + stop - start]
                    target[side, p ^ ours_ref[0, 0], start:stop] = value

    pl.when(core_ref[0, 0] == 0)(lambda: finish(0))
    pl.when(core_ref[0, 0] != 0)(lambda: finish(1))
    for p, start, stop, _ in runs(per_block * held, parts * part, part):
        for side in range(halves):
            for ref in (keep_ref, send_ref):
                ref[side, p ^ ours_ref[0, 0], start:stop] = jnp.zeros((stop - start, 128), F32)


def vmem(count):
    return [pl.BlockSpec(memory_space=pltpu.VMEM)] * count


SCALARS = pl.BlockSpec(memory_space=pltpu.SMEM)


def pick(ours, index, rows, proj, taps, gain):
    dp, slot = index.shape
    width = rows.shape[1]
    if dp > FEW:
        index = index.reshape(1, -1)
        shapes = [jax.ShapeDtypeStruct((dp * slot, width), BF16)]
    else:
        shapes = [jax.ShapeDtypeStruct((slot, width), BF16)] * dp
    return pl.pallas_call(
        pick_kernel,
        out_shape=[jax.ShapeDtypeStruct((proj.shape[0] + 32, proj.shape[1]), BF16)] + shapes,
        in_specs=[SCALARS] + vmem(5),
        out_specs=vmem(1 + len(shapes)),
        scratch_shapes=[pltpu.VMEM((32, proj.shape[1]), F32)],
        compiler_params=pltpu.CompilerParams(vmem_limit_bytes=VMEM_LIMIT),
        cost_estimate=pl.CostEstimate(
            flops=2 * dp * slot * rows.size, bytes_accessed=6 * rows.size, transcendentals=0
        ),
        name="pick_rows",
    )(ours, index, rows, proj, taps, gain)


def unpack(ours, pieces, parts, part, depth, tap_count, width):
    return pl.pallas_call(
        functools.partial(unpack_kernel, len(pieces)),
        out_shape=[
            jax.ShapeDtypeStruct((depth, width), F32),
            jax.ShapeDtypeStruct((tap_count, width), F32),
            jax.ShapeDtypeStruct((width,), F32),
        ],
        in_specs=[SCALARS] + vmem(len(pieces)),
        out_specs=vmem(3),
        scratch_shapes=[pltpu.VMEM((parts, part, 128), F32)],
        compiler_params=pltpu.CompilerParams(vmem_limit_bytes=VMEM_LIMIT),
        cost_estimate=pl.CostEstimate(flops=10**6, bytes_accessed=12 * 10**5, transcendentals=0),
        name="unpack_gradients",
    )(ours, *pieces)


def positions(utterances):
    steps = utterances.shape[0]
    place = jnp.arange(steps, dtype=jnp.int32) + GAP * utterances
    most = max(sum(sizes) for sizes in WIDE_K + BLOCK_K)
    lines = []
    for kind, (ranges, sizes_of) in enumerate(((WIDE_STEPS, WIDE_K), (BLOCK_STEPS, BLOCK_K))):
        for j in range(3):
            local = place - (STARTS[j] - GAP)
            low, high = (0, LENGTHS[j] + 2 * GAP) if kind == 0 else (GAP, LENGTHS[j] + GAP)
            local = jnp.where((local >= low) & (local < high), local, -1)
            inside = jnp.arange(steps)
            local = jnp.where((inside >= ranges[j][0]) & (inside < ranges[j][1]), local, -1)
            pieces = [local[a:b] for a, b in k_slices(ranges[j], sizes_of[j])]
            line = jnp.concatenate(pieces)
            lines.append(jnp.pad(line, (0, most - line.shape[0]), constant_values=-1))
    lines.extend([jnp.full((most,), -1, jnp.int32)] * 2)
    return jnp.stack(lines)


def prepare(utterances, f_hi, f_lo, back):
    shapes = [
        jax.ShapeDtypeStruct((POINTS, AHEAD_AT[-1]), BF16),
        jax.ShapeDtypeStruct((BEHIND_AT[-1], 3 * POINTS), BF16),
    ]
    return pl.pallas_call(
        prep_kernel,
        out_shape=shapes,
        in_specs=vmem(4),
        out_specs=vmem(2),
        compiler_params=pltpu.CompilerParams(vmem_limit_bytes=VMEM_LIMIT),
        cost_estimate=pl.CostEstimate(flops=3 * 10**9, bytes_accessed=8 * 10**6, transcendentals=0),
        name="prepare_transforms",
    )(positions(utterances), f_hi, f_lo, back)


def layer(
    ids, arrived, take, params, upstream, tap_fwd, lags, ahead, behind, parts, part, halves
):
    steps, width = upstream.shape
    depth = arrived[0].shape[1] // 2
    hbm = pl.BlockSpec(memory_space=pltpu.HBM)
    scratch = [
        pltpu.VMEM(params.shape, BF16),
        pltpu.VMEM(upstream.shape, BF16),
        pltpu.VMEM(ahead.shape, BF16),
        pltpu.VMEM(behind.shape, BF16),
        pltpu.SemaphoreType.DMA((4,)),
        pltpu.VMEM((steps, depth), BF16),
        pltpu.VMEM((depth, steps), BF16),
        pltpu.VMEM((steps, width), F32),
        pltpu.VMEM((steps, width), F32),
        pltpu.VMEM((3, steps, 128), F32),
        pltpu.VMEM((steps, 128), F32),
        pltpu.VMEM((steps, 128), F32),
        pltpu.VMEM((2, steps, CH), BF16),
        pltpu.VMEM((2, steps, CH), BF16),
        pltpu.VMEM((2, steps, CH), BF16),
        pltpu.VMEM((2, steps, CH), BF16),
        pltpu.VMEM((2, 3, POINTS, CH), F32),
        pltpu.VMEM((2, 3, POINTS, CH), F32),
        pltpu.VMEM((2, 4, POINTS, CH), BF16),
        pltpu.VMEM((2, 4, POINTS, CH), BF16),
        pltpu.VMEM((2, POINTS, CH), F32),
        pltpu.VMEM((2, steps, CH), F32),
        pltpu.VMEM((32, width), F32),
        pltpu.VMEM((1, CH), F32),
    ]
    return pl.pallas_call(
        functools.partial(layer_kernel, len(arrived)),
        out_shape=[
            jax.ShapeDtypeStruct((halves, parts, part, 128), F32),
            jax.ShapeDtypeStruct((halves, parts, part, 128), F32),
            jax.ShapeDtypeStruct((1, 1), F32),
        ],
        in_specs=[SCALARS] * 3 + vmem(len(arrived) + 3) + [hbm] * 4,
        out_specs=vmem(3),
        scratch_shapes=scratch,
        compiler_params=pltpu.CompilerParams(vmem_limit_bytes=VMEM_LIMIT),
        cost_estimate=pl.CostEstimate(flops=10**10, bytes_accessed=16 * 10**6, transcendentals=10**6),
        name="layer_step",
    )(*ids, *arrived, take, tap_fwd, lags, params, upstream, ahead, behind)


def per_device(
    dp, fsdp, cached, send_rows, take_rows, utt_index, upstream, in_proj, norm_gain, conv_kernel
):
    tap_count = conv_kernel.shape[0]
    f_hi, f_lo, back, tap_fwd, lags = [jnp.asarray(m) for m in transforms(tap_count)]
    few = dp <= FEW
    place = lax.axis_index("fsdp")
    ours = lax.axis_index("dp") if few else jnp.zeros((), jnp.int32)
    ids = [v.astype(jnp.int32).reshape(1, 1) for v in (place % 2, place // 2, ours)]
    wanted = send_rows[0, 0]
    packed, *outgoing = pick(ids[2], wanted, cached[0, 0], in_proj, conv_kernel, norm_gain[None, :])
    params = lax.all_gather(packed, "fsdp", axis=1, tiled=True)
    outgoing, take_own, utt_own = lax.optimization_barrier(
        (outgoing, take_rows[0, 0], utt_index[0, 0])
    )

    def swap(value, k):
        return lax.ppermute(value, "dp", [(i, i ^ k) for i in range(dp)])

    far_first = [k for k in range(dp // 2, dp)] + [k for k in range(dp // 2 - 1, 0, -1)]
    if few:
        got = {k: swap(outgoing[k], k) for k in far_first}
        arrived = [outgoing[0]] + [got[k] for k in range(1, dp)]
        take_own = jnp.where(take_own >= 0, take_own ^ (ours * wanted.shape[1]), -1)
    else:
        sent = outgoing[0].reshape(wanted.shape + outgoing[0].shape[1:])
        back_in = lax.all_to_all(sent, "dp", split_axis=0, concat_axis=0, tiled=True)
        arrived = [back_in.reshape(-1, back_in.shape[2])]
    take = jnp.repeat(take_own, 2)[None, :]
    ahead, behind = prepare(jnp.repeat(utt_own, 2), f_hi, f_lo, back)

    depth, shard_cols = in_proj.shape
    held = depth + 32
    tiles = shard_cols // 128
    part = -(-(held * tiles) // dp)
    part = -(-part // 16) * 16
    halves = fsdp // 2
    keep, send, loss = layer(
        ids, arrived, take, params, upstream[0, 0], tap_fwd, lags, ahead, behind,
        dp, part, halves,
    )
    other = lax.ppermute(send, "fsdp", [(i, i ^ 1) for i in range(fsdp)])
    half = dp // 2
    across = [(i, i ^ 2) for i in range(fsdp)]
    spans = ((half, dp), (0, half))
    sent = [(keep[1, low:high] + other[1, low:high]).astype(BF16) for low, high in spans]
    far_in, near_in = [lax.ppermute(v, "fsdp", across) for v in sent]
    far_sum = keep[0, half:] + other[0, half:] + far_in.astype(F32)
    far_out = far_sum.astype(BF16)
    near_in, far_out = lax.optimization_barrier((near_in, far_out))
    near_sum = keep[0, :half] + other[0, :half] + near_in.astype(F32)
    near_out = near_sum.astype(BF16)
    if few:
        got = {}
        for k in far_first:
            got[k] = swap(far_out[k - half] if k >= half else near_out[k], k)
        total = near_sum[0]
        for k in range(1, dp):
            total = total + got[k].astype(F32)
        piece = total.astype(BF16)
        far = {k: swap(piece, k) for k in range(dp - 2, 0, -2)}
        pieces = {0: piece, 1: swap(piece, 1), **far}
        for k in far:
            pieces[k + 1] = swap(far[k], 1)
        pieces = [pieces[k] for k in range(dp)]
    else:
        chip = jnp.concatenate([near_out, far_out], axis=0)
        shared = lax.all_to_all(chip, "dp", split_axis=0, concat_axis=0, tiled=True)
        piece = jnp.sum(shared.astype(F32), axis=0).astype(BF16)
        pieces = [lax.all_gather(piece, "dp", axis=0, tiled=True)]
    proj, taps, gain = unpack(ids[2], pieces, dp, part, depth, tap_count, shard_cols)
    return (proj, taps, gain, loss)


def solution(mesh):
    placed = (
        P("dp", "fsdp", None, None),
        P("dp", "fsdp", None, None),
        P("dp", "fsdp", None),
        P("dp", "fsdp", None),
        P("dp", "fsdp", None, None),
        P(None, "fsdp"),
        P("fsdp"),
        P(None, "fsdp"),
    )
    return jax.shard_map(
        functools.partial(per_device, mesh.shape["dp"], mesh.shape["fsdp"]),
        mesh=mesh,
        in_specs=placed,
        out_specs=(P(None, "fsdp"), P(None, "fsdp"), P("fsdp"), P("dp", "fsdp")),
        check_vma=False,
    )
```

```python
import functools
import math

import jax
import jax.numpy as jnp
import numpy as np
from jax import lax
from jax.experimental import pallas as pl
from jax.experimental.pallas import tpu as pltpu
from jax.sharding import PartitionSpec as P

GAP = 16
POINTS = 256
FREQS = 128
STARTS = (0, 224, 432)
LENGTHS = (224, 208, 224)
BLOCK_STEPS = ((0, 208), (128, 384), (304, 512))
WIDE_STEPS = ((0, 224), (112, 400), (288, 512))
BLOCK_K = ((208, 208, 224), (256, 256, 256), (208, 208, 224))
WIDE_K = ((224, 224, 320), (288, 288, 320), (224, 224, 320))
AHEAD_AT = tuple(int(v) for v in np.cumsum([0] + [sum(k) for k in WIDE_K + BLOCK_K]))
BEHIND_AT = tuple(int(v) for v in np.cumsum([0] + [b - a for a, b in WIDE_STEPS + BLOCK_STEPS]))
CH = 256
ROWS = 64
F32 = jnp.float32
BF16 = jnp.bfloat16
VMEM_LIMIT = 60 * 1024 * 1024
FEW = 16


def k_slices(steps, sizes):
    out = []
    for size in sizes:
        first = steps[0] if steps[0] + size <= 512 else 512 - size
        out.append((first, first + size))
    return out


def split(value):
    hi = value.astype(BF16)
    return hi, (value - hi.astype(F32)).astype(BF16)


def split_np(value):
    hi = value.astype(jnp.bfloat16)
    lo = (value - hi.astype(np.float64)).astype(jnp.bfloat16)
    return hi, lo


def transforms(tap_count):
    omega = 2 * np.pi * (np.arange(FREQS) + 0.5) / POINTS
    angle = omega[:, None] * np.arange(POINTS)[None, :]
    forward = np.concatenate([np.cos(angle), -np.sin(angle)], axis=0)
    f_hi, f_lo = split_np(forward)
    back = np.concatenate([f_hi.T, f_lo.T, f_hi.T], axis=1)
    shift = omega[:, None] * (np.arange(32) - tap_count // 2)[None, :]
    tap_ok = (np.arange(32) < tap_count)[None, :]
    taps = np.concatenate([np.cos(shift), np.sin(shift)], axis=0) * tap_ok / FREQS
    t_hi, t_lo = split_np(taps)
    tap_fwd = np.concatenate([t_hi, t_lo], axis=1)
    lag = np.concatenate([np.cos(shift), -np.sin(shift)], axis=0) * tap_ok / FREQS
    l_hi, l_lo = split_np(lag.T)
    lags = np.concatenate([l_hi, l_lo, l_hi], axis=1)
    return f_hi, f_lo, back, tap_fwd, lags


def dot(a, b):
    return jnp.dot(a, b, preferred_element_type=F32)


def dot_t(a, b):
    return lax.dot_general(a, b, (((0,), (0,)), ((), ())), preferred_element_type=F32)


def pick_kernel(ours_ref, index_ref, rows_ref, proj_ref, taps_ref, gain_ref, packed_ref, *refs):
    out_refs, tail_ref = refs[:-1], refs[-1]
    depth, tap_count = proj_ref.shape[0], taps_ref.shape[0]
    packed_ref[:depth] = proj_ref[...]
    tail_ref[:tap_count] = taps_ref[...].astype(F32)
    tail_ref[tap_count:] = gain_ref[...].astype(F32)[None, :]
    packed_ref[depth:] = tail_ref[...].astype(BF16)
    count = rows_ref.shape[0]
    rows = rows_ref[...]
    if len(out_refs) == 1:
        index = index_ref[...]
        number = lax.broadcasted_iota(jnp.int32, (count, index.shape[1]), 0)
        choose = jnp.where(number == index, 1.0, 0.0).astype(BF16)
        out_refs[0][...] = dot_t(choose, rows).astype(BF16)
        return
    slot = index_ref.shape[1]
    number = lax.broadcasted_iota(jnp.int32, (count, slot), 0)
    for k, out_ref in enumerate(out_refs):
        index = index_ref[pl.ds(ours_ref[0, 0] ^ k, 1), :]
        choose = jnp.where(number == index, 1.0, 0.0).astype(BF16)
        out_ref[...] = dot_t(choose, rows).astype(BF16)


def runs(first, last, part):
    out = []
    row = first
    while row < last:
        stop = min(last, (row // part + 1) * part)
        out.append((row // part, row % part, row % part + stop - row, row - first))
        row = stop
    return out


def unpack_kernel(count, ours_ref, *refs):
    piece_refs, (proj_ref, taps_ref, gain_ref, held_ref) = refs[:count], refs[count:]
    parts, part, _ = held_ref.shape
    for k in range(parts):
        piece = piece_refs[k][...] if count == parts else piece_refs[0][k * part : (k + 1) * part]
        held_ref[k] = piece.astype(F32)
    depth, width = proj_ref.shape
    held = depth + 32
    for tile in range(width // 128):
        lanes = slice(tile * 128, tile * 128 + 128)
        for p, start, stop, offset in runs(tile * held, tile * held + depth, part):
            proj_ref[offset : offset + stop - start, lanes] = held_ref[p ^ ours_ref[0, 0], start:stop]
        last = [
            held_ref[p ^ ours_ref[0, 0], start:stop]
            for p, start, stop, _ in runs(tile * held + depth, tile * held + held, part)
        ]
        last = last[0] if len(last) == 1 else jnp.concatenate(last, axis=0)
        taps_ref[:, lanes] = last[: taps_ref.shape[0]]
        gain_ref[lanes] = last[taps_ref.shape[0] : taps_ref.shape[0] + 1].reshape(128)


def prep_kernel(pos_ref, hi_ref, lo_ref, back_ref, ahead_ref, behind_ref):
    f_hi = hi_ref[...]
    f_lo = lo_ref[...]
    back = back_ref[...]
    for part in range(6):
        sizes = (WIDE_K + BLOCK_K)[part]
        steps = (WIDE_STEPS + BLOCK_STEPS)[part]
        total = sum(sizes)
        place = pos_ref[part : part + 1, :total]
        number = lax.broadcasted_iota(jnp.int32, (POINTS, total), 0)
        hot = jnp.where(number == place, 1.0, 0.0).astype(BF16)
        lane = lax.broadcasted_iota(jnp.int32, (1, total), 1)
        middle = (lane >= sizes[0]) & (lane < sizes[0] + sizes[1])
        ahead = jnp.where(middle, dot(f_lo, hot), dot(f_hi, hot)).astype(BF16)
        ahead_ref[:, AHEAD_AT[part] : AHEAD_AT[part + 1]] = ahead
        held = steps[1] - steps[0]
        padded = -(-held // 128) * 128
        wide = dot_t(hot[:, :padded], back)
        behind_ref[BEHIND_AT[part] : BEHIND_AT[part + 1]] = wide[:held].astype(BF16)


def layer_kernel(count, core_ref, side_ref, ours_ref, *refs):
    arrived_refs = refs[:count]
    (
        take_ref, tapf_ref, lag_ref, params_hbm, up_hbm, ahead_hbm, behind_hbm,
        keep_ref, send_ref, loss_ref,
        params_ref, up_ref, ahead_ref, behind_ref, sems,
        frames_ref, frames_t_ref, x_ref, h_ref, stat_ref, acc_ref, acc2_ref,
        hi_ref, lo_ref, ghi_ref, glo_ref, spec_ref, nspec_ref, phi_ref, plo_ref,
        coef_ref, c_ref, small_ref, lossacc_ref,
    ) = refs[count:]
    copies = [
        pltpu.make_async_copy(source, target, sems.at[k])
        for k, (source, target) in enumerate(
            ((params_hbm, params_ref), (ahead_hbm, ahead_ref), (behind_hbm, behind_ref), (up_hbm, up_ref))
        )
    ]
    for copy in copies:
        copy.start()
    steps, width = up_ref.shape
    slots = sum(ref.shape[0] for ref in arrived_refs)
    pair_width = arrived_refs[0].shape[1]
    depth = pair_width // 2
    chunks = width // CH
    scale = (steps * width) ** -0.5
    tiles = [slice(r, r + ROWS) for r in range(0, steps, ROWS)]
    wide_of = [slice(AHEAD_AT[j], AHEAD_AT[j + 1]) for j in range(3)]
    block_of = [slice(AHEAD_AT[j], AHEAD_AT[j + 1]) for j in range(3, 6)]
    back_wide = [slice(BEHIND_AT[j], BEHIND_AT[j + 1]) for j in range(3)]
    back_block = [slice(BEHIND_AT[j], BEHIND_AT[j + 1]) for j in range(3, 6)]

    take = take_ref[...]
    number = lax.broadcasted_iota(jnp.int32, (slots, steps), 0)
    odd = lax.broadcasted_iota(jnp.int32, (slots, steps), 1) % 2
    here = number == take
    even_hot = jnp.where(here & (odd == 0), 1.0, 0.0).astype(BF16)
    odd_hot = jnp.where(here & (odd == 1), 1.0, 0.0).astype(BF16)
    first = jnp.concatenate([ref[:, :depth] for ref in arrived_refs], axis=0)
    second = jnp.concatenate([ref[:, depth:] for ref in arrived_refs], axis=0)
    frames = dot_t(even_hot, first) + dot_t(odd_hot, second)
    frames_ref[...] = frames.astype(BF16)
    frames_t_ref[...] = jnp.transpose(frames).astype(BF16)
    live = dot_t(even_hot + odd_hot, jnp.ones((slots, 128), BF16))
    stat_ref[2] = live * scale

    acc_ref[...] = jnp.zeros_like(acc_ref)
    copies[0].wait()

    def project(i, carry):
        cols = pl.ds(pl.multiple_of(i * CH, CH), CH)
        x = dot(frames_ref[...], params_ref[:depth, cols])
        x_ref[:, cols] = x
        acc_ref[...] += x[:, :128] + x[:, 128:]
        return carry

    lax.fori_loop(0, chunks, project, 0)
    mean = jnp.sum(acc_ref[...], axis=1, keepdims=True) * (1.0 / width)
    stat_ref[0] = jnp.broadcast_to(mean, (steps, 128))

    for rows in tiles:
        m = stat_ref[0, rows]
        total = jnp.zeros((ROWS, 128), F32)
        for k in range(width // 128):
            d = x_ref[rows, k * 128 : (k + 1) * 128] - m
            total = total + d * d
        var = jnp.sum(total, axis=1, keepdims=True) * (1.0 / width)
        stat_ref[1, rows] = jnp.broadcast_to(lax.rsqrt(var + 1e-05), (ROWS, 128))

    acc_ref[...] = jnp.zeros_like(acc_ref)
    acc2_ref[...] = jnp.zeros_like(acc2_ref)
    lossacc_ref[...] = jnp.zeros_like(lossacc_ref)

    for copy in copies[1:]:
        copy.wait()

    def twice(value):
        return jnp.concatenate([value, value], axis=1)

    def stack(hi, lo, slices):
        (a, b), (c, d), (e, f) = slices
        return jnp.concatenate([hi[a:b], hi[c:d], lo[e:f]], axis=0)

    def chunk(i, b):
        hi_b, lo_b, ghi_b, glo_b = hi_ref.at[b], lo_ref.at[b], ghi_ref.at[b], glo_ref.at[b]
        spec_b, nspec_b, phi_b, plo_b = spec_ref.at[b], nspec_ref.at[b], phi_ref.at[b], plo_ref.at[b]
        coef_b, c_b = coef_ref.at[b], c_ref.at[b]
        cols = slice(i * CH, (i + 1) * CH)
        gain = params_ref[depth + 16 : depth + 32, cols][15:16].astype(F32)
        taps = params_ref[depth : depth + 32, cols]
        coef_b[...] = dot(tapf_ref[...], jnp.concatenate([taps, taps], axis=0))
        for t, rows in enumerate(tiles):
            xhat = (x_ref[rows, cols] - twice(stat_ref[0, rows])) * twice(stat_ref[1, rows])
            hi, lo = split(xhat * gain)
            hi_b[rows] = hi
            lo_b[rows] = lo
            if t in (2, 5):
                yield
        yield
        for j in range(3):
            nspec_b[j] = dot(ahead_ref[:, block_of[j]], stack(hi_b, lo_b, k_slices(BLOCK_STEPS[j], BLOCK_K[j])))
            yield
        for j in range(3):
            for f in range(0, FREQS, 32):
                lower, upper = slice(f, f + 32), slice(FREQS + f, FREQS + f + 32)
                re, im = nspec_b[j, lower], nspec_b[j, upper]
                cre, cim = coef_b[lower], coef_b[upper]
                hi, lo = split(re * cre - im * cim)
                phi_b[j, lower] = hi
                plo_b[j, lower] = lo
                hi, lo = split(re * cim + im * cre)
                phi_b[j, upper] = hi
                plo_b[j, upper] = lo
            yield
        parts = []
        for j in range(3):
            held_j = jnp.concatenate([phi_b[j], phi_b[j], plo_b[j]], axis=0)
            parts.append(dot(behind_ref[back_wide[j]], held_j))
            if j == 1:
                c_b[0:112] = parts[0][0:112]
                c_b[112:224] = parts[0][112:224] + parts[1][0:112]
                c_b[224:288] = parts[1][112:176]
            if j == 2:
                c_b[288:400] = parts[1][176:288] + parts[2][0:112]
                c_b[400:512] = parts[2][112:224]
            yield
        loss = jnp.zeros((1, CH), F32)
        for t, rows in enumerate(tiles):
            conv = c_b[rows]
            sig = jax.nn.sigmoid(conv)
            go = up_ref[rows, cols].astype(F32) * twice(stat_ref[2, rows])
            out = x_ref[rows, cols] + conv * sig
            loss = loss + jnp.sum(out * go, axis=0, keepdims=True)
            hi, lo = split(go * (sig * (1.0 + conv * (1.0 - sig))))
            ghi_b[rows] = hi
            glo_b[rows] = lo
            if t in (2, 5):
                yield
        lossacc_ref[...] += loss
        yield
        for j in range(3):
            spec_b[j] = dot(ahead_ref[:, wide_of[j]], stack(ghi_b, glo_b, k_slices(WIDE_STEPS[j], WIDE_K[j])))
            yield
        for f in range(0, FREQS, 32):
            lower, upper = slice(f, f + 32), slice(FREQS + f, FREQS + f + 32)
            cre, cim = coef_b[lower], coef_b[upper]
            zre = jnp.zeros((32, CH), F32)
            zim = jnp.zeros((32, CH), F32)
            for j in range(3):
                nre, nim = nspec_b[j, lower], nspec_b[j, upper]
                re, im = spec_b[j, lower], spec_b[j, upper]
                zre = zre + (nre * re + nim * im)
                zim = zim + (nim * re - nre * im)
                hi, lo = split(re * cre + im * cim)
                phi_b[j, lower] = hi
                plo_b[j, lower] = lo
                hi, lo = split(im * cre - re * cim)
                phi_b[j, upper] = hi
                plo_b[j, upper] = lo
            hi, lo = split(zre)
            phi_b[3, lower] = hi
            plo_b[3, lower] = lo
            hi, lo = split(zim)
            phi_b[3, upper] = hi
            plo_b[3, upper] = lo
            if f != 32:
                yield
        parts = []
        for j in range(3):
            held_j = jnp.concatenate([phi_b[j], phi_b[j], plo_b[j]], axis=0)
            parts.append(dot(behind_ref[back_block[j]], held_j))
            if j == 1:
                c_b[0:128] = parts[0][0:128]
                c_b[128:208] = parts[0][128:208] + parts[1][0:80]
                c_b[208:304] = parts[1][80:176]
            if j == 2:
                c_b[304:384] = parts[1][176:256] + parts[2][0:80]
                c_b[384:512] = parts[2][80:208]
            yield
        tap_grad = dot(lag_ref[...], jnp.concatenate([phi_b[3], phi_b[3], plo_b[3]], axis=0))
        gain_grad = jnp.zeros((1, CH), F32)
        for t, rows in enumerate(tiles):
            gn = c_b[rows]
            xhat = (x_ref[rows, cols] - twice(stat_ref[0, rows])) * twice(stat_ref[1, rows])
            gain_grad = gain_grad + jnp.sum(gn * xhat, axis=0, keepdims=True)
            h = gn * gain
            hx = h * xhat
            h_ref[rows, cols] = h
            acc_ref[rows] += h[:, :128] + h[:, 128:]
            acc2_ref[rows] += hx[:, :128] + hx[:, 128:]
            if t in (2, 5):
                yield
        last = lax.broadcasted_iota(jnp.int32, (32, CH), 0) == 31
        small_ref[:, cols] = jnp.where(last, gain_grad, tap_grad)
        for _ in range(4):
            yield

    waiting = [chunk(i, i % 2) for i in range(chunks)]
    running = [waiting.pop(0)]
    for _ in range(15):
        next(running[0])
    while running:
        if waiting and len(running) < 2:
            running.append(waiting.pop(0))
        running = [g for g in running if next(g, waiting) is not waiting]

    loss_ref[...] = jnp.sum(lossacc_ref[...], axis=1, keepdims=True)
    for rows in tiles:
        m1 = jnp.sum(acc_ref[rows], axis=1, keepdims=True) * (1.0 / width)
        m2 = jnp.sum(acc2_ref[rows], axis=1, keepdims=True) * (1.0 / width)
        acc_ref[rows] = jnp.broadcast_to(m1, (ROWS, 128))
        acc2_ref[rows] = jnp.broadcast_to(m2, (ROWS, 128))

    halves, parts, part, _ = keep_ref.shape
    per_block = width // (2 * halves) // 128
    held = depth + 32

    def grad_rows(i):
        cols = slice(i * CH, (i + 1) * CH)
        for rows in tiles:
            inv = twice(stat_ref[1, rows])
            xhat = (x_ref[rows, cols] - twice(stat_ref[0, rows])) * inv
            go = up_ref[rows, cols].astype(F32) * twice(stat_ref[2, rows])
            inner = h_ref[rows, cols] - twice(acc_ref[rows]) - xhat * twice(acc2_ref[rows])
            hi_ref[i % 2, rows] = (go + inv * inner).astype(BF16)

    def finish(core):
        grad_rows(0)
        for i in range(chunks):
            if i + 1 < chunks:
                grad_rows(i + 1)
            weight = dot(frames_t_ref[...], hi_ref[i % 2])
            for half in range(CH // 128):
                tile = i * (CH // 128) + half
                block, inside = tile // per_block, (tile % per_block) * held
                lanes = slice(half * 128, half * 128 + 128)
                small = small_ref[:, tile * 128 : (tile + 1) * 128]
                target = keep_ref if block % 2 == core else send_ref
                side = (block // 2) ^ side_ref[0, 0]
                for p, start, stop, offset in runs(inside, inside + depth, part):
                    value = weight[offset : offset + stop - start, lanes]
                    target[side, p ^ ours_ref[0, 0], start:stop] = value
                for p, start, stop, offset in runs(inside + depth, inside + held, part):
                    value = small[offset : offset + stop - start]
                    target[side, p ^ ours_ref[0, 0], start:stop] = value

    pl.when(core_ref[0, 0] == 0)(lambda: finish(0))
    pl.when(core_ref[0, 0] != 0)(lambda: finish(1))
    for p, start, stop, _ in runs(per_block * held, parts * part, part):
        for side in range(halves):
            for ref in (keep_ref, send_ref):
                ref[side, p ^ ours_ref[0, 0], start:stop] = jnp.zeros((stop - start, 128), F32)


def vmem(count):
    return [pl.BlockSpec(memory_space=pltpu.VMEM)] * count


SCALARS = pl.BlockSpec(memory_space=pltpu.SMEM)


def pick(ours, index, rows, proj, taps, gain):
    dp, slot = index.shape
    width = rows.shape[1]
    if dp > FEW:
        index = index.reshape(1, -1)
        shapes = [jax.ShapeDtypeStruct((dp * slot, width), BF16)]
    else:
        shapes = [jax.ShapeDtypeStruct((slot, width), BF16)] * dp
    return pl.pallas_call(
        pick_kernel,
        out_shape=[jax.ShapeDtypeStruct((proj.shape[0] + 32, proj.shape[1]), BF16)] + shapes,
        in_specs=[SCALARS] + vmem(5),
        out_specs=vmem(1 + len(shapes)),
        scratch_shapes=[pltpu.VMEM((32, proj.shape[1]), F32)],
        compiler_params=pltpu.CompilerParams(vmem_limit_bytes=VMEM_LIMIT),
        cost_estimate=pl.CostEstimate(
            flops=2 * dp * slot * rows.size, bytes_accessed=6 * rows.size, transcendentals=0
        ),
        name="pick_rows",
    )(ours, index, rows, proj, taps, gain)


def unpack(ours, pieces, parts, part, depth, tap_count, width):
    return pl.pallas_call(
        functools.partial(unpack_kernel, len(pieces)),
        out_shape=[
            jax.ShapeDtypeStruct((depth, width), F32),
            jax.ShapeDtypeStruct((tap_count, width), F32),
            jax.ShapeDtypeStruct((width,), F32),
        ],
        in_specs=[SCALARS] + vmem(len(pieces)),
        out_specs=vmem(3),
        scratch_shapes=[pltpu.VMEM((parts, part, 128), F32)],
        compiler_params=pltpu.CompilerParams(vmem_limit_bytes=VMEM_LIMIT),
        cost_estimate=pl.CostEstimate(flops=10**6, bytes_accessed=12 * 10**5, transcendentals=0),
        name="unpack_gradients",
    )(ours, *pieces)


def positions(utterances):
    steps = utterances.shape[0]
    place = jnp.arange(steps, dtype=jnp.int32) + GAP * utterances
    most = max(sum(sizes) for sizes in WIDE_K + BLOCK_K)
    lines = []
    for kind, (ranges, sizes_of) in enumerate(((WIDE_STEPS, WIDE_K), (BLOCK_STEPS, BLOCK_K))):
        for j in range(3):
            local = place - (STARTS[j] - GAP)
            low, high = (0, LENGTHS[j] + 2 * GAP) if kind == 0 else (GAP, LENGTHS[j] + GAP)
            local = jnp.where((local >= low) & (local < high), local, -1)
            inside = jnp.arange(steps)
            local = jnp.where((inside >= ranges[j][0]) & (inside < ranges[j][1]), local, -1)
            pieces = [local[a:b] for a, b in k_slices(ranges[j], sizes_of[j])]
            line = jnp.concatenate(pieces)
            lines.append(jnp.pad(line, (0, most - line.shape[0]), constant_values=-1))
    lines.extend([jnp.full((most,), -1, jnp.int32)] * 2)
    return jnp.stack(lines)


def prepare(utterances, f_hi, f_lo, back):
    shapes = [
        jax.ShapeDtypeStruct((POINTS, AHEAD_AT[-1]), BF16),
        jax.ShapeDtypeStruct((BEHIND_AT[-1], 3 * POINTS), BF16),
    ]
    return pl.pallas_call(
        prep_kernel,
        out_shape=shapes,
        in_specs=vmem(4),
        out_specs=vmem(2),
        compiler_params=pltpu.CompilerParams(vmem_limit_bytes=VMEM_LIMIT),
        cost_estimate=pl.CostEstimate(flops=3 * 10**9, bytes_accessed=8 * 10**6, transcendentals=0),
        name="prepare_transforms",
    )(positions(utterances), f_hi, f_lo, back)


def layer(
    ids, arrived, take, params, upstream, tap_fwd, lags, ahead, behind, parts, part, halves
):
    steps, width = upstream.shape
    depth = arrived[0].shape[1] // 2
    hbm = pl.BlockSpec(memory_space=pltpu.HBM)
    scratch = [
        pltpu.VMEM(params.shape, BF16),
        pltpu.VMEM(upstream.shape, BF16),
        pltpu.VMEM(ahead.shape, BF16),
        pltpu.VMEM(behind.shape, BF16),
        pltpu.SemaphoreType.DMA((4,)),
        pltpu.VMEM((steps, depth), BF16),
        pltpu.VMEM((depth, steps), BF16),
        pltpu.VMEM((steps, width), F32),
        pltpu.VMEM((steps, width), F32),
        pltpu.VMEM((3, steps, 128), F32),
        pltpu.VMEM((steps, 128), F32),
        pltpu.VMEM((steps, 128), F32),
        pltpu.VMEM((2, steps, CH), BF16),
        pltpu.VMEM((2, steps, CH), BF16),
        pltpu.VMEM((2, steps, CH), BF16),
        pltpu.VMEM((2, steps, CH), BF16),
        pltpu.VMEM((2, 3, POINTS, CH), F32),
        pltpu.VMEM((2, 3, POINTS, CH), F32),
        pltpu.VMEM((2, 4, POINTS, CH), BF16),
        pltpu.VMEM((2, 4, POINTS, CH), BF16),
        pltpu.VMEM((2, POINTS, CH), F32),
        pltpu.VMEM((2, steps, CH), F32),
        pltpu.VMEM((32, width), F32),
        pltpu.VMEM((1, CH), F32),
    ]
    return pl.pallas_call(
        functools.partial(layer_kernel, len(arrived)),
        out_shape=[
            jax.ShapeDtypeStruct((halves, parts, part, 128), F32),
            jax.ShapeDtypeStruct((halves, parts, part, 128), F32),
            jax.ShapeDtypeStruct((1, 1), F32),
        ],
        in_specs=[SCALARS] * 3 + vmem(len(arrived) + 3) + [hbm] * 4,
        out_specs=vmem(3),
        scratch_shapes=scratch,
        compiler_params=pltpu.CompilerParams(vmem_limit_bytes=VMEM_LIMIT),
        cost_estimate=pl.CostEstimate(flops=10**10, bytes_accessed=16 * 10**6, transcendentals=10**6),
        name="layer_step",
    )(*ids, *arrived, take, tap_fwd, lags, params, upstream, ahead, behind)


def per_device(
    dp, fsdp, cached, send_rows, take_rows, utt_index, upstream, in_proj, norm_gain, conv_kernel
):
    tap_count = conv_kernel.shape[0]
    f_hi, f_lo, back, tap_fwd, lags = [jnp.asarray(m) for m in transforms(tap_count)]
    few = dp <= FEW
    place = lax.axis_index("fsdp")
    ours = lax.axis_index("dp") if few else jnp.zeros((), jnp.int32)
    ids = [v.astype(jnp.int32).reshape(1, 1) for v in (place % 2, place // 2, ours)]
    wanted = send_rows[0, 0]
    packed, *outgoing = pick(ids[2], wanted, cached[0, 0], in_proj, conv_kernel, norm_gain)
    params = lax.all_gather(packed, "fsdp", axis=1, tiled=True)
    outgoing, take_own, utt_own = lax.optimization_barrier(
        (outgoing, take_rows[0, 0], utt_index[0, 0])
    )

    def swap(value, k):
        return lax.ppermute(value, "dp", [(i, i ^ k) for i in range(dp)])

    far_first = [k for k in range(dp // 2, dp)] + [k for k in range(dp // 2 - 1, 0, -1)]
    if few:
        got = {k: swap(outgoing[k], k) for k in far_first}
        arrived = [outgoing[0]] + [got[k] for k in range(1, dp)]
        take_own = jnp.where(take_own >= 0, take_own ^ (ours * wanted.shape[1]), -1)
    else:
        sent = outgoing[0].reshape(wanted.shape + outgoing[0].shape[1:])
        back_in = lax.all_to_all(sent, "dp", split_axis=0, concat_axis=0, tiled=True)
        arrived = [back_in.reshape(-1, back_in.shape[2])]
    take = jnp.repeat(take_own, 2)[None, :]
    ahead, behind = prepare(jnp.repeat(utt_own, 2), f_hi, f_lo, back)

    depth, shard_cols = in_proj.shape
    held = depth + 32
    tiles = shard_cols // 128
    part = -(-(held * tiles) // dp)
    part = -(-part // 16) * 16
    halves = fsdp // 2
    keep, send, loss = layer(
        ids, arrived, take, params, upstream[0, 0], tap_fwd, lags, ahead, behind,
        dp, part, halves,
    )
    other = lax.ppermute(send, "fsdp", [(i, i ^ 1) for i in range(fsdp)])
    half = dp // 2
    across = [(i, i ^ 2) for i in range(fsdp)]
    spans = ((half, dp), (0, half))
    sent = [(keep[1, low:high] + other[1, low:high]).astype(BF16) for low, high in spans]
    far_in, near_in = [lax.ppermute(v, "fsdp", across) for v in sent]
    far_sum = keep[0, half:] + other[0, half:] + far_in.astype(F32)
    far_out = far_sum.astype(BF16)
    near_in, _ = lax.optimization_barrier((near_in, far_out))
    near_sum = keep[0, :half] + other[0, :half] + near_in.astype(F32)
    near_out = near_sum.astype(BF16)
    if few:
        got = {}
        for k in far_first:
            got[k] = swap(far_out[k - half] if k >= half else near_out[k], k)
        total = near_sum[0]
        for k in range(1, dp):
            total = total + got[k].astype(F32)
        piece = total.astype(BF16)
        far = {k: swap(piece, k) for k in range(dp - 2, 0, -2)}
        pieces = {0: piece, 1: swap(piece, 1), **far}
        for k in far:
            pieces[k + 1] = swap(far[k], 1)
        pieces = [pieces[k] for k in range(dp)]
    else:
        chip = jnp.concatenate([near_out, far_out], axis=0)
        shared = lax.all_to_all(chip, "dp", split_axis=0, concat_axis=0, tiled=True)
        piece = jnp.sum(shared.astype(F32), axis=0).astype(BF16)
        pieces = [lax.all_gather(piece, "dp", axis=0, tiled=True)]
    proj, taps, gain = unpack(ids[2], pieces, dp, part, depth, tap_count, shard_cols)
    return (proj, taps, gain, loss)


def solution(mesh):
    placed = (
        P("dp", "fsdp", None, None),
        P("dp", "fsdp", None, None),
        P("dp", "fsdp", None),
        P("dp", "fsdp", None),
        P("dp", "fsdp", None, None),
        P(None, "fsdp"),
        P("fsdp"),
        P(None, "fsdp"),
    )
    return jax.shard_map(
        functools.partial(per_device, mesh.shape["dp"], mesh.shape["fsdp"]),
        mesh=mesh,
        in_specs=placed,
        out_specs=(P(None, "fsdp"), P(None, "fsdp"), P("fsdp"), P("dp", "fsdp")),
        check_vma=False,
    )
```

```python
import functools
import math

import jax
import jax.numpy as jnp
import numpy as np
from jax import lax
from jax.experimental import pallas as pl
from jax.experimental.pallas import tpu as pltpu
from jax.sharding import PartitionSpec as P

GAP = 16
POINTS = 256
FREQS = 128
STARTS = (0, 224, 432)
LENGTHS = (224, 208, 224)
BLOCK_STEPS = ((0, 208), (128, 384), (304, 512))
WIDE_STEPS = ((0, 224), (112, 400), (288, 512))
BLOCK_K = ((208, 208, 224), (256, 256, 256), (208, 208, 224))
WIDE_K = ((224, 224, 320), (288, 288, 320), (224, 224, 320))
AHEAD_AT = tuple(int(v) for v in np.cumsum([0] + [sum(k) for k in WIDE_K + BLOCK_K]))
BEHIND_AT = tuple(int(v) for v in np.cumsum([0] + [b - a for a, b in WIDE_STEPS + BLOCK_STEPS]))
CH = 256
ROWS = 64
F32 = jnp.float32
BF16 = jnp.bfloat16
VMEM_LIMIT = 60 * 1024 * 1024
FEW = 16


def k_slices(steps, sizes):
    out = []
    for size in sizes:
        first = steps[0] if steps[0] + size <= 512 else 512 - size
        out.append((first, first + size))
    return out


def split(value):
    hi = value.astype(BF16)
    return hi, (value - hi.astype(F32)).astype(BF16)


def split_np(value):
    hi = value.astype(jnp.bfloat16)
    lo = (value - hi.astype(np.float64)).astype(jnp.bfloat16)
    return hi, lo


def transforms(tap_count):
    omega = 2 * np.pi * (np.arange(FREQS) + 0.5) / POINTS
    angle = omega[:, None] * np.arange(POINTS)[None, :]
    forward = np.concatenate([np.cos(angle), -np.sin(angle)], axis=0)
    f_hi, f_lo = split_np(forward)
    back = np.concatenate([f_hi.T, f_lo.T, f_hi.T], axis=1)
    shift = omega[:, None] * (np.arange(32) - tap_count // 2)[None, :]
    tap_ok = (np.arange(32) < tap_count)[None, :]
    taps = np.concatenate([np.cos(shift), np.sin(shift)], axis=0) * tap_ok / FREQS
    t_hi, t_lo = split_np(taps)
    tap_fwd = np.concatenate([t_hi, t_lo], axis=1)
    lag = np.concatenate([np.cos(shift), -np.sin(shift)], axis=0) * tap_ok / FREQS
    l_hi, l_lo = split_np(lag.T)
    lags = np.concatenate([l_hi, l_lo, l_hi], axis=1)
    return f_hi, f_lo, back, tap_fwd, lags


def dot(a, b):
    return jnp.dot(a, b, preferred_element_type=F32)


def dot_t(a, b):
    return lax.dot_general(a, b, (((0,), (0,)), ((), ())), preferred_element_type=F32)


def pick_kernel(ours_ref, index_ref, rows_ref, proj_ref, taps_ref, gain_ref, packed_ref, *refs):
    out_refs, tail_ref = refs[:-1], refs[-1]
    depth, tap_count = proj_ref.shape[0], taps_ref.shape[0]
    packed_ref[:depth] = proj_ref[...]
    tail_ref[:tap_count] = taps_ref[...].astype(F32)
    tail_ref[tap_count:] = gain_ref[...].astype(F32)[None, :]
    packed_ref[depth:] = tail_ref[...].astype(BF16)
    count = rows_ref.shape[0]
    rows = rows_ref[...]
    if len(out_refs) == 1:
        index = index_ref[...]
        number = lax.broadcasted_iota(jnp.int32, (count, index.shape[1]), 0)
        choose = jnp.where(number == index, 1.0, 0.0).astype(BF16)
        out_refs[0][...] = dot_t(choose, rows).astype(BF16)
        return
    slot = index_ref.shape[1]
    number = lax.broadcasted_iota(jnp.int32, (count, slot), 0)
    for k, out_ref in enumerate(out_refs):
        index = index_ref[pl.ds(ours_ref[0, 0] ^ k, 1), :]
        choose = jnp.where(number == index, 1.0, 0.0).astype(BF16)
        out_ref[...] = dot_t(choose, rows).astype(BF16)


def runs(first, last, part):
    out = []
    row = first
    while row < last:
        stop = min(last, (row // part + 1) * part)
        out.append((row // part, row % part, row % part + stop - row, row - first))
        row = stop
    return out


def unpack_kernel(count, ours_ref, *refs):
    piece_refs, (proj_ref, taps_ref, gain_ref, held_ref) = refs[:count], refs[count:]
    parts, part, _ = held_ref.shape
    for k in range(parts):
        piece = piece_refs[k][...] if count == parts else piece_refs[0][k * part : (k + 1) * part]
        held_ref[k] = piece.astype(F32)
    depth, width = proj_ref.shape
    held = depth + 32
    for tile in range(width // 128):
        lanes = slice(tile * 128, tile * 128 + 128)
        for p, start, stop, offset in runs(tile * held, tile * held + depth, part):
            proj_ref[offset : offset + stop - start, lanes] = held_ref[p ^ ours_ref[0, 0], start:stop]
        last = [
            held_ref[p ^ ours_ref[0, 0], start:stop]
            for p, start, stop, _ in runs(tile * held + depth, tile * held + held, part)
        ]
        last = last[0] if len(last) == 1 else jnp.concatenate(last, axis=0)
        taps_ref[:, lanes] = last[: taps_ref.shape[0]]
        gain_ref[lanes] = last[taps_ref.shape[0] : taps_ref.shape[0] + 1].reshape(128)


def prep_kernel(pos_ref, hi_ref, lo_ref, back_ref, ahead_ref, behind_ref):
    f_hi = hi_ref[...]
    f_lo = lo_ref[...]
    back = back_ref[...]
    for part in range(6):
        sizes = (WIDE_K + BLOCK_K)[part]
        steps = (WIDE_STEPS + BLOCK_STEPS)[part]
        total = sum(sizes)
        place = pos_ref[part : part + 1, :total]
        number = lax.broadcasted_iota(jnp.int32, (POINTS, total), 0)
        hot = jnp.where(number == place, 1.0, 0.0).astype(BF16)
        lane = lax.broadcasted_iota(jnp.int32, (1, total), 1)
        middle = (lane >= sizes[0]) & (lane < sizes[0] + sizes[1])
        ahead = jnp.where(middle, dot(f_lo, hot), dot(f_hi, hot)).astype(BF16)
        ahead_ref[:, AHEAD_AT[part] : AHEAD_AT[part + 1]] = ahead
        held = steps[1] - steps[0]
        padded = -(-held // 128) * 128
        wide = dot_t(hot[:, :padded], back)
        behind_ref[BEHIND_AT[part] : BEHIND_AT[part + 1]] = wide[:held].astype(BF16)


def layer_kernel(count, core_ref, side_ref, ours_ref, *refs):
    arrived_refs = refs[:count]
    (
        take_ref, tapf_ref, lag_ref, params_hbm, up_hbm, ahead_hbm, behind_hbm,
        keep_ref, send_ref, loss_ref,
        params_ref, up_ref, ahead_ref, behind_ref, sems,
        frames_ref, frames_t_ref, x_ref, h_ref, stat_ref, acc_ref, acc2_ref,
        hi_ref, lo_ref, ghi_ref, glo_ref, spec_ref, nspec_ref, phi_ref, plo_ref,
        coef_ref, c_ref, small_ref, lossacc_ref,
    ) = refs[count:]
    copies = [
        pltpu.make_async_copy(source, target, sems.at[k])
        for k, (source, target) in enumerate(
            ((params_hbm, params_ref), (ahead_hbm, ahead_ref), (behind_hbm, behind_ref), (up_hbm, up_ref))
        )
    ]
    for copy in copies:
        copy.start()
    steps, width = up_ref.shape
    slots = sum(ref.shape[0] for ref in arrived_refs)
    pair_width = arrived_refs[0].shape[1]
    depth = pair_width // 2
    chunks = width // CH
    scale = (steps * width) ** -0.5
    tiles = [slice(r, r + ROWS) for r in range(0, steps, ROWS)]
    wide_of = [slice(AHEAD_AT[j], AHEAD_AT[j + 1]) for j in range(3)]
    block_of = [slice(AHEAD_AT[j], AHEAD_AT[j + 1]) for j in range(3, 6)]
    back_wide = [slice(BEHIND_AT[j], BEHIND_AT[j + 1]) for j in range(3)]
    back_block = [slice(BEHIND_AT[j], BEHIND_AT[j + 1]) for j in range(3, 6)]

    first = jnp.concatenate([ref[:, :depth] for ref in arrived_refs], axis=0)
    second = jnp.concatenate([ref[:, depth:] for ref in arrived_refs], axis=0)
    for rows in [slice(r, r + 128) for r in range(0, steps, 128)]:
        take = take_ref[rows]
        odd = lax.broadcasted_iota(jnp.int32, (128, 128), 0) % 2
        lane = lax.broadcasted_iota(jnp.int32, (128, 128), 1)
        even_take = jnp.where(odd == 0, take, -1)
        odd_take = jnp.where(odd == 1, take, -1)
        even_hot, odd_hot = [
            jnp.concatenate(
                [jnp.where(lane + at == t, 1.0, 0.0).astype(BF16) for at in range(0, slots, 128)], axis=1
            )
            for t in (even_take, odd_take)
        ]
        frames_ref[rows] = (dot(even_hot, first) + dot(odd_hot, second)).astype(BF16)
        stat_ref[2, rows] = jnp.where(take >= 0, scale, 0.0)

    copies[0].wait()
    acc = jnp.zeros((steps, 128), F32)
    for i in range(chunks):
        cols = slice(i * CH, (i + 1) * CH)
        x = dot(frames_ref[...], params_ref[:depth, cols])
        x_ref[:, cols] = x
        acc = acc + x[:, :128] + x[:, 128:]
        if i < steps // 128:
            part_t = jnp.transpose(frames_ref[i * 128 : i * 128 + 128].astype(F32))
            frames_t_ref[:, i * 128 : i * 128 + 128] = part_t.astype(BF16)
    acc_ref[...] = acc
    mean = jnp.sum(acc_ref[...], axis=1, keepdims=True) * (1.0 / width)
    stat_ref[0] = jnp.broadcast_to(mean, (steps, 128))

    for rows in tiles:
        m = stat_ref[0, rows]
        total = jnp.zeros((ROWS, 128), F32)
        for k in range(width // 128):
            d = x_ref[rows, k * 128 : (k + 1) * 128] - m
            total = total + d * d
        var = jnp.sum(total, axis=1, keepdims=True) * (1.0 / width)
        stat_ref[1, rows] = jnp.broadcast_to(lax.rsqrt(var + 1e-05), (ROWS, 128))

    acc_ref[...] = jnp.zeros_like(acc_ref)
    acc2_ref[...] = jnp.zeros_like(acc2_ref)
    lossacc_ref[...] = jnp.zeros_like(lossacc_ref)

    for copy in copies[1:]:
        copy.wait()

    def twice(value):
        return jnp.concatenate([value, value], axis=1)

    def stack(hi, lo, slices):
        (a, b), (c, d), (e, f) = slices
        return jnp.concatenate([hi[a:b], hi[c:d], lo[e:f]], axis=0)

    def chunk(i, b):
        hi_b, lo_b, ghi_b, glo_b = hi_ref.at[b], lo_ref.at[b], ghi_ref.at[b], glo_ref.at[b]
        spec_b, nspec_b, phi_b, plo_b = spec_ref.at[b], nspec_ref.at[b], phi_ref.at[b], plo_ref.at[b]
        coef_b, c_b = coef_ref.at[b], c_ref.at[b]
        cols = pl.ds(pl.multiple_of(i * CH, CH), CH)
        gain = params_ref[depth + 16 : depth + 32, cols][15:16].astype(F32)
        taps = params_ref[depth : depth + 32, cols]
        coef_b[...] = dot(tapf_ref[...], jnp.concatenate([taps, taps], axis=0))
        for t, rows in enumerate(tiles):
            xhat = (x_ref[rows, cols] - twice(stat_ref[0, rows])) * twice(stat_ref[1, rows])
            hi, lo = split(xhat * gain)
            hi_b[rows] = hi
            lo_b[rows] = lo
            if t in (2, 5):
                yield
        yield
        for j in range(3):
            nspec_b[j] = dot(ahead_ref[:, block_of[j]], stack(hi_b, lo_b, k_slices(BLOCK_STEPS[j], BLOCK_K[j])))
            yield
        for j in range(3):
            for f in range(0, FREQS, 32):
                lower, upper = slice(f, f + 32), slice(FREQS + f, FREQS + f + 32)
                re, im = nspec_b[j, lower], nspec_b[j, upper]
                cre, cim = coef_b[lower], coef_b[upper]
                hi, lo = split(re * cre - im * cim)
                phi_b[j, lower] = hi
                plo_b[j, lower] = lo
                hi, lo = split(re * cim + im * cre)
                phi_b[j, upper] = hi
                plo_b[j, upper] = lo
            yield
        parts = []
        for j in range(3):
            held_j = jnp.concatenate([phi_b[j], phi_b[j], plo_b[j]], axis=0)
            parts.append(dot(behind_ref[back_wide[j]], held_j))
            if j == 1:
                c_b[0:112] = parts[0][0:112]
                c_b[112:224] = parts[0][112:224] + parts[1][0:112]
                c_b[224:288] = parts[1][112:176]
            if j == 2:
                c_b[288:400] = parts[1][176:288] + parts[2][0:112]
                c_b[400:512] = parts[2][112:224]
            yield
        loss = jnp.zeros((1, CH), F32)
        for t, rows in enumerate(tiles):
            conv = c_b[rows]
            sig = 0.5 + 0.5 * jnp.tanh(0.5 * conv)
            go = up_ref[rows, cols].astype(F32) * twice(stat_ref[2, rows])
            out = x_ref[rows, cols] + conv * sig
            loss = loss + jnp.sum(out * go, axis=0, keepdims=True)
            hi, lo = split(go * (sig * (1.0 + conv * (1.0 - sig))))
            ghi_b[rows] = hi
            glo_b[rows] = lo
            if t in (2, 5):
                yield
        lossacc_ref[...] += loss
        yield
        for j in range(3):
            spec_b[j] = dot(ahead_ref[:, wide_of[j]], stack(ghi_b, glo_b, k_slices(WIDE_STEPS[j], WIDE_K[j])))
            yield
        for f in range(0, FREQS, 32):
            lower, upper = slice(f, f + 32), slice(FREQS + f, FREQS + f + 32)
            cre, cim = coef_b[lower], coef_b[upper]
            zre = jnp.zeros((32, CH), F32)
            zim = jnp.zeros((32, CH), F32)
            for j in range(3):
                nre, nim = nspec_b[j, lower], nspec_b[j, upper]
                re, im = spec_b[j, lower], spec_b[j, upper]
                zre = zre + (nre * re + nim * im)
                zim = zim + (nim * re - nre * im)
                hi, lo = split(re * cre + im * cim)
                phi_b[j, lower] = hi
                plo_b[j, lower] = lo
                hi, lo = split(im * cre - re * cim)
                phi_b[j, upper] = hi
                plo_b[j, upper] = lo
            hi, lo = split(zre)
            phi_b[3, lower] = hi
            plo_b[3, lower] = lo
            hi, lo = split(zim)
            phi_b[3, upper] = hi
            plo_b[3, upper] = lo
            if f != 32:
                yield
        parts = []
        for j in range(3):
            held_j = jnp.concatenate([phi_b[j], phi_b[j], plo_b[j]], axis=0)
            parts.append(dot(behind_ref[back_block[j]], held_j))
            if j == 1:
                c_b[0:128] = parts[0][0:128]
                c_b[128:208] = parts[0][128:208] + parts[1][0:80]
                c_b[208:304] = parts[1][80:176]
            if j == 2:
                c_b[304:384] = parts[1][176:256] + parts[2][0:80]
                c_b[384:512] = parts[2][80:208]
            yield
        tap_grad = dot(lag_ref[...], jnp.concatenate([phi_b[3], phi_b[3], plo_b[3]], axis=0))
        gain_grad = jnp.zeros((1, CH), F32)
        for t, rows in enumerate(tiles):
            gn = c_b[rows]
            xhat = (x_ref[rows, cols] - twice(stat_ref[0, rows])) * twice(stat_ref[1, rows])
            gain_grad = gain_grad + jnp.sum(gn * xhat, axis=0, keepdims=True)
            h = gn * gain
            hx = h * xhat
            h_ref[rows, cols] = h
            acc_ref[rows] += h[:, :128] + h[:, 128:]
            acc2_ref[rows] += hx[:, :128] + hx[:, 128:]
            if t in (2, 5):
                yield
        last = lax.broadcasted_iota(jnp.int32, (32, CH), 0) == 31
        small_ref[:, cols] = jnp.where(last, gain_grad, tap_grad)

    def middle(i, carry):
        lead, follow = chunk(2 * i, 0), chunk(2 * i + 1, 1)
        for _ in range(3):
            next(lead)
        running = [lead, follow]
        while running:
            running = [g for g in running if next(g, running) is not running]
        return carry

    lax.fori_loop(0, chunks // 2, middle, 0)
    loss_ref[...] = jnp.sum(lossacc_ref[...], axis=1, keepdims=True)
    for rows in tiles:
        m1 = jnp.sum(acc_ref[rows], axis=1, keepdims=True) * (1.0 / width)
        m2 = jnp.sum(acc2_ref[rows], axis=1, keepdims=True) * (1.0 / width)
        acc_ref[rows] = jnp.broadcast_to(m1, (ROWS, 128))
        acc2_ref[rows] = jnp.broadcast_to(m2, (ROWS, 128))

    halves, parts, part, _ = keep_ref.shape
    per_block = width // (2 * halves) // 128
    held = depth + 32

    def grad_rows(i):
        cols = slice(i * CH, (i + 1) * CH)
        for rows in tiles:
            inv = twice(stat_ref[1, rows])
            xhat = (x_ref[rows, cols] - twice(stat_ref[0, rows])) * inv
            go = up_ref[rows, cols].astype(F32) * twice(stat_ref[2, rows])
            inner = h_ref[rows, cols] - twice(acc_ref[rows]) - xhat * twice(acc2_ref[rows])
            hi_ref[i % 2, rows] = (go + inv * inner).astype(BF16)

    def finish(core):
        grad_rows(0)
        for i in range(chunks):
            if i + 1 < chunks:
                grad_rows(i + 1)
            weight = dot(frames_t_ref[...], hi_ref[i % 2])
            for half in range(CH // 128):
                tile = i * (CH // 128) + half
                block, inside = tile // per_block, (tile % per_block) * held
                lanes = slice(half * 128, half * 128 + 128)
                small = small_ref[:, tile * 128 : (tile + 1) * 128]
                target = keep_ref if block % 2 == core else send_ref
                side = (block // 2) ^ side_ref[0, 0]
                for p, start, stop, offset in runs(inside, inside + depth, part):
                    value = weight[offset : offset + stop - start, lanes]
                    target[side, p ^ ours_ref[0, 0], start:stop] = value
                for p, start, stop, offset in runs(inside + depth, inside + held, part):
                    value = small[offset : offset + stop - start]
                    target[side, p ^ ours_ref[0, 0], start:stop] = value

    pl.when(core_ref[0, 0] == 0)(lambda: finish(0))
    pl.when(core_ref[0, 0] != 0)(lambda: finish(1))
    for p, start, stop, _ in runs(per_block * held, parts * part, part):
        for side in range(halves):
            for ref in (keep_ref, send_ref):
                ref[side, p ^ ours_ref[0, 0], start:stop] = jnp.zeros((stop - start, 128), F32)


def vmem(count):
    return [pl.BlockSpec(memory_space=pltpu.VMEM)] * count


SCALARS = pl.BlockSpec(memory_space=pltpu.SMEM)


def pick(ours, index, rows, proj, taps, gain):
    dp, slot = index.shape
    width = rows.shape[1]
    if dp > FEW:
        index = index.reshape(1, -1)
        shapes = [jax.ShapeDtypeStruct((dp * slot, width), BF16)]
    else:
        shapes = [jax.ShapeDtypeStruct((slot, width), BF16)] * dp
    return pl.pallas_call(
        pick_kernel,
        out_shape=[jax.ShapeDtypeStruct((proj.shape[0] + 32, proj.shape[1]), BF16)] + shapes,
        in_specs=[SCALARS] + vmem(5),
        out_specs=vmem(1 + len(shapes)),
        scratch_shapes=[pltpu.VMEM((32, proj.shape[1]), F32)],
        compiler_params=pltpu.CompilerParams(vmem_limit_bytes=VMEM_LIMIT),
        cost_estimate=pl.CostEstimate(
            flops=2 * dp * slot * rows.size, bytes_accessed=6 * rows.size, transcendentals=0
        ),
        name="pick_rows",
    )(ours, index, rows, proj, taps, gain)


def unpack(ours, pieces, parts, part, depth, tap_count, width):
    return pl.pallas_call(
        functools.partial(unpack_kernel, len(pieces)),
        out_shape=[
            jax.ShapeDtypeStruct((depth, width), F32),
            jax.ShapeDtypeStruct((tap_count, width), F32),
            jax.ShapeDtypeStruct((width,), F32),
        ],
        in_specs=[SCALARS] + vmem(len(pieces)),
        out_specs=vmem(3),
        scratch_shapes=[pltpu.VMEM((parts, part, 128), F32)],
        compiler_params=pltpu.CompilerParams(vmem_limit_bytes=VMEM_LIMIT),
        cost_estimate=pl.CostEstimate(flops=10**6, bytes_accessed=12 * 10**5, transcendentals=0),
        name="unpack_gradients",
    )(ours, *pieces)


def positions(utterances):
    steps = utterances.shape[0]
    place = jnp.arange(steps, dtype=jnp.int32) + GAP * utterances
    most = max(sum(sizes) for sizes in WIDE_K + BLOCK_K)
    lines = []
    for kind, (ranges, sizes_of) in enumerate(((WIDE_STEPS, WIDE_K), (BLOCK_STEPS, BLOCK_K))):
        for j in range(3):
            local = place - (STARTS[j] - GAP)
            low, high = (0, LENGTHS[j] + 2 * GAP) if kind == 0 else (GAP, LENGTHS[j] + GAP)
            local = jnp.where((local >= low) & (local < high), local, -1)
            inside = jnp.arange(steps)
            local = jnp.where((inside >= ranges[j][0]) & (inside < ranges[j][1]), local, -1)
            pieces = [local[a:b] for a, b in k_slices(ranges[j], sizes_of[j])]
            line = jnp.concatenate(pieces)
            lines.append(jnp.pad(line, (0, most - line.shape[0]), constant_values=-1))
    lines.extend([jnp.full((most,), -1, jnp.int32)] * 2)
    return jnp.stack(lines)


def prepare(utterances, f_hi, f_lo, back):
    shapes = [
        jax.ShapeDtypeStruct((POINTS, AHEAD_AT[-1]), BF16),
        jax.ShapeDtypeStruct((BEHIND_AT[-1], 3 * POINTS), BF16),
    ]
    return pl.pallas_call(
        prep_kernel,
        out_shape=shapes,
        in_specs=vmem(4),
        out_specs=vmem(2),
        compiler_params=pltpu.CompilerParams(vmem_limit_bytes=VMEM_LIMIT),
        cost_estimate=pl.CostEstimate(flops=3 * 10**9, bytes_accessed=8 * 10**6, transcendentals=0),
        name="prepare_transforms",
    )(positions(utterances), f_hi, f_lo, back)


def layer(
    ids, arrived, take, params, upstream, tap_fwd, lags, ahead, behind, parts, part, halves
):
    steps, width = upstream.shape
    depth = arrived[0].shape[1] // 2
    hbm = pl.BlockSpec(memory_space=pltpu.HBM)
    scratch = [
        pltpu.VMEM(params.shape, BF16),
        pltpu.VMEM(upstream.shape, BF16),
        pltpu.VMEM(ahead.shape, BF16),
        pltpu.VMEM(behind.shape, BF16),
        pltpu.SemaphoreType.DMA((4,)),
        pltpu.VMEM((steps, depth), BF16),
        pltpu.VMEM((depth, steps), BF16),
        pltpu.VMEM((steps, width), F32),
        pltpu.VMEM((steps, width), F32),
        pltpu.VMEM((3, steps, 128), F32),
        pltpu.VMEM((steps, 128), F32),
        pltpu.VMEM((steps, 128), F32),
        pltpu.VMEM((2, steps, CH), BF16),
        pltpu.VMEM((2, steps, CH), BF16),
        pltpu.VMEM((2, steps, CH), BF16),
        pltpu.VMEM((2, steps, CH), BF16),
        pltpu.VMEM((2, 3, POINTS, CH), F32),
        pltpu.VMEM((2, 3, POINTS, CH), F32),
        pltpu.VMEM((2, 4, POINTS, CH), BF16),
        pltpu.VMEM((2, 4, POINTS, CH), BF16),
        pltpu.VMEM((2, POINTS, CH), F32),
        pltpu.VMEM((2, steps, CH), F32),
        pltpu.VMEM((32, width), F32),
        pltpu.VMEM((1, CH), F32),
    ]
    return pl.pallas_call(
        functools.partial(layer_kernel, len(arrived)),
        out_shape=[
            jax.ShapeDtypeStruct((halves, parts, part, 128), F32),
            jax.ShapeDtypeStruct((halves, parts, part, 128), F32),
            jax.ShapeDtypeStruct((1, 1), F32),
        ],
        in_specs=[SCALARS] * 3 + vmem(len(arrived) + 3) + [hbm] * 4,
        out_specs=vmem(3),
        scratch_shapes=scratch,
        compiler_params=pltpu.CompilerParams(vmem_limit_bytes=VMEM_LIMIT),
        cost_estimate=pl.CostEstimate(flops=10**10, bytes_accessed=16 * 10**6, transcendentals=10**6),
        name="layer_step",
    )(*ids, *arrived, take, tap_fwd, lags, params, upstream, ahead, behind)


def per_device(
    dp, fsdp, cached, send_rows, take_rows, utt_index, upstream, in_proj, norm_gain, conv_kernel
):
    tap_count = conv_kernel.shape[0]
    f_hi, f_lo, back, tap_fwd, lags = [jnp.asarray(m) for m in transforms(tap_count)]
    few = dp <= FEW
    place = lax.axis_index("fsdp")
    ours = lax.axis_index("dp") if few else jnp.zeros((), jnp.int32)
    ids = [v.astype(jnp.int32).reshape(1, 1) for v in (place % 2, place // 2, ours)]
    wanted = send_rows[0, 0]
    packed, *outgoing = pick(ids[2], wanted, cached[0, 0], in_proj, conv_kernel, norm_gain)
    params = lax.all_gather(packed, "fsdp", axis=1, tiled=True)
    outgoing, take_own, utt_own = lax.optimization_barrier(
        (outgoing, take_rows[0, 0], utt_index[0, 0])
    )

    def swap(value, k):
        return lax.ppermute(value, "dp", [(i, i ^ k) for i in range(dp)])

    far_first = [k for k in range(dp // 2, dp)] + [k for k in range(dp // 2 - 1, 0, -1)]
    if few:
        got = {k: swap(outgoing[k], k) for k in far_first}
        arrived = [outgoing[0]] + [got[k] for k in range(1, dp)]
        take_own = jnp.where(take_own >= 0, take_own ^ (ours * wanted.shape[1]), -1)
    else:
        sent = outgoing[0].reshape(wanted.shape + outgoing[0].shape[1:])
        back_in = lax.all_to_all(sent, "dp", split_axis=0, concat_axis=0, tiled=True)
        arrived = [back_in.reshape(-1, back_in.shape[2])]
    take = jnp.broadcast_to(jnp.repeat(take_own, 2)[:, None], (2 * take_own.shape[0], 128))
    ahead, behind = prepare(jnp.repeat(utt_own, 2), f_hi, f_lo, back)

    depth, shard_cols = in_proj.shape
    held = depth + 32
    tiles = shard_cols // 128
    part = -(-(held * tiles) // dp)
    part = -(-part // 16) * 16
    halves = fsdp // 2
    keep, send, loss = layer(
        ids, arrived, take, params, upstream[0, 0], tap_fwd, lags, ahead, behind,
        dp, part, halves,
    )
    other = lax.ppermute(send, "fsdp", [(i, i ^ 1) for i in range(fsdp)])
    half = dp // 2
    across = [(i, i ^ 2) for i in range(fsdp)]
    spans = ((half, dp), (0, half))
    sent = [(keep[1, low:high] + other[1, low:high]).astype(BF16) for low, high in spans]
    far_in, near_in = [lax.ppermute(v, "fsdp", across) for v in sent]
    far_sum = keep[0, half:] + other[0, half:] + far_in.astype(F32)
    far_out = far_sum.astype(BF16)
    near_in, _ = lax.optimization_barrier((near_in, far_out))
    near_sum = keep[0, :half] + other[0, :half] + near_in.astype(F32)
    near_out = near_sum.astype(BF16)
    if few:
        got = {}
        for k in far_first:
            got[k] = swap(far_out[k - half] if k >= half else near_out[k], k)
        total = near_sum[0]
        for k in range(1, dp):
            total = total + got[k].astype(F32)
        piece = total.astype(BF16)
        far = {k: swap(piece, k) for k in range(dp - 2, 0, -2)}
        pieces = {0: piece, 1: swap(piece, 1), **far}
        for k in far:
            pieces[k + 1] = swap(far[k], 1)
        pieces = [pieces[k] for k in range(dp)]
    else:
        chip = jnp.concatenate([near_out, far_out], axis=0)
        shared = lax.all_to_all(chip, "dp", split_axis=0, concat_axis=0, tiled=True)
        piece = jnp.sum(shared.astype(F32), axis=0).astype(BF16)
        pieces = [lax.all_gather(piece, "dp", axis=0, tiled=True)]
    proj, taps, gain = unpack(ids[2], pieces, dp, part, depth, tap_count, shard_cols)
    return (proj, taps, gain, loss)


def solution(mesh):
    placed = (
        P("dp", "fsdp", None, None),
        P("dp", "fsdp", None, None),
        P("dp", "fsdp", None),
        P("dp", "fsdp", None),
        P("dp", "fsdp", None, None),
        P(None, "fsdp"),
        P("fsdp"),
        P(None, "fsdp"),
    )
    return jax.shard_map(
        functools.partial(per_device, mesh.shape["dp"], mesh.shape["fsdp"]),
        mesh=mesh,
        in_specs=placed,
        out_specs=(P(None, "fsdp"), P(None, "fsdp"), P("fsdp"), P("dp", "fsdp")),
        check_vma=False,
    )
```

```python
import functools
import math

import jax
import jax.numpy as jnp
import numpy as np
from jax import lax
from jax.experimental import pallas as pl
from jax.experimental.pallas import tpu as pltpu
from jax.sharding import PartitionSpec as P

GAP = 16
POINTS = 256
FREQS = 128
STARTS = (0, 224, 432)
LENGTHS = (224, 208, 224)
BLOCK_STEPS = ((0, 208), (128, 384), (304, 512))
WIDE_STEPS = ((0, 224), (112, 400), (288, 512))
BLOCK_K = ((208, 208, 224), (256, 256, 256), (208, 208, 224))
WIDE_K = ((224, 224, 320), (288, 288, 320), (224, 224, 320))
AHEAD_AT = tuple(int(v) for v in np.cumsum([0] + [sum(k) for k in WIDE_K + BLOCK_K]))
BEHIND_AT = tuple(int(v) for v in np.cumsum([0] + [b - a for a, b in WIDE_STEPS + BLOCK_STEPS]))
CH = 256
ROWS = 64
F32 = jnp.float32
BF16 = jnp.bfloat16
VMEM_LIMIT = 60 * 1024 * 1024
LAYER_LIMIT = 52 * 1024 * 1024
UNPACK_LIMIT = 16 * 1024 * 1024
FEW = 16


def k_slices(steps, sizes):
    out = []
    for size in sizes:
        first = steps[0] if steps[0] + size <= 512 else 512 - size
        out.append((first, first + size))
    return out


def split(value):
    hi = value.astype(BF16)
    return hi, (value - hi.astype(F32)).astype(BF16)


def split_np(value):
    hi = value.astype(jnp.bfloat16)
    lo = (value - hi.astype(np.float64)).astype(jnp.bfloat16)
    return hi, lo


def transforms(tap_count):
    omega = 2 * np.pi * (np.arange(FREQS) + 0.5) / POINTS
    angle = omega[:, None] * np.arange(POINTS)[None, :]
    forward = np.concatenate([np.cos(angle), -np.sin(angle)], axis=0)
    f_hi, f_lo = split_np(forward)
    back = np.concatenate([f_hi.T, f_lo.T, f_hi.T], axis=1)
    shift = omega[:, None] * (np.arange(32) - tap_count // 2)[None, :]
    tap_ok = (np.arange(32) < tap_count)[None, :]
    taps = np.concatenate([np.cos(shift), np.sin(shift)], axis=0) * tap_ok / FREQS
    t_hi, t_lo = split_np(taps)
    tap_fwd = np.concatenate([t_hi, t_lo], axis=1)
    lag = np.concatenate([np.cos(shift), -np.sin(shift)], axis=0) * tap_ok / FREQS
    l_hi, l_lo = split_np(lag.T)
    lags = np.concatenate([l_hi, l_lo, l_hi], axis=1)
    return f_hi, f_lo, back, tap_fwd, lags


def dot(a, b):
    return jnp.dot(a, b, preferred_element_type=F32)


def dot_t(a, b):
    return lax.dot_general(a, b, (((0,), (0,)), ((), ())), preferred_element_type=F32)


def pick_kernel(ours_ref, index_ref, rows_ref, proj_ref, taps_ref, gain_ref, packed_ref, *refs):
    out_refs, tail_ref = refs[:-1], refs[-1]
    depth, tap_count = proj_ref.shape[0], taps_ref.shape[0]
    packed_ref[:depth] = proj_ref[...]
    tail_ref[:tap_count] = taps_ref[...].astype(F32)
    tail_ref[tap_count:] = gain_ref[...].astype(F32)[None, :]
    packed_ref[depth:] = tail_ref[...].astype(BF16)
    count = rows_ref.shape[0]
    rows = rows_ref[...]
    if len(out_refs) == 1:
        index = index_ref[...]
        number = lax.broadcasted_iota(jnp.int32, (count, index.shape[1]), 0)
        choose = jnp.where(number == index, 1.0, 0.0).astype(BF16)
        out_refs[0][...] = dot_t(choose, rows).astype(BF16)
        return
    slot = index_ref.shape[1]
    number = lax.broadcasted_iota(jnp.int32, (count, slot), 0)
    for k, out_ref in enumerate(out_refs):
        index = index_ref[pl.ds(ours_ref[0, 0] ^ k, 1), :]
        choose = jnp.where(number == index, 1.0, 0.0).astype(BF16)
        out_ref[...] = dot_t(choose, rows).astype(BF16)


def runs(first, last, part):
    out = []
    row = first
    while row < last:
        stop = min(last, (row // part + 1) * part)
        out.append((row // part, row % part, row % part + stop - row, row - first))
        row = stop
    return out


def unpack_kernel(count, ours_ref, *refs):
    piece_refs, (proj_ref, taps_ref, gain_ref, held_ref) = refs[:count], refs[count:]
    parts, part, _ = held_ref.shape
    for k in range(parts):
        piece = piece_refs[k][...] if count == parts else piece_refs[0][k * part : (k + 1) * part]
        held_ref[k] = piece.astype(F32)
    depth, width = proj_ref.shape
    held = depth + 32
    for tile in range(width // 128):
        lanes = slice(tile * 128, tile * 128 + 128)
        for p, start, stop, offset in runs(tile * held, tile * held + depth, part):
            proj_ref[offset : offset + stop - start, lanes] = held_ref[p ^ ours_ref[0, 0], start:stop]
        last = [
            held_ref[p ^ ours_ref[0, 0], start:stop]
            for p, start, stop, _ in runs(tile * held + depth, tile * held + held, part)
        ]
        last = last[0] if len(last) == 1 else jnp.concatenate(last, axis=0)
        taps_ref[:, lanes] = last[: taps_ref.shape[0]]
        gain_ref[lanes] = last[taps_ref.shape[0] : taps_ref.shape[0] + 1].reshape(128)


def prep_kernel(take_ref, pos_ref, hi_ref, lo_ref, back_ref, column_ref, ahead_ref, behind_ref):
    wide = jnp.broadcast_to(take_ref[...].astype(F32), (128, take_ref.shape[1]))
    column_ref[...] = jnp.transpose(wide).astype(jnp.int32)
    f_hi = hi_ref[...]
    f_lo = lo_ref[...]
    back = back_ref[...]
    for part in range(6):
        sizes = (WIDE_K + BLOCK_K)[part]
        steps = (WIDE_STEPS + BLOCK_STEPS)[part]
        total = sum(sizes)
        place = pos_ref[part : part + 1, :total]
        number = lax.broadcasted_iota(jnp.int32, (POINTS, total), 0)
        hot = jnp.where(number == place, 1.0, 0.0).astype(BF16)
        lane = lax.broadcasted_iota(jnp.int32, (1, total), 1)
        middle = (lane >= sizes[0]) & (lane < sizes[0] + sizes[1])
        ahead = jnp.where(middle, dot(f_lo, hot), dot(f_hi, hot)).astype(BF16)
        ahead_ref[:, AHEAD_AT[part] : AHEAD_AT[part + 1]] = ahead
        held = steps[1] - steps[0]
        padded = -(-held // 128) * 128
        wide = dot_t(hot[:, :padded], back)
        behind_ref[BEHIND_AT[part] : BEHIND_AT[part + 1]] = wide[:held].astype(BF16)


def layer_kernel(count, core_ref, side_ref, ours_ref, *refs):
    arrived_refs = refs[:count]
    (
        take_ref, tapf_ref, lag_ref, params_hbm, up_hbm, ahead_hbm, behind_hbm,
        keep_ref, send_ref, loss_ref,
        params_ref, up_ref, ahead_ref, behind_ref, sems,
        frames_ref, frames_t_ref, x_ref, h_ref, stat_ref, acc_ref, acc2_ref,
        hi_ref, lo_ref, ghi_ref, glo_ref, spec_ref, nspec_ref, phi_ref, plo_ref,
        coef_ref, c_ref, small_ref, lossacc_ref,
    ) = refs[count:]
    copies = [
        pltpu.make_async_copy(source, target, sems.at[k])
        for k, (source, target) in enumerate(
            ((params_hbm, params_ref), (ahead_hbm, ahead_ref), (behind_hbm, behind_ref), (up_hbm, up_ref))
        )
    ]
    for copy in copies:
        copy.start()
    steps, width = up_ref.shape
    slots = sum(ref.shape[0] for ref in arrived_refs)
    pair_width = arrived_refs[0].shape[1]
    depth = pair_width // 2
    chunks = width // CH
    scale = (steps * width) ** -0.5
    tiles = [slice(r, r + ROWS) for r in range(0, steps, ROWS)]
    wide_of = [slice(AHEAD_AT[j], AHEAD_AT[j + 1]) for j in range(3)]
    block_of = [slice(AHEAD_AT[j], AHEAD_AT[j + 1]) for j in range(3, 6)]
    back_wide = [slice(BEHIND_AT[j], BEHIND_AT[j + 1]) for j in range(3)]
    back_block = [slice(BEHIND_AT[j], BEHIND_AT[j + 1]) for j in range(3, 6)]

    first = jnp.concatenate([ref[:, :depth] for ref in arrived_refs], axis=0)
    second = jnp.concatenate([ref[:, depth:] for ref in arrived_refs], axis=0)
    for rows in [slice(r, r + 128) for r in range(0, steps, 128)]:
        take = take_ref[rows]
        odd = lax.broadcasted_iota(jnp.int32, (128, 128), 0) % 2
        lane = lax.broadcasted_iota(jnp.int32, (128, 128), 1)
        even_take = jnp.where(odd == 0, take, -1)
        odd_take = jnp.where(odd == 1, take, -1)
        even_hot, odd_hot = [
            jnp.concatenate(
                [jnp.where(lane + at == t, 1.0, 0.0).astype(BF16) for at in range(0, slots, 128)], axis=1
            )
            for t in (even_take, odd_take)
        ]
        frames_ref[rows] = (dot(even_hot, first) + dot(odd_hot, second)).astype(BF16)
        stat_ref[2, rows] = jnp.where(take >= 0, scale, 0.0)

    copies[0].wait()
    acc = jnp.zeros((steps, 128), F32)
    for i in range(chunks):
        cols = slice(i * CH, (i + 1) * CH)
        x = dot(frames_ref[...], params_ref[:depth, cols])
        x_ref[:, cols] = x
        acc = acc + x[:, :128] + x[:, 128:]
        if i < steps // 128:
            part_t = jnp.transpose(frames_ref[i * 128 : i * 128 + 128].astype(F32))
            frames_t_ref[:, i * 128 : i * 128 + 128] = part_t.astype(BF16)
    acc_ref[...] = acc
    mean = jnp.sum(acc_ref[...], axis=1, keepdims=True) * (1.0 / width)
    stat_ref[0] = jnp.broadcast_to(mean, (steps, 128))

    for rows in tiles:
        m = stat_ref[0, rows]
        total = jnp.zeros((ROWS, 128), F32)
        for k in range(width // 128):
            d = x_ref[rows, k * 128 : (k + 1) * 128] - m
            total = total + d * d
        var = jnp.sum(total, axis=1, keepdims=True) * (1.0 / width)
        stat_ref[1, rows] = jnp.broadcast_to(lax.rsqrt(var + 1e-05), (ROWS, 128))

    acc_ref[...] = jnp.zeros_like(acc_ref)
    acc2_ref[...] = jnp.zeros_like(acc2_ref)
    lossacc_ref[...] = jnp.zeros_like(lossacc_ref)

    for copy in copies[1:]:
        copy.wait()

    def twice(value):
        return jnp.concatenate([value, value], axis=1)

    def stack(hi, lo, slices):
        (a, b), (c, d), (e, f) = slices
        return jnp.concatenate([hi[a:b], hi[c:d], lo[e:f]], axis=0)

    def chunk(i, b):
        hi_b, lo_b, ghi_b, glo_b = hi_ref.at[b], lo_ref.at[b], ghi_ref.at[b], glo_ref.at[b]
        spec_b, nspec_b, phi_b, plo_b = spec_ref.at[b], nspec_ref.at[b], phi_ref.at[b], plo_ref.at[b]
        coef_b, c_b = coef_ref.at[b], c_ref.at[b]
        cols = pl.ds(pl.multiple_of(i * CH, CH), CH)
        gain = params_ref[depth + 16 : depth + 32, cols][15:16].astype(F32)
        taps = params_ref[depth : depth + 32, cols]
        coef_b[...] = dot(tapf_ref[...], jnp.concatenate([taps, taps], axis=0))
        for t, rows in enumerate(tiles):
            xhat = (x_ref[rows, cols] - twice(stat_ref[0, rows])) * twice(stat_ref[1, rows])
            hi, lo = split(xhat * gain)
            hi_b[rows] = hi
            lo_b[rows] = lo
            if t in (2, 5):
                yield
        yield
        for j in range(3):
            nspec_b[j] = dot(ahead_ref[:, block_of[j]], stack(hi_b, lo_b, k_slices(BLOCK_STEPS[j], BLOCK_K[j])))
            yield
        for j in range(3):
            for f in range(0, FREQS, 32):
                lower, upper = slice(f, f + 32), slice(FREQS + f, FREQS + f + 32)
                re, im = nspec_b[j, lower], nspec_b[j, upper]
                cre, cim = coef_b[lower], coef_b[upper]
                hi, lo = split(re * cre - im * cim)
                phi_b[j, lower] = hi
                plo_b[j, lower] = lo
                hi, lo = split(re * cim + im * cre)
                phi_b[j, upper] = hi
                plo_b[j, upper] = lo
            yield
        parts = []
        for j in range(3):
            held_j = jnp.concatenate([phi_b[j], phi_b[j], plo_b[j]], axis=0)
            parts.append(dot(behind_ref[back_wide[j]], held_j))
            if j == 1:
                c_b[0:112] = parts[0][0:112]
                c_b[112:224] = parts[0][112:224] + parts[1][0:112]
                c_b[224:288] = parts[1][112:176]
            if j == 2:
                c_b[288:400] = parts[1][176:288] + parts[2][0:112]
                c_b[400:512] = parts[2][112:224]
            yield
        loss = jnp.zeros((1, CH), F32)
        for t, rows in enumerate(tiles):
            conv = c_b[rows]
            sig = 0.5 + 0.5 * jnp.tanh(0.5 * conv)
            go = up_ref[rows, cols].astype(F32) * twice(stat_ref[2, rows])
            out = x_ref[rows, cols] + conv * sig
            loss = loss + jnp.sum(out * go, axis=0, keepdims=True)
            hi, lo = split(go * (sig * (1.0 + conv * (1.0 - sig))))
            ghi_b[rows] = hi
            glo_b[rows] = lo
            if t in (2, 5):
                yield
        lossacc_ref[...] += loss
        yield
        for j in range(3):
            spec_b[j] = dot(ahead_ref[:, wide_of[j]], stack(ghi_b, glo_b, k_slices(WIDE_STEPS[j], WIDE_K[j])))
            yield
        for f in range(0, FREQS, 32):
            lower, upper = slice(f, f + 32), slice(FREQS + f, FREQS + f + 32)
            cre, cim = coef_b[lower], coef_b[upper]
            zre = jnp.zeros((32, CH), F32)
            zim = jnp.zeros((32, CH), F32)
            for j in range(3):
                nre, nim = nspec_b[j, lower], nspec_b[j, upper]
                re, im = spec_b[j, lower], spec_b[j, upper]
                zre = zre + (nre * re + nim * im)
                zim = zim + (nim * re - nre * im)
                hi, lo = split(re * cre + im * cim)
                phi_b[j, lower] = hi
                plo_b[j, lower] = lo
                hi, lo = split(im * cre - re * cim)
                phi_b[j, upper] = hi
                plo_b[j, upper] = lo
            hi, lo = split(zre)
            phi_b[3, lower] = hi
            plo_b[3, lower] = lo
            hi, lo = split(zim)
            phi_b[3, upper] = hi
            plo_b[3, upper] = lo
            if f != 32:
                yield
        parts = []
        for j in range(3):
            held_j = jnp.concatenate([phi_b[j], phi_b[j], plo_b[j]], axis=0)
            parts.append(dot(behind_ref[back_block[j]], held_j))
            if j == 1:
                c_b[0:128] = parts[0][0:128]
                c_b[128:208] = parts[0][128:208] + parts[1][0:80]
                c_b[208:304] = parts[1][80:176]
            if j == 2:
                c_b[304:384] = parts[1][176:256] + parts[2][0:80]
                c_b[384:512] = parts[2][80:208]
            yield
        tap_grad = dot(lag_ref[...], jnp.concatenate([phi_b[3], phi_b[3], plo_b[3]], axis=0))
        gain_grad = jnp.zeros((1, CH), F32)
        for t, rows in enumerate(tiles):
            gn = c_b[rows]
            xhat = (x_ref[rows, cols] - twice(stat_ref[0, rows])) * twice(stat_ref[1, rows])
            gain_grad = gain_grad + jnp.sum(gn * xhat, axis=0, keepdims=True)
            h = gn * gain
            hx = h * xhat
            h_ref[rows, cols] = h
            acc_ref[rows] += h[:, :128] + h[:, 128:]
            acc2_ref[rows] += hx[:, :128] + hx[:, 128:]
            if t in (2, 5):
                yield
        last = lax.broadcasted_iota(jnp.int32, (32, CH), 0) == 31
        small_ref[:, cols] = jnp.where(last, gain_grad, tap_grad)

    def middle(i, carry):
        lead, follow = chunk(2 * i, 0), chunk(2 * i + 1, 1)
        for _ in range(3):
            next(lead)
        running = [lead, follow]
        while running:
            running = [g for g in running if next(g, running) is not running]
        return carry

    lax.fori_loop(0, chunks // 2, middle, 0)
    loss_ref[...] = jnp.sum(lossacc_ref[...], axis=1, keepdims=True)
    for rows in tiles:
        m1 = jnp.sum(acc_ref[rows], axis=1, keepdims=True) * (1.0 / width)
        m2 = jnp.sum(acc2_ref[rows], axis=1, keepdims=True) * (1.0 / width)
        acc_ref[rows] = jnp.broadcast_to(m1, (ROWS, 128))
        acc2_ref[rows] = jnp.broadcast_to(m2, (ROWS, 128))

    halves, parts, part, _ = keep_ref.shape
    per_block = width // (2 * halves) // 128
    held = depth + 32

    def grad_rows(i):
        cols = slice(i * CH, (i + 1) * CH)
        for rows in tiles:
            inv = twice(stat_ref[1, rows])
            xhat = (x_ref[rows, cols] - twice(stat_ref[0, rows])) * inv
            go = up_ref[rows, cols].astype(F32) * twice(stat_ref[2, rows])
            inner = h_ref[rows, cols] - twice(acc_ref[rows]) - xhat * twice(acc2_ref[rows])
            hi_ref[i % 2, rows] = (go + inv * inner).astype(BF16)

    def finish(core):
        grad_rows(0)
        for i in range(chunks):
            if i + 1 < chunks:
                grad_rows(i + 1)
            weight = dot(frames_t_ref[...], hi_ref[i % 2])
            for half in range(CH // 128):
                tile = i * (CH // 128) + half
                block, inside = tile // per_block, (tile % per_block) * held
                lanes = slice(half * 128, half * 128 + 128)
                small = small_ref[:, tile * 128 : (tile + 1) * 128]
                target = keep_ref if block % 2 == core else send_ref
                side = (block // 2) ^ side_ref[0, 0]
                for p, start, stop, offset in runs(inside, inside + depth, part):
                    value = weight[offset : offset + stop - start, lanes]
                    target[side, p ^ ours_ref[0, 0], start:stop] = value
                for p, start, stop, offset in runs(inside + depth, inside + held, part):
                    value = small[offset : offset + stop - start]
                    target[side, p ^ ours_ref[0, 0], start:stop] = value

    pl.when(core_ref[0, 0] == 0)(lambda: finish(0))
    pl.when(core_ref[0, 0] != 0)(lambda: finish(1))
    for p, start, stop, _ in runs(per_block * held, parts * part, part):
        for side in range(halves):
            for ref in (keep_ref, send_ref):
                ref[side, p ^ ours_ref[0, 0], start:stop] = jnp.zeros((stop - start, 128), F32)


def vmem(count):
    return [pl.BlockSpec(memory_space=pltpu.VMEM)] * count


SCALARS = pl.BlockSpec(memory_space=pltpu.SMEM)


def pick(ours, index, rows, proj, taps, gain):
    dp, slot = index.shape
    width = rows.shape[1]
    if dp > FEW:
        index = index.reshape(1, -1)
        shapes = [jax.ShapeDtypeStruct((dp * slot, width), BF16)]
    else:
        shapes = [jax.ShapeDtypeStruct((slot, width), BF16)] * dp
    return pl.pallas_call(
        pick_kernel,
        out_shape=[jax.ShapeDtypeStruct((proj.shape[0] + 32, proj.shape[1]), BF16)] + shapes,
        in_specs=[SCALARS] + vmem(5),
        out_specs=vmem(1 + len(shapes)),
        scratch_shapes=[pltpu.VMEM((32, proj.shape[1]), F32)],
        compiler_params=pltpu.CompilerParams(vmem_limit_bytes=VMEM_LIMIT),
        cost_estimate=pl.CostEstimate(
            flops=2 * dp * slot * rows.size, bytes_accessed=6 * rows.size, transcendentals=0
        ),
        name="pick_rows",
    )(ours, index, rows, proj, taps, gain)


def unpack(ours, pieces, parts, part, depth, tap_count, width):
    return pl.pallas_call(
        functools.partial(unpack_kernel, len(pieces)),
        out_shape=[
            jax.ShapeDtypeStruct((depth, width), F32),
            jax.ShapeDtypeStruct((tap_count, width), F32),
            jax.ShapeDtypeStruct((width,), F32),
        ],
        in_specs=[SCALARS] + vmem(len(pieces)),
        out_specs=vmem(3),
        scratch_shapes=[pltpu.VMEM((parts, part, 128), F32)],
        compiler_params=pltpu.CompilerParams(vmem_limit_bytes=UNPACK_LIMIT),
        cost_estimate=pl.CostEstimate(flops=10**6, bytes_accessed=12 * 10**5, transcendentals=0),
        name="unpack_gradients",
    )(ours, *pieces)


def positions(utterances):
    steps = utterances.shape[0]
    place = jnp.arange(steps, dtype=jnp.int32) + GAP * utterances
    most = max(sum(sizes) for sizes in WIDE_K + BLOCK_K)
    lines = []
    for kind, (ranges, sizes_of) in enumerate(((WIDE_STEPS, WIDE_K), (BLOCK_STEPS, BLOCK_K))):
        for j in range(3):
            local = place - (STARTS[j] - GAP)
            low, high = (0, LENGTHS[j] + 2 * GAP) if kind == 0 else (GAP, LENGTHS[j] + GAP)
            local = jnp.where((local >= low) & (local < high), local, -1)
            inside = jnp.arange(steps)
            local = jnp.where((inside >= ranges[j][0]) & (inside < ranges[j][1]), local, -1)
            pieces = [local[a:b] for a, b in k_slices(ranges[j], sizes_of[j])]
            line = jnp.concatenate(pieces)
            lines.append(jnp.pad(line, (0, most - line.shape[0]), constant_values=-1))
    lines.extend([jnp.full((most,), -1, jnp.int32)] * 2)
    return jnp.stack(lines)


def prepare(take, utterances, f_hi, f_lo, back):
    shapes = [
        jax.ShapeDtypeStruct((take.shape[1], 128), jnp.int32),
        jax.ShapeDtypeStruct((POINTS, AHEAD_AT[-1]), BF16),
        jax.ShapeDtypeStruct((BEHIND_AT[-1], 3 * POINTS), BF16),
    ]
    return pl.pallas_call(
        prep_kernel,
        out_shape=shapes,
        in_specs=vmem(5),
        out_specs=vmem(3),
        compiler_params=pltpu.CompilerParams(vmem_limit_bytes=VMEM_LIMIT),
        cost_estimate=pl.CostEstimate(flops=3 * 10**9, bytes_accessed=8 * 10**6, transcendentals=0),
        name="prepare_transforms",
    )(take, positions(utterances), f_hi, f_lo, back)


def layer(
    ids, arrived, take, params, upstream, tap_fwd, lags, ahead, behind, parts, part, halves
):
    steps, width = upstream.shape
    depth = arrived[0].shape[1] // 2
    hbm = pl.BlockSpec(memory_space=pltpu.HBM)
    scratch = [
        pltpu.VMEM(params.shape, BF16),
        pltpu.VMEM(upstream.shape, BF16),
        pltpu.VMEM(ahead.shape, BF16),
        pltpu.VMEM(behind.shape, BF16),
        pltpu.SemaphoreType.DMA((4,)),
        pltpu.VMEM((steps, depth), BF16),
        pltpu.VMEM((depth, steps), BF16),
        pltpu.VMEM((steps, width), F32),
        pltpu.VMEM((steps, width), F32),
        pltpu.VMEM((3, steps, 128), F32),
        pltpu.VMEM((steps, 128), F32),
        pltpu.VMEM((steps, 128), F32),
        pltpu.VMEM((2, steps, CH), BF16),
        pltpu.VMEM((2, steps, CH), BF16),
        pltpu.VMEM((2, steps, CH), BF16),
        pltpu.VMEM((2, steps, CH), BF16),
        pltpu.VMEM((2, 3, POINTS, CH), F32),
        pltpu.VMEM((2, 3, POINTS, CH), F32),
        pltpu.VMEM((2, 4, POINTS, CH), BF16),
        pltpu.VMEM((2, 4, POINTS, CH), BF16),
        pltpu.VMEM((2, POINTS, CH), F32),
        pltpu.VMEM((2, steps, CH), F32),
        pltpu.VMEM((32, width), F32),
        pltpu.VMEM((1, CH), F32),
    ]
    return pl.pallas_call(
        functools.partial(layer_kernel, len(arrived)),
        out_shape=[
            jax.ShapeDtypeStruct((halves, parts, part, 128), F32),
            jax.ShapeDtypeStruct((halves, parts, part, 128), F32),
            jax.ShapeDtypeStruct((1, 1), F32),
        ],
        in_specs=[SCALARS] * 3 + vmem(len(arrived) + 3) + [hbm] * 4,
        out_specs=vmem(3),
        scratch_shapes=scratch,
        compiler_params=pltpu.CompilerParams(vmem_limit_bytes=LAYER_LIMIT),
        cost_estimate=pl.CostEstimate(flops=10**10, bytes_accessed=16 * 10**6, transcendentals=10**6),
        name="layer_step",
    )(*ids, *arrived, take, tap_fwd, lags, params, upstream, ahead, behind)


def per_device(
    dp, fsdp, cached, send_rows, take_rows, utt_index, upstream, in_proj, norm_gain, conv_kernel
):
    tap_count = conv_kernel.shape[0]
    f_hi, f_lo, back, tap_fwd, lags = [jnp.asarray(m) for m in transforms(tap_count)]
    few = dp <= FEW
    place = lax.axis_index("fsdp")
    ours = lax.axis_index("dp") if few else jnp.zeros((), jnp.int32)
    ids = [v.astype(jnp.int32).reshape(1, 1) for v in (place % 2, place // 2, ours)]
    wanted = send_rows[0, 0]
    packed, *outgoing = pick(ids[2], wanted, cached[0, 0], in_proj, conv_kernel, norm_gain)
    params = lax.all_gather(packed, "fsdp", axis=1, tiled=True)
    outgoing, take_own, utt_own = lax.optimization_barrier(
        (outgoing, take_rows[0, 0], utt_index[0, 0])
    )

    def swap(value, k):
        return lax.ppermute(value, "dp", [(i, i ^ k) for i in range(dp)])

    far_first = [k for k in range(dp // 2, dp)] + [k for k in range(dp // 2 - 1, 0, -1)]
    if few:
        got = {k: swap(outgoing[k], k) for k in far_first}
        arrived = [outgoing[0]] + [got[k] for k in range(1, dp)]
        take_own = jnp.where(take_own >= 0, take_own ^ (ours * wanted.shape[1]), -1)
    else:
        sent = outgoing[0].reshape(wanted.shape + outgoing[0].shape[1:])
        back_in = lax.all_to_all(sent, "dp", split_axis=0, concat_axis=0, tiled=True)
        arrived = [back_in.reshape(-1, back_in.shape[2])]
    take, ahead, behind = prepare(
        jnp.repeat(take_own, 2)[None, :], jnp.repeat(utt_own, 2), f_hi, f_lo, back
    )

    depth, shard_cols = in_proj.shape
    held = depth + 32
    tiles = shard_cols // 128
    part = -(-(held * tiles) // dp)
    part = -(-part // 16) * 16
    halves = fsdp // 2
    keep, send, loss = layer(
        ids, arrived, take, params, upstream[0, 0], tap_fwd, lags, ahead, behind,
        dp, part, halves,
    )
    other = lax.ppermute(send, "fsdp", [(i, i ^ 1) for i in range(fsdp)])
    half = dp // 2
    across = [(i, i ^ 2) for i in range(fsdp)]
    spans = ((half, dp), (0, half))
    sent = [(keep[1, low:high] + other[1, low:high]).astype(BF16) for low, high in spans]
    far_in, near_in = [lax.ppermute(v, "fsdp", across) for v in sent]
    far_sum = keep[0, half:] + other[0, half:] + far_in.astype(F32)
    far_out = far_sum.astype(BF16)
    near_in, _ = lax.optimization_barrier((near_in, far_out))
    near_sum = keep[0, :half] + other[0, :half] + near_in.astype(F32)
    near_out = near_sum.astype(BF16)
    if few:
        got = {}
        for k in far_first:
            got[k] = swap(far_out[k - half] if k >= half else near_out[k], k)
        total = near_sum[0]
        for k in range(1, dp):
            total = total + got[k].astype(F32)
        piece = total.astype(BF16)
        far = {k: swap(piece, k) for k in range(dp - 2, 0, -2)}
        pieces = {0: piece, 1: swap(piece, 1), **far}
        for k in far:
            pieces[k + 1] = swap(far[k], 1)
        pieces = [pieces[k] for k in range(dp)]
    else:
        chip = jnp.concatenate([near_out, far_out], axis=0)
        shared = lax.all_to_all(chip, "dp", split_axis=0, concat_axis=0, tiled=True)
        piece = jnp.sum(shared.astype(F32), axis=0).astype(BF16)
        pieces = [lax.all_gather(piece, "dp", axis=0, tiled=True)]
    proj, taps, gain = unpack(ids[2], pieces, dp, part, depth, tap_count, shard_cols)
    return (proj, taps, gain, loss)


def solution(mesh):
    placed = (
        P("dp", "fsdp", None, None),
        P("dp", "fsdp", None, None),
        P("dp", "fsdp", None),
        P("dp", "fsdp", None),
        P("dp", "fsdp", None, None),
        P(None, "fsdp"),
        P("fsdp"),
        P(None, "fsdp"),
    )
    return jax.shard_map(
        functools.partial(per_device, mesh.shape["dp"], mesh.shape["fsdp"]),
        mesh=mesh,
        in_specs=placed,
        out_specs=(P(None, "fsdp"), P(None, "fsdp"), P("fsdp"), P("dp", "fsdp")),
        check_vma=False,
    )
```

```python
import functools
import math

import jax
import jax.numpy as jnp
import numpy as np
from jax import lax
from jax.experimental import pallas as pl
from jax.experimental.pallas import tpu as pltpu
from jax.sharding import PartitionSpec as P

GAP = 16
POINTS = 256
FREQS = 128
STARTS = (0, 224, 432)
LENGTHS = (224, 208, 224)
BLOCK_STEPS = ((0, 208), (128, 384), (304, 512))
WIDE_STEPS = ((0, 224), (112, 400), (288, 512))
BLOCK_K = ((208, 208, 224), (256, 256, 256), (208, 208, 224))
WIDE_K = ((224, 224, 320), (288, 288, 320), (224, 224, 320))
AHEAD_AT = tuple(int(v) for v in np.cumsum([0] + [sum(k) for k in WIDE_K + BLOCK_K]))
BEHIND_AT = tuple(int(v) for v in np.cumsum([0] + [b - a for a, b in WIDE_STEPS + BLOCK_STEPS]))
CH = 256
ROWS = 64
F32 = jnp.float32
BF16 = jnp.bfloat16
VMEM_LIMIT = 60 * 1024 * 1024
LAYER_LIMIT = 52 * 1024 * 1024
UNPACK_LIMIT = 16 * 1024 * 1024
FEW = 16


def k_slices(steps, sizes):
    out = []
    for size in sizes:
        first = steps[0] if steps[0] + size <= 512 else 512 - size
        out.append((first, first + size))
    return out


def split(value):
    hi = value.astype(BF16)
    return hi, (value - hi.astype(F32)).astype(BF16)


def split_np(value):
    hi = value.astype(jnp.bfloat16)
    lo = (value - hi.astype(np.float64)).astype(jnp.bfloat16)
    return hi, lo


def transforms(tap_count):
    omega = 2 * np.pi * (np.arange(FREQS) + 0.5) / POINTS
    angle = omega[:, None] * np.arange(POINTS)[None, :]
    forward = np.concatenate([np.cos(angle), -np.sin(angle)], axis=0)
    f_hi, f_lo = split_np(forward)
    back = np.concatenate([f_hi.T, f_lo.T, f_hi.T], axis=1)
    shift = omega[:, None] * (np.arange(32) - tap_count // 2)[None, :]
    tap_ok = (np.arange(32) < tap_count)[None, :]
    taps = np.concatenate([np.cos(shift), np.sin(shift)], axis=0) * tap_ok / FREQS
    t_hi, t_lo = split_np(taps)
    tap_fwd = np.concatenate([t_hi, t_lo], axis=1)
    lag = np.concatenate([np.cos(shift), -np.sin(shift)], axis=0) * tap_ok / FREQS
    l_hi, l_lo = split_np(lag.T)
    lags = np.concatenate([l_hi, l_lo, l_hi], axis=1)
    return f_hi, f_lo, back, tap_fwd, lags


def dot(a, b):
    return jnp.dot(a, b, preferred_element_type=F32)


def dot_t(a, b):
    return lax.dot_general(a, b, (((0,), (0,)), ((), ())), preferred_element_type=F32)


def pick_kernel(ours_ref, index_ref, rows_ref, proj_ref, taps_ref, gain_ref, packed_ref, *refs):
    out_refs, tail_ref = refs[:-1], refs[-1]
    depth, tap_count = proj_ref.shape[0], taps_ref.shape[0]
    packed_ref[:depth] = proj_ref[...]
    tail_ref[:tap_count] = taps_ref[...].astype(F32)
    tail_ref[tap_count:] = gain_ref[...].astype(F32)[None, :]
    packed_ref[depth:] = tail_ref[...].astype(BF16)
    count = rows_ref.shape[0]
    rows = rows_ref[...]
    if len(out_refs) == 1:
        index = index_ref[...]
        number = lax.broadcasted_iota(jnp.int32, (count, index.shape[1]), 0)
        choose = jnp.where(number == index, 1.0, 0.0).astype(BF16)
        out_refs[0][...] = dot_t(choose, rows).astype(BF16)
        return
    slot = index_ref.shape[1]
    number = lax.broadcasted_iota(jnp.int32, (count, slot), 0)
    for k, out_ref in enumerate(out_refs):
        index = index_ref[pl.ds(ours_ref[0, 0] ^ k, 1), :]
        choose = jnp.where(number == index, 1.0, 0.0).astype(BF16)
        out_ref[...] = dot_t(choose, rows).astype(BF16)


def runs(first, last, part):
    out = []
    row = first
    while row < last:
        stop = min(last, (row // part + 1) * part)
        out.append((row // part, row % part, row % part + stop - row, row - first))
        row = stop
    return out


def unpack_kernel(count, ours_ref, *refs):
    piece_refs, (proj_ref, taps_ref, gain_ref, held_ref) = refs[:count], refs[count:]
    parts, part, _ = held_ref.shape
    for k in range(parts):
        piece = piece_refs[k][...] if count == parts else piece_refs[0][k * part : (k + 1) * part]
        held_ref[k] = piece.astype(F32)
    depth, width = proj_ref.shape
    held = depth + 32
    for tile in range(width // 128):
        lanes = slice(tile * 128, tile * 128 + 128)
        for p, start, stop, offset in runs(tile * held, tile * held + depth, part):
            proj_ref[offset : offset + stop - start, lanes] = held_ref[p ^ ours_ref[0, 0], start:stop]
        last = [
            held_ref[p ^ ours_ref[0, 0], start:stop]
            for p, start, stop, _ in runs(tile * held + depth, tile * held + held, part)
        ]
        last = last[0] if len(last) == 1 else jnp.concatenate(last, axis=0)
        taps_ref[:, lanes] = last[: taps_ref.shape[0]]
        gain_ref[lanes] = last[taps_ref.shape[0] : taps_ref.shape[0] + 1].reshape(128)


def prep_kernel(take_ref, pos_ref, hi_ref, lo_ref, back_ref, column_ref, ahead_ref, behind_ref):
    wide = jnp.broadcast_to(take_ref[...].astype(F32), (128, take_ref.shape[1]))
    column_ref[...] = jnp.transpose(wide).astype(jnp.int32)
    f_hi = hi_ref[...]
    f_lo = lo_ref[...]
    back = back_ref[...]
    for part in range(6):
        sizes = (WIDE_K + BLOCK_K)[part]
        steps = (WIDE_STEPS + BLOCK_STEPS)[part]
        total = sum(sizes)
        place = pos_ref[part : part + 1, :total]
        number = lax.broadcasted_iota(jnp.int32, (POINTS, total), 0)
        hot = jnp.where(number == place, 1.0, 0.0).astype(BF16)
        lane = lax.broadcasted_iota(jnp.int32, (1, total), 1)
        middle = (lane >= sizes[0]) & (lane < sizes[0] + sizes[1])
        ahead = jnp.where(middle, dot(f_lo, hot), dot(f_hi, hot)).astype(BF16)
        ahead_ref[:, AHEAD_AT[part] : AHEAD_AT[part + 1]] = ahead
        held = steps[1] - steps[0]
        padded = -(-held // 128) * 128
        wide = dot_t(hot[:, :padded], back)
        behind_ref[BEHIND_AT[part] : BEHIND_AT[part + 1]] = wide[:held].astype(BF16)


def layer_kernel(count, core_ref, side_ref, ours_ref, *refs):
    arrived_refs = refs[:count]
    (
        take_ref, tapf_ref, lag_ref, params_hbm, up_hbm, ahead_hbm, behind_hbm,
        keep_ref, send_ref, loss_ref,
        params_ref, up_ref, ahead_ref, behind_ref, sems,
        frames_ref, frames_t_ref, x_ref, h_ref, stat_ref, acc_ref, acc2_ref,
        hi_ref, lo_ref, ghi_ref, glo_ref, spec_ref, nspec_ref, phi_ref, plo_ref,
        coef_ref, c_ref, small_ref, lossacc_ref,
    ) = refs[count:]
    copies = [
        pltpu.make_async_copy(source, target, sems.at[k])
        for k, (source, target) in enumerate(
            ((params_hbm, params_ref), (ahead_hbm, ahead_ref), (behind_hbm, behind_ref), (up_hbm, up_ref))
        )
    ]
    for copy in copies:
        copy.start()
    steps, width = up_ref.shape
    slots = sum(ref.shape[0] for ref in arrived_refs)
    pair_width = arrived_refs[0].shape[1]
    depth = pair_width // 2
    chunks = width // CH
    scale = (steps * width) ** -0.5
    tiles = [slice(r, r + ROWS) for r in range(0, steps, ROWS)]
    wide_of = [slice(AHEAD_AT[j], AHEAD_AT[j + 1]) for j in range(3)]
    block_of = [slice(AHEAD_AT[j], AHEAD_AT[j + 1]) for j in range(3, 6)]
    back_wide = [slice(BEHIND_AT[j], BEHIND_AT[j + 1]) for j in range(3)]
    back_block = [slice(BEHIND_AT[j], BEHIND_AT[j + 1]) for j in range(3, 6)]

    first = jnp.concatenate([ref[:, :depth] for ref in arrived_refs], axis=0)
    second = jnp.concatenate([ref[:, depth:] for ref in arrived_refs], axis=0)
    for rows in [slice(r, r + 128) for r in range(0, steps, 128)]:
        take = take_ref[rows]
        odd = lax.broadcasted_iota(jnp.int32, (128, 128), 0) % 2
        lane = lax.broadcasted_iota(jnp.int32, (128, 128), 1)
        even_take = jnp.where(odd == 0, take, -1)
        odd_take = jnp.where(odd == 1, take, -1)
        even_hot, odd_hot = [
            jnp.concatenate(
                [jnp.where(lane + at == t, 1.0, 0.0).astype(BF16) for at in range(0, slots, 128)], axis=1
            )
            for t in (even_take, odd_take)
        ]
        frames_ref[rows] = (dot(even_hot, first) + dot(odd_hot, second)).astype(BF16)
        stat_ref[2, rows] = jnp.where(take >= 0, scale, 0.0)

    copies[0].wait()
    acc = jnp.zeros((steps, 128), F32)
    for i in range(chunks):
        cols = slice(i * CH, (i + 1) * CH)
        x = dot(frames_ref[...], params_ref[:depth, cols])
        x_ref[:, cols] = x
        acc = acc + x[:, :128] + x[:, 128:]
        if i < steps // 128:
            part_t = jnp.transpose(frames_ref[i * 128 : i * 128 + 128].astype(F32))
            frames_t_ref[:, i * 128 : i * 128 + 128] = part_t.astype(BF16)
    acc_ref[...] = acc
    mean = jnp.sum(acc_ref[...], axis=1, keepdims=True) * (1.0 / width)
    stat_ref[0] = jnp.broadcast_to(mean, (steps, 128))

    for rows in tiles:
        m = stat_ref[0, rows]
        total = jnp.zeros((ROWS, 128), F32)
        for k in range(width // 128):
            d = x_ref[rows, k * 128 : (k + 1) * 128] - m
            total = total + d * d
        var = jnp.sum(total, axis=1, keepdims=True) * (1.0 / width)
        stat_ref[1, rows] = jnp.broadcast_to(lax.rsqrt(var + 1e-05), (ROWS, 128))

    acc_ref[...] = jnp.zeros_like(acc_ref)
    acc2_ref[...] = jnp.zeros_like(acc2_ref)
    lossacc_ref[...] = jnp.zeros_like(lossacc_ref)

    for copy in copies[1:]:
        copy.wait()

    def twice(value):
        return jnp.concatenate([value, value], axis=1)

    def stack(hi, lo, slices):
        (a, b), (c, d), (e, f) = slices
        return jnp.concatenate([hi[a:b], hi[c:d], lo[e:f]], axis=0)

    def chunk(i, b):
        hi_b, lo_b, ghi_b, glo_b = hi_ref.at[b], lo_ref.at[b], ghi_ref.at[b], glo_ref.at[b]
        spec_b, nspec_b, phi_b, plo_b = spec_ref.at[b], nspec_ref.at[b], phi_ref.at[b], plo_ref.at[b]
        coef_b, c_b = coef_ref.at[b], c_ref.at[b]
        cols = pl.ds(pl.multiple_of(i * CH, CH), CH)
        gain = params_ref[depth + 16 : depth + 32, cols][15:16].astype(F32)
        taps = params_ref[depth : depth + 32, cols]
        coef_b[...] = dot(tapf_ref[...], jnp.concatenate([taps, taps], axis=0))
        for t, rows in enumerate(tiles):
            xhat = (x_ref[rows, cols] - twice(stat_ref[0, rows])) * twice(stat_ref[1, rows])
            hi, lo = split(xhat * gain)
            hi_b[rows] = hi
            lo_b[rows] = lo
            if t in (2, 5):
                yield
        yield
        for j in range(3):
            nspec_b[j] = dot(ahead_ref[:, block_of[j]], stack(hi_b, lo_b, k_slices(BLOCK_STEPS[j], BLOCK_K[j])))
            yield
        for j in range(3):
            for f in range(0, FREQS, 32):
                lower, upper = slice(f, f + 32), slice(FREQS + f, FREQS + f + 32)
                re, im = nspec_b[j, lower], nspec_b[j, upper]
                cre, cim = coef_b[lower], coef_b[upper]
                hi, lo = split(re * cre - im * cim)
                phi_b[j, lower] = hi
                plo_b[j, lower] = lo
                hi, lo = split(re * cim + im * cre)
                phi_b[j, upper] = hi
                plo_b[j, upper] = lo
            yield
        parts = []
        for j in range(3):
            held_j = jnp.concatenate([phi_b[j], phi_b[j], plo_b[j]], axis=0)
            parts.append(dot(behind_ref[back_wide[j]], held_j))
            if j == 1:
                c_b[0:112] = parts[0][0:112]
                c_b[112:224] = parts[0][112:224] + parts[1][0:112]
                c_b[224:288] = parts[1][112:176]
            if j == 2:
                c_b[288:400] = parts[1][176:288] + parts[2][0:112]
                c_b[400:512] = parts[2][112:224]
            yield
        loss = jnp.zeros((1, CH), F32)
        for t, rows in enumerate(tiles):
            conv = c_b[rows]
            sig = 0.5 + 0.5 * jnp.tanh(0.5 * conv)
            go = up_ref[rows, cols].astype(F32) * twice(stat_ref[2, rows])
            out = x_ref[rows, cols] + conv * sig
            loss = loss + jnp.sum(out * go, axis=0, keepdims=True)
            hi, lo = split(go * (sig * (1.0 + conv * (1.0 - sig))))
            ghi_b[rows] = hi
            glo_b[rows] = lo
            if t in (2, 5):
                yield
        lossacc_ref[...] += loss
        yield
        for j in range(3):
            spec_b[j] = dot(ahead_ref[:, wide_of[j]], stack(ghi_b, glo_b, k_slices(WIDE_STEPS[j], WIDE_K[j])))
            yield
        for f in range(0, FREQS, 32):
            lower, upper = slice(f, f + 32), slice(FREQS + f, FREQS + f + 32)
            cre, cim = coef_b[lower], coef_b[upper]
            zre = jnp.zeros((32, CH), F32)
            zim = jnp.zeros((32, CH), F32)
            for j in range(3):
                nre, nim = nspec_b[j, lower], nspec_b[j, upper]
                re, im = spec_b[j, lower], spec_b[j, upper]
                zre = zre + (nre * re + nim * im)
                zim = zim + (nim * re - nre * im)
                hi, lo = split(re * cre + im * cim)
                phi_b[j, lower] = hi
                plo_b[j, lower] = lo
                hi, lo = split(im * cre - re * cim)
                phi_b[j, upper] = hi
                plo_b[j, upper] = lo
            hi, lo = split(zre)
            phi_b[3, lower] = hi
            plo_b[3, lower] = lo
            hi, lo = split(zim)
            phi_b[3, upper] = hi
            plo_b[3, upper] = lo
            if f != 32:
                yield
        parts = []
        for j in range(3):
            held_j = jnp.concatenate([phi_b[j], phi_b[j], plo_b[j]], axis=0)
            parts.append(dot(behind_ref[back_block[j]], held_j))
            if j == 1:
                c_b[0:128] = parts[0][0:128]
                c_b[128:208] = parts[0][128:208] + parts[1][0:80]
                c_b[208:304] = parts[1][80:176]
            if j == 2:
                c_b[304:384] = parts[1][176:256] + parts[2][0:80]
                c_b[384:512] = parts[2][80:208]
            yield
        tap_grad = dot(lag_ref[...], jnp.concatenate([phi_b[3], phi_b[3], plo_b[3]], axis=0))
        gain_grad = jnp.zeros((1, CH), F32)
        for t, rows in enumerate(tiles):
            gn = c_b[rows]
            xhat = (x_ref[rows, cols] - twice(stat_ref[0, rows])) * twice(stat_ref[1, rows])
            gain_grad = gain_grad + jnp.sum(gn * xhat, axis=0, keepdims=True)
            h = gn * gain
            hx = h * xhat
            h_ref[rows, cols] = h
            acc_ref[rows] += h[:, :128] + h[:, 128:]
            acc2_ref[rows] += hx[:, :128] + hx[:, 128:]
            if t in (2, 5):
                yield
        last = lax.broadcasted_iota(jnp.int32, (32, CH), 0) == 31
        small_ref[:, cols] = jnp.where(last, gain_grad, tap_grad)

    def middle(i, carry):
        lead, follow = chunk(2 * i, 0), chunk(2 * i + 1, 1)
        for _ in range(3):
            next(lead)
        running = [lead, follow]
        while running:
            running = [g for g in running if next(g, running) is not running]
        return carry

    lax.fori_loop(0, chunks // 2, middle, 0)
    loss_ref[...] = jnp.sum(lossacc_ref[...], axis=1, keepdims=True)
    for rows in tiles:
        m1 = jnp.sum(acc_ref[rows], axis=1, keepdims=True) * (1.0 / width)
        m2 = jnp.sum(acc2_ref[rows], axis=1, keepdims=True) * (1.0 / width)
        acc_ref[rows] = jnp.broadcast_to(m1, (ROWS, 128))
        acc2_ref[rows] = jnp.broadcast_to(m2, (ROWS, 128))

    halves, parts, part, _ = keep_ref.shape
    per_block = width // (2 * halves) // 128
    held = depth + 32

    def grad_rows(i):
        cols = slice(i * CH, (i + 1) * CH)
        for rows in tiles:
            inv = twice(stat_ref[1, rows])
            xhat = (x_ref[rows, cols] - twice(stat_ref[0, rows])) * inv
            go = up_ref[rows, cols].astype(F32) * twice(stat_ref[2, rows])
            inner = h_ref[rows, cols] - twice(acc_ref[rows]) - xhat * twice(acc2_ref[rows])
            hi_ref[i % 2, rows] = (go + inv * inner).astype(BF16)

    def finish(core):
        grad_rows(0)
        for i in range(chunks):
            if i + 1 < chunks:
                grad_rows(i + 1)
            weight = dot(frames_t_ref[...], hi_ref[i % 2])
            for half in range(CH // 128):
                tile = i * (CH // 128) + half
                block, inside = tile // per_block, (tile % per_block) * held
                lanes = slice(half * 128, half * 128 + 128)
                small = small_ref[:, tile * 128 : (tile + 1) * 128]
                target = keep_ref if block % 2 == core else send_ref
                side = (block // 2) ^ side_ref[0, 0]
                for p, start, stop, offset in runs(inside, inside + depth, part):
                    value = weight[offset : offset + stop - start, lanes]
                    target[side, p ^ ours_ref[0, 0], start:stop] = value
                for p, start, stop, offset in runs(inside + depth, inside + held, part):
                    value = small[offset : offset + stop - start]
                    target[side, p ^ ours_ref[0, 0], start:stop] = value

    pl.when(core_ref[0, 0] == 0)(lambda: finish(0))
    pl.when(core_ref[0, 0] != 0)(lambda: finish(1))
    for p, start, stop, _ in runs(per_block * held, parts * part, part):
        for side in range(halves):
            for ref in (keep_ref, send_ref):
                ref[side, p ^ ours_ref[0, 0], start:stop] = jnp.zeros((stop - start, 128), F32)


def vmem(count):
    return [pl.BlockSpec(memory_space=pltpu.VMEM)] * count


SCALARS = pl.BlockSpec(memory_space=pltpu.SMEM)


def pick(ours, index, rows, proj, taps, gain):
    dp, slot = index.shape
    width = rows.shape[1]
    if dp > FEW:
        index = index.reshape(1, -1)
        shapes = [jax.ShapeDtypeStruct((dp * slot, width), BF16)]
    else:
        shapes = [jax.ShapeDtypeStruct((slot, width), BF16)] * dp
    return pl.pallas_call(
        pick_kernel,
        out_shape=[jax.ShapeDtypeStruct((proj.shape[0] + 32, proj.shape[1]), BF16)] + shapes,
        in_specs=[SCALARS] + vmem(5),
        out_specs=vmem(1 + len(shapes)),
        scratch_shapes=[pltpu.VMEM((32, proj.shape[1]), F32)],
        compiler_params=pltpu.CompilerParams(vmem_limit_bytes=VMEM_LIMIT),
        cost_estimate=pl.CostEstimate(
            flops=2 * dp * slot * rows.size, bytes_accessed=6 * rows.size, transcendentals=0
        ),
        name="pick_rows",
    )(ours, index, rows, proj, taps, gain)


def unpack(ours, pieces, parts, part, depth, tap_count, width):
    return pl.pallas_call(
        functools.partial(unpack_kernel, len(pieces)),
        out_shape=[
            jax.ShapeDtypeStruct((depth, width), F32),
            jax.ShapeDtypeStruct((tap_count, width), F32),
            jax.ShapeDtypeStruct((width,), F32),
        ],
        in_specs=[SCALARS] + vmem(len(pieces)),
        out_specs=vmem(3),
        scratch_shapes=[pltpu.VMEM((parts, part, 128), F32)],
        compiler_params=pltpu.CompilerParams(vmem_limit_bytes=UNPACK_LIMIT),
        cost_estimate=pl.CostEstimate(flops=10**6, bytes_accessed=12 * 10**5, transcendentals=0),
        name="unpack_gradients",
    )(ours, *pieces)


def positions(utterances):
    steps = utterances.shape[0]
    place = jnp.arange(steps, dtype=jnp.int32) + GAP * utterances
    most = max(sum(sizes) for sizes in WIDE_K + BLOCK_K)
    lines = []
    for kind, (ranges, sizes_of) in enumerate(((WIDE_STEPS, WIDE_K), (BLOCK_STEPS, BLOCK_K))):
        for j in range(3):
            local = place - (STARTS[j] - GAP)
            low, high = (0, LENGTHS[j] + 2 * GAP) if kind == 0 else (GAP, LENGTHS[j] + GAP)
            local = jnp.where((local >= low) & (local < high), local, -1)
            inside = jnp.arange(steps)
            local = jnp.where((inside >= ranges[j][0]) & (inside < ranges[j][1]), local, -1)
            pieces = [local[a:b] for a, b in k_slices(ranges[j], sizes_of[j])]
            line = jnp.concatenate(pieces)
            lines.append(jnp.pad(line, (0, most - line.shape[0]), constant_values=-1))
    lines.extend([jnp.full((most,), -1, jnp.int32)] * 2)
    return jnp.stack(lines)


def prepare(take, utterances, f_hi, f_lo, back):
    shapes = [
        jax.ShapeDtypeStruct((take.shape[1], 128), jnp.int32),
        jax.ShapeDtypeStruct((POINTS, AHEAD_AT[-1]), BF16),
        jax.ShapeDtypeStruct((BEHIND_AT[-1], 3 * POINTS), BF16),
    ]
    return pl.pallas_call(
        prep_kernel,
        out_shape=shapes,
        in_specs=vmem(5),
        out_specs=vmem(3),
        compiler_params=pltpu.CompilerParams(vmem_limit_bytes=VMEM_LIMIT),
        cost_estimate=pl.CostEstimate(flops=3 * 10**9, bytes_accessed=8 * 10**6, transcendentals=0),
        name="prepare_transforms",
    )(take, positions(utterances), f_hi, f_lo, back)


def layer(
    ids, arrived, take, params, upstream, tap_fwd, lags, ahead, behind, parts, part, halves
):
    steps, width = upstream.shape
    depth = arrived[0].shape[1] // 2
    hbm = pl.BlockSpec(memory_space=pltpu.HBM)
    scratch = [
        pltpu.VMEM(params.shape, BF16),
        pltpu.VMEM(upstream.shape, BF16),
        pltpu.VMEM(ahead.shape, BF16),
        pltpu.VMEM(behind.shape, BF16),
        pltpu.SemaphoreType.DMA((4,)),
        pltpu.VMEM((steps, depth), BF16),
        pltpu.VMEM((depth, steps), BF16),
        pltpu.VMEM((steps, width), F32),
        pltpu.VMEM((steps, width), F32),
        pltpu.VMEM((3, steps, 128), F32),
        pltpu.VMEM((steps, 128), F32),
        pltpu.VMEM((steps, 128), F32),
        pltpu.VMEM((2, steps, CH), BF16),
        pltpu.VMEM((2, steps, CH), BF16),
        pltpu.VMEM((2, steps, CH), BF16),
        pltpu.VMEM((2, steps, CH), BF16),
        pltpu.VMEM((2, 3, POINTS, CH), F32),
        pltpu.VMEM((2, 3, POINTS, CH), F32),
        pltpu.VMEM((2, 4, POINTS, CH), BF16),
        pltpu.VMEM((2, 4, POINTS, CH), BF16),
        pltpu.VMEM((2, POINTS, CH), F32),
        pltpu.VMEM((2, steps, CH), F32),
        pltpu.VMEM((32, width), F32),
        pltpu.VMEM((1, CH), F32),
    ]
    return pl.pallas_call(
        functools.partial(layer_kernel, len(arrived)),
        out_shape=[
            pltpu.VMEM((halves, parts, part, 128), F32),
            pltpu.VMEM((halves, parts, part, 128), F32),
            jax.ShapeDtypeStruct((1, 1), F32),
        ],
        in_specs=[SCALARS] * 3 + vmem(len(arrived) + 3) + [hbm] * 4,
        out_specs=vmem(3),
        scratch_shapes=scratch,
        compiler_params=pltpu.CompilerParams(vmem_limit_bytes=LAYER_LIMIT),
        cost_estimate=pl.CostEstimate(flops=10**10, bytes_accessed=16 * 10**6, transcendentals=10**6),
        name="layer_step",
    )(*ids, *arrived, take, tap_fwd, lags, params, upstream, ahead, behind)


def per_device(
    dp, fsdp, cached, send_rows, take_rows, utt_index, upstream, in_proj, norm_gain, conv_kernel
):
    tap_count = conv_kernel.shape[0]
    f_hi, f_lo, back, tap_fwd, lags = [jnp.asarray(m) for m in transforms(tap_count)]
    few = dp <= FEW
    place = lax.axis_index("fsdp")
    ours = lax.axis_index("dp") if few else jnp.zeros((), jnp.int32)
    ids = [v.astype(jnp.int32).reshape(1, 1) for v in (place % 2, place // 2, ours)]
    wanted = send_rows[0, 0]
    packed, *outgoing = pick(ids[2], wanted, cached[0, 0], in_proj, conv_kernel, norm_gain)
    params = lax.all_gather(packed, "fsdp", axis=1, tiled=True)
    outgoing, take_own, utt_own = lax.optimization_barrier(
        (outgoing, take_rows[0, 0], utt_index[0, 0])
    )

    def swap(value, k):
        return lax.ppermute(value, "dp", [(i, i ^ k) for i in range(dp)])

    far_first = [k for k in range(dp // 2, dp)] + [k for k in range(dp // 2 - 1, 0, -1)]
    if few:
        got = {k: swap(outgoing[k], k) for k in far_first}
        arrived = [outgoing[0]] + [got[k] for k in range(1, dp)]
        take_own = jnp.where(take_own >= 0, take_own ^ (ours * wanted.shape[1]), -1)
    else:
        sent = outgoing[0].reshape(wanted.shape + outgoing[0].shape[1:])
        back_in = lax.all_to_all(sent, "dp", split_axis=0, concat_axis=0, tiled=True)
        arrived = [back_in.reshape(-1, back_in.shape[2])]
    take, ahead, behind = prepare(
        jnp.repeat(take_own, 2)[None, :], jnp.repeat(utt_own, 2), f_hi, f_lo, back
    )

    depth, shard_cols = in_proj.shape
    held = depth + 32
    tiles = shard_cols // 128
    part = -(-(held * tiles) // dp)
    part = -(-part // 16) * 16
    halves = fsdp // 2
    keep, send, loss = layer(
        ids, arrived, take, params, upstream[0, 0], tap_fwd, lags, ahead, behind,
        dp, part, halves,
    )
    other = lax.ppermute(send, "fsdp", [(i, i ^ 1) for i in range(fsdp)])
    half = dp // 2
    across = [(i, i ^ 2) for i in range(fsdp)]
    spans = ((half, dp), (0, half))
    sent = [(keep[1, low:high] + other[1, low:high]).astype(BF16) for low, high in spans]
    far_in = lax.ppermute(sent[0], "fsdp", across)
    far_sum = keep[0, half:] + other[0, half:] + far_in.astype(F32)
    far_out = far_sum.astype(BF16)
    near_sent, _ = lax.optimization_barrier((sent[1], far_out))
    near_in = lax.ppermute(near_sent, "fsdp", across)
    near_sum = keep[0, :half] + other[0, :half] + near_in.astype(F32)
    near_out = near_sum.astype(BF16)
    if few:
        got = {}
        for k in far_first:
            got[k] = swap(far_out[k - half] if k >= half else near_out[k], k)
        total = near_sum[0]
        for k in range(1, dp):
            total = total + got[k].astype(F32)
        piece = total.astype(BF16)
        far = {k: swap(piece, k) for k in range(dp - 2, 0, -2)}
        pieces = {0: piece, 1: swap(piece, 1), **far}
        for k in far:
            pieces[k + 1] = swap(far[k], 1)
        pieces = [pieces[k] for k in range(dp)]
    else:
        chip = jnp.concatenate([near_out, far_out], axis=0)
        shared = lax.all_to_all(chip, "dp", split_axis=0, concat_axis=0, tiled=True)
        piece = jnp.sum(shared.astype(F32), axis=0).astype(BF16)
        pieces = [lax.all_gather(piece, "dp", axis=0, tiled=True)]
    proj, taps, gain = unpack(ids[2], pieces, dp, part, depth, tap_count, shard_cols)
    return (proj, taps, gain, loss)


def solution(mesh):
    placed = (
        P("dp", "fsdp", None, None),
        P("dp", "fsdp", None, None),
        P("dp", "fsdp", None),
        P("dp", "fsdp", None),
        P("dp", "fsdp", None, None),
        P(None, "fsdp"),
        P("fsdp"),
        P(None, "fsdp"),
    )
    return jax.shard_map(
        functools.partial(per_device, mesh.shape["dp"], mesh.shape["fsdp"]),
        mesh=mesh,
        in_specs=placed,
        out_specs=(P(None, "fsdp"), P(None, "fsdp"), P("fsdp"), P("dp", "fsdp")),
        check_vma=False,
    )
```
